32 devices in a mesh: section: 2 (over core), dp: 4 (over z), tensor: 4 (over y, x).
Axes of the slice: x: 2, y: 2, z: 4, core: 2. Of those that a mesh axis runs over, the one named last changes fastest.
Arguments:
- tokens: bfloat16 [2, 1024, 2048], P(None, ('dp', 'tensor')), may hold values from -6 to 6
- lengths: int32 [2, 4], P(None, 'dp'), may hold values from 1 to 256, as said below
- cotangent: bfloat16 [2, 1024, 2048], P(None, ('dp', 'tensor')), may hold values from -6 to 6
- attn_gain: float32 [2, 2048], P('section'), may hold values from 0.5 to 1.5
- mlp_gain: float32 [2, 2048], P('section'), may hold values from 0.5 to 1.5
- w_query: bfloat16 [2, 2048, 2048], P('section', None, 'tensor'), may hold values from -0.125 to 0.125
- w_key: bfloat16 [2, 2048, 512], P('section', None, 'tensor'), may hold values from -0.125 to 0.125
- w_value: bfloat16 [2, 2048, 512], P('section', None, 'tensor'), may hold values from -0.125 to 0.125
- w_out: bfloat16 [2, 2048, 2048], P('section', 'tensor'), may hold values from -1 to 1
- w_gate: bfloat16 [2, 2048, 8192], P('section', None, 'tensor'), may hold values from -0.125 to 0.125
- w_up: bfloat16 [2, 2048, 8192], P('section', None, 'tensor'), may hold values from -0.125 to 0.125
- w_down: bfloat16 [2, 8192, 2048], P('section', 'tensor'), may hold values from -0.0625 to 0.0625
Outputs:
- activations: bfloat16 [2, 2, 1024, 2048], P('section', None, ('dp', 'tensor'))
- input_grads: float32 [2, 2, 1024, 2048], P('section', None, ('dp', 'tensor'))
- attn_gain_grad: float32 [2, 2048], P('section', ('dp', 'tensor'))
- mlp_gain_grad: float32 [2, 2048], P('section', ('dp', 'tensor'))
- w_query_grad: float32 [2, 2048, 2048], P('section', 'dp', 'tensor')
- w_key_grad: float32 [2, 2048, 512], P('section', 'dp', 'tensor')
- w_value_grad: float32 [2, 2048, 512], P('section', 'dp', 'tensor')
- w_out_grad: float32 [2, 2048, 2048], P('section', 'tensor', 'dp')
- w_gate_grad: float32 [2, 2048, 8192], P('section', 'dp', 'tensor')
- w_up_grad: float32 [2, 2048, 8192], P('section', 'dp', 'tensor')
- w_down_grad: float32 [2, 8192, 2048], P('section', 'tensor', 'dp')
The draws below stay inside these ranges and needn't reach their ends.
Inputs may be any that keep to these rules, and one draw needn't show every extreme that they name: `lengths`: in every data group one of its 2 sequences, drawn from the seed, has all 256 positions valid.
All inputs are finite; a program needn't handle non-finite values.
Results may differ from the reference program's by a relative error of at most 0.025.
Values may be sent and summed in bfloat16 or wider, within the bound.
No kernel may reach another device: no remote copies, remote signals or barrier semaphores. Data moves between devices by JAX's collectives and lax.ppermute only.
A program may use at most 256 MiB of HBM per device.

```python
import jax
import jax.numpy as jnp
from jax import lax

D = 2048
H = 32
KVH = 8
HD = 64
FF = 8192
LEN = 256
MB = 2
LAYERS = 2
GROUPS = 4
ROWS = 1024


def draw_lengths(key, part):
    key = jax.random.fold_in(key, 11)
    key_base, key_full = jax.random.split(key)
    drawn = jax.random.randint(key_base, (MB, GROUPS), 1, LEN + 1)
    chosen = jax.random.randint(key_full, (GROUPS,), 0, MB)
    micro_rows = jnp.arange(MB, dtype=jnp.int32)[:, None]
    return jnp.where(micro_rows == chosen[None, :], LEN, drawn).astype(jnp.int32)


def shard_levels(rng, dims, cuts, least, high):
    gain = 1.0
    for dim, shards_of in cuts:
        steps = jax.random.uniform(jax.random.fold_in(jax.random.fold_in(rng, 6), dim), (shards_of,), jnp.float32, least / len(cuts), high / len(cuts))
        gain = gain * jnp.repeat(jnp.exp(steps), dims[dim] // shards_of).reshape((-1,) + (1,) * (len(dims) - 1 - dim))
    return gain


def gaussian(own_key, dims, spread, bound, cuts=(), held_as=jnp.bfloat16):
    values = jax.random.normal(own_key, dims, jnp.float32) * spread
    if len(cuts) > 0:
        values = shard_levels(own_key, dims, cuts, -0.22, 0.18) * values
    return jnp.clip(values, min=-bound, max=bound).astype(held_as)


def setup_inputs(seed: int = 0) -> dict:
    streams_of = jax.random.split(jax.random.key(seed), 13)
    return {
        "tokens": gaussian(streams_of[0], (MB, ROWS, D), 1.0, 6.0, ((1, 16),)),
        "lengths": draw_lengths(jax.random.fold_in(streams_of[12], 71), 0),
        "cotangent": gaussian(streams_of[2], (MB, ROWS, D), 1.0, 6.0, ((1, 16),)),
        "attn_gain": jnp.clip(1.0 + 0.1 * jax.random.normal(streams_of[3], (LAYERS, D), jnp.float32), 0.5, 1.5),
        "mlp_gain": jnp.clip(1.0 + 0.1 * jax.random.normal(streams_of[4], (LAYERS, D), jnp.float32), 0.5, 1.5),
        "w_query": gaussian(streams_of[5], (LAYERS, D, H * HD), D ** -0.5, 0.125, ((0, 2), (2, 4))),
        "w_key": gaussian(streams_of[6], (LAYERS, D, KVH * HD), D ** -0.5, 0.125, ((0, 2), (2, 4))),
        "w_value": gaussian(streams_of[7], (LAYERS, D, KVH * HD), D ** -0.5, 0.125, ((0, 2), (2, 4))),
        "w_out": gaussian(streams_of[8], (LAYERS, H * HD, D), (H * HD // 64) ** -0.5, 1.0, ((0, 2), (1, 4))),
        "w_gate": gaussian(streams_of[9], (LAYERS, D, FF), D ** -0.5, 0.125, ((0, 2), (2, 4))),
        "w_up": gaussian(streams_of[10], (LAYERS, D, FF), D ** -0.5, 0.125, ((0, 2), (2, 4))),
        "w_down": gaussian(streams_of[11], (LAYERS, FF, D), FF ** -0.5, 0.0625, ((0, 2), (1, 4))),
    }


EPSILON = 1e-05
HIGHEST = lax.Precision.HIGHEST
NEGATIVE = -1e+30

@jax.custom_vjp
def low(v):
    return lax.optimization_barrier(v.astype(jnp.bfloat16)).astype(jnp.float32)

@jax.custom_vjp
def low_back(v):
    return v

def low_keep(v):
    return (low(v), None)

def low_pass(kept, grad):
    return (grad,)

def back_keep(v):
    return (v, None)

def back_low(kept, grad):
    return (low(grad),)
low.defvjp(low_keep, low_pass)
low_back.defvjp(back_keep, back_low)

def rope_tables(span_rows, head_size):
    half_width = head_size // 2
    counter = jnp.arange(half_width, dtype=jnp.float32)
    base_freq = 1.0 / 500000.0 ** (2.0 * counter / head_size)
    wavelength = 2.0 * jnp.pi / base_freq
    blend_part = (8192.0 / wavelength - 1.0) / 3.0
    middle = (1.0 - blend_part) * base_freq / 32.0 + blend_part * base_freq
    frequency = jnp.where(wavelength < 2048.0, base_freq, jnp.where(wavelength > 8192.0, base_freq / 32.0, middle))
    angles = jnp.arange(span_rows, dtype=jnp.float32)[:, None] * frequency[None, :]
    return (jnp.cos(angles), jnp.sin(angles))

def rotate(stacked, cosine, sine_table):
    half_width = stacked.shape[-1] // 2
    front_half = stacked[..., :half_width]
    back_half = stacked[..., half_width:]
    cos_wide = cosine[:, None, :]
    sin_wide = sine_table[:, None, :]
    return jnp.concatenate([front_half * cos_wide - back_half * sin_wide, back_half * cos_wide + front_half * sin_wide], axis=-1)

def rms_norm(stream, gain_row):
    scale_row = lax.rsqrt(lax.optimization_barrier(jnp.mean(stream * stream, axis=-1, keepdims=True)) + EPSILON)
    return stream * scale_row * gain_row

def project(left_side, matrix):
    return jnp.einsum('bld,de->ble', left_side, matrix, precision=HIGHEST)

def attend(pieces):
    queries, keys_rot, values_in, length = pieces
    group_size = queries.shape[1] // keys_rot.shape[1]
    keys_wide = jnp.repeat(keys_rot, group_size, axis=1)
    values_wide = jnp.repeat(values_in, group_size, axis=1)
    raw_scores = low_back(jnp.einsum('qhd,khd->hqk', queries, keys_wide, precision=HIGHEST))
    places = jnp.arange(queries.shape[0], dtype=jnp.int32)
    allowed = (places[None, :] <= places[:, None]) & (places[None, :] < length)
    scores = jnp.where(allowed[None], raw_scores * HD ** (-0.5), NEGATIVE)
    row_max = lax.optimization_barrier(jnp.max(scores, axis=-1, keepdims=True))
    lifted = jnp.exp(scores - row_max)
    softmax_w = low(lifted / lax.optimization_barrier(jnp.sum(lifted, axis=-1, keepdims=True)))
    return jnp.einsum('hqk,khd->qhd', softmax_w, values_wide, precision=HIGHEST)

def block_layer(stream, seq_lengths, weights, cosine, sine_table):
    attn_gain, mlp_gain, w_query, w_key, w_value, w_out, w_gate, w_up, w_down = weights
    batch_size = stream.shape[0]
    span_rows = stream.shape[1]
    attn_normed = low(rms_norm(stream, attn_gain))
    queries = low(rotate(low_back(project(attn_normed, w_query)).reshape(batch_size, span_rows, H, HD), cosine, sine_table))
    keys_rot = low(rotate(low_back(project(attn_normed, w_key)).reshape(batch_size, span_rows, KVH, HD), cosine, sine_table))
    values_in = low(low_back(project(attn_normed, w_value)).reshape(batch_size, span_rows, KVH, HD))
    attended = lax.map(jax.checkpoint(attend), (queries, keys_rot, values_in, seq_lengths))
    attended = low(low_back(attended.reshape(batch_size, span_rows, H * HD)))
    mid_stream = stream + low_back(project(attended, w_out))
    mlp_normed = low(rms_norm(mid_stream, mlp_gain))
    gate_val = low_back(project(mlp_normed, w_gate))
    up_val = low_back(project(mlp_normed, w_up))
    hidden = low(gate_val * jax.nn.sigmoid(gate_val) * up_val)
    return mid_stream + low_back(project(hidden, w_down))

def layer_stack(inputs, probes, params, seq_lengths, cosine, sine_table):
    stream = inputs
    layer_outs = []
    for layer_index in range(LAYERS):
        if layer_index > 0:
            stream = low_back(low(stream)) + probes[layer_index - 1]
        weights = tuple((matrix[layer_index] for matrix in params))
        stream = block_layer(stream, seq_lengths, weights, cosine, sine_table)
        layer_outs.append(stream)
    return (stream, jnp.stack(layer_outs))

def reference(tokens, lengths, cotangent, attn_gain, mlp_gain, w_query, w_key, w_value, w_out, w_gate, w_up, w_down):
    cosine, sine_table = rope_tables(LEN, HD)
    params = (attn_gain.astype(jnp.float32), mlp_gain.astype(jnp.float32), w_query.astype(jnp.float32), w_key.astype(jnp.float32), w_value.astype(jnp.float32), w_out.astype(jnp.float32), w_gate.astype(jnp.float32), w_up.astype(jnp.float32), w_down.astype(jnp.float32))
    seqs_in = tokens.astype(jnp.float32).reshape(MB, GROUPS, LEN, D)
    seqs_cot = cotangent.astype(jnp.float32).reshape(MB, GROUPS, LEN, D)
    positions = jnp.arange(LEN, dtype=jnp.int32)

    def one_batch(running, pieces):
        inputs, seq_lengths, cot_rows = pieces
        valid_rows = (positions[None, :] < seq_lengths[:, None]).astype(jnp.float32)[:, :, None]
        probes = jnp.zeros((LAYERS - 1,) + inputs.shape, jnp.float32)

        def run_stack(inputs_arg, probes_arg, params_arg):
            return layer_stack(inputs_arg, probes_arg, params_arg, seq_lengths, cosine, sine_table)
        final_out, pullback, layer_outs = jax.vjp(run_stack, inputs, probes, params, has_aux=True)
        d_tokens, d_probes, d_params = pullback(valid_rows * cot_rows)
        running = jax.tree.map(jnp.add, running, d_params)
        grads_in = jnp.concatenate([d_tokens[None], d_probes], axis=0)
        return (running, (layer_outs.astype(jnp.bfloat16), grads_in))
    zero_grads = jax.tree.map(jnp.zeros_like, params)
    totals, (activations, grads_in) = lax.scan(one_batch, zero_grads, (seqs_in, lengths, seqs_cot))
    activations = jnp.transpose(activations, (1, 0, 2, 3, 4)).reshape(LAYERS, MB, ROWS, D)
    grads_in = jnp.transpose(grads_in, (1, 0, 2, 3, 4)).reshape(LAYERS, MB, ROWS, D)
    return (activations, grads_in, totals[0], totals[1], totals[2], totals[3], totals[4], totals[5], totals[6], totals[7], totals[8])
```

```python
import functools

import jax
import jax.numpy as jnp
from jax import lax
from jax.experimental import pallas as pl
from jax.experimental.pallas import tpu as pltpu
from jax.sharding import PartitionSpec as P

HD = 64
EPSILON = 1e-05
NEGATIVE = -1e30
BF = jnp.bfloat16
F32 = jnp.float32
VMEM = pl.BlockSpec(memory_space=pltpu.VMEM)
ANY = pl.BlockSpec(memory_space=pl.ANY)
LIMIT = 56 * 1024 * 1024


def nn(a, b):
    return jnp.dot(a, b, preferred_element_type=F32)


def nt(a, b):
    return lax.dot_general(a, b, (((1,), (1,)), ((), ())), preferred_element_type=F32)


def tn(a, b):
    return lax.dot_general(a, b, (((0,), (0,)), ((), ())), preferred_element_type=F32)


def shaped(shape, dtype):
    return jax.ShapeDtypeStruct(shape, dtype)


def cost(flops, nbytes):
    return pl.CostEstimate(flops=int(flops), bytes_accessed=int(nbytes), transcendentals=0)


def partners(size):
    return [[(a, a ^ k) for a in range(size)] for k in range(1, size)]


def gather_rows(x, size):
    return [x] + [lax.ppermute(x, "tensor", pairs) for pairs in partners(size)]


def scatter_rows(parts, size):
    return [parts[0]] + [
        lax.ppermute(part, "tensor", pairs) for part, pairs in zip(parts[1:], partners(size))
    ]


def swapped(x):
    return lax.ppermute(x, "section", [(0, 1), (1, 0)])


def norm_kernel(x_ref, gain_ref, out_ref):
    x = x_ref[...].astype(F32)
    scale = lax.rsqrt(jnp.mean(x * x, axis=-1, keepdims=True) + EPSILON)
    out_ref[...] = (x * scale * gain_ref[...]).astype(BF)


def norm_rows(x, gain):
    return pl.pallas_call(
        norm_kernel, out_shape=shaped(x.shape, BF), in_specs=[VMEM] * 2, out_specs=VMEM
    )(x, gain)


def add_norm_kernel(round_out, base_ref, a_ref, b_ref, c_ref, d_ref, gain_ref, out_ref, normed_ref):
    x = base_ref[...].astype(F32) + (
        (a_ref[...].astype(F32) + b_ref[...].astype(F32))
        + (c_ref[...].astype(F32) + d_ref[...].astype(F32))
    )
    if round_out:
        x = x.astype(BF)
        out_ref[...] = x
        x = x.astype(F32)
    else:
        out_ref[...] = x
    scale = lax.rsqrt(jnp.mean(x * x, axis=-1, keepdims=True) + EPSILON)
    normed_ref[...] = (x * scale * gain_ref[...]).astype(BF)


def add_norm(base, terms, gain, round_out):
    return pl.pallas_call(
        functools.partial(add_norm_kernel, round_out),
        out_shape=(shaped(base.shape, BF if round_out else F32), shaped(base.shape, BF)),
        in_specs=[VMEM] * 6,
        out_specs=(VMEM, VMEM),
    )(base, *terms, gain)


def norm_back_kernel(base_ref, a_ref, b_ref, c_ref, d_ref, gain_ref, res_ref, out_ref, low_ref, gp_ref):
    g = (a_ref[...].astype(F32) + b_ref[...].astype(F32)) + (
        c_ref[...].astype(F32) + d_ref[...].astype(F32)
    )
    x = base_ref[...].astype(F32)
    scale = lax.rsqrt(jnp.mean(x * x, axis=-1, keepdims=True) + EPSILON)
    y = x * scale
    gp_ref[...] = jnp.sum(g * y, axis=0, keepdims=True)
    e = g * gain_ref[...]
    out = res_ref[...].astype(F32) + scale * (e - y * jnp.mean(e * y, axis=-1, keepdims=True))
    out_ref[...] = out
    low_ref[...] = out.astype(BF)


def norm_back(base, terms, gain, residual):
    return pl.pallas_call(
        norm_back_kernel,
        out_shape=(shaped(base.shape, F32), shaped(base.shape, BF), shaped((1, base.shape[1]), F32)),
        in_specs=[VMEM] * 7,
        out_specs=(VMEM,) * 3,
    )(base, *terms, gain, residual)


def turn(x, cos, sin, low):
    return x * cos + jnp.where(low, pltpu.roll(x, 96, 1), pltpu.roll(x, 32, 1)) * sin


def fetch_start(mine, ours, theirs, buffer, sem):
    @pl.when(mine)
    def _():
        pltpu.make_async_copy(ours, buffer, sem).start()

    @pl.when(jnp.logical_not(mine))
    def _():
        pltpu.make_async_copy(theirs, buffer, sem).start()


def fetch_wait(ours, buffer, sem):
    pltpu.make_async_copy(ours, buffer, sem).wait()


def spread(x, first_lanes):
    x = x.astype(F32)
    moved = pltpu.roll(x, 64, 1)
    zero = jnp.zeros_like(x)
    return [
        (jnp.where(first_lanes, x, zero).astype(BF), jnp.where(first_lanes, zero, moved).astype(BF)),
        (jnp.where(first_lanes, moved, zero).astype(BF), jnp.where(first_lanes, zero, x).astype(BF)),
    ]


def soft(q, k, mask):
    scores = jnp.where(mask, nt(q, k) * HD**-0.5, NEGATIVE)
    lifted = jnp.exp(scores - jnp.max(scores, axis=-1, keepdims=True))
    return lifted * (1.0 / jnp.sum(lifted, axis=-1, keepdims=True))


def attend_fwd_kernel(
    layer, x0, x1, x2, x3, wq_a, wq_b, wk_a, wk_b, wv_a, wv_b, wo_a, wo_b, cos_ref, sin_ref, pq_ref, pk_ref,
    p0, p1, p2, p3, x_out, q_out, k_out, v_out, att_out, wq, wk, wv, wo, sems,
):
    mine = lax.axis_index("section") == layer
    pairs = [(wq_a, wq_b, wq), (wk_a, wk_b, wk), (wv_a, wv_b, wv), (wo_a, wo_b, wo)]
    for n, (a, b, buffer) in enumerate(pairs):
        fetch_start(mine, a, b, buffer, sems.at[n])
    rows = x0.shape[0]
    for n, x in enumerate((x0, x1, x2, x3)):
        x_out[n * rows : (n + 1) * rows, :] = x[...]
    whole = 4 * rows
    lane = lax.broadcasted_iota(jnp.int32, (whole, 128), 1)
    low = (lane & (HD - 1)) < HD // 2
    first_lanes = lane < HD
    cos, sin = cos_ref[...], sin_ref[...]
    mask = pk_ref[...] <= pq_ref[...]
    for n in range(3):
        fetch_wait(pairs[n][0], pairs[n][2], sems.at[n])
    x = x_out[...]
    k = turn(nn(x, wk[...]), cos, sin, low).astype(BF)
    v = nn(x, wv[...]).astype(BF)
    k_out[...] = k
    v_out[...] = v
    keys, values = spread(k, first_lanes), spread(v, first_lanes)
    for p in range(q_out.shape[1] // 128):
        cut = slice(p * 128, (p + 1) * 128)
        q = turn(nn(x, wq[:, cut]), cos, sin, low).astype(BF)
        q_out[:, cut] = q
        head = p // 2
        att_out[:, cut] = (
            nn(soft(q, keys[head][0], mask).astype(BF), values[head][0])
            + nn(soft(q, keys[head][1], mask).astype(BF), values[head][1])
        ).astype(BF)
    fetch_wait(wo_a, wo, sems.at[3])
    att = att_out[...]
    for n, part in enumerate((p0, p1, p2, p3)):
        part[...] = jnp.zeros_like(part)
    columns = 512
    for c in range(p0.shape[1] // columns):
        cut = slice(c * columns, (c + 1) * columns)
        out = nn(att, wo[:, cut]).astype(BF)
        for n, part in enumerate((p0, p1, p2, p3)):
            part[:, cut] = out[n * rows : (n + 1) * rows, :]


def attend_fwd(layer, blocks, weights, tables):
    rows, depth = blocks[0].shape
    wq, wk, wv, wo = weights
    whole, width, narrow = 4 * rows, wq[0].shape[1], wk[0].shape[1]
    block = shaped((rows, depth), BF)
    return pl.pallas_call(
        functools.partial(attend_fwd_kernel, layer),
        out_shape=(block,) * 4
        + (
            shaped((whole, depth), BF),
            shaped((whole, width), BF),
            shaped((whole, narrow), BF),
            shaped((whole, narrow), BF),
            shaped((whole, width), BF),
        ),
        in_specs=[VMEM] * 4 + [ANY] * 8 + [VMEM] * 4,
        out_specs=(VMEM,) * 9,
        scratch_shapes=[
            pltpu.VMEM(wq[0].shape, BF),
            pltpu.VMEM(wk[0].shape, BF),
            pltpu.VMEM(wv[0].shape, BF),
            pltpu.VMEM(wo[0].shape, BF),
            pltpu.SemaphoreType.DMA((4,)),
        ],
        compiler_params=pltpu.CompilerParams(vmem_limit_bytes=LIMIT),
        cost_estimate=cost(4e9, 12e6),
    )(*blocks, *wq, *wk, *wv, *wo, *tables)


def attend_bwd_kernel(
    layer, d0, d1, d2, d3, q_ref, k_ref, v_ref, wq_a, wq_b, wk_a, wk_b, wv_a, wv_b, wo_a, wo_b,
    cos_ref, sin_ref, pq_ref, pk_ref,
    p0, p1, p2, p3, dm_out, dq_out, dk_out, dv_out, wq, wk, wv, wo, sems,
):
    mine = lax.axis_index("section") == layer
    pairs = [(wo_a, wo_b, wo), (wq_a, wq_b, wq), (wk_a, wk_b, wk), (wv_a, wv_b, wv)]
    for n, (a, b, buffer) in enumerate(pairs):
        fetch_start(mine, a, b, buffer, sems.at[n])
    rows = d0.shape[0]
    for n, d in enumerate((d0, d1, d2, d3)):
        dm_out[n * rows : (n + 1) * rows, :] = d[...]
    whole = 4 * rows
    lane = lax.broadcasted_iota(jnp.int32, (whole, 128), 1)
    low = (lane & (HD - 1)) < HD // 2
    first_lanes = lane < HD
    cos, sin = cos_ref[...], -sin_ref[...]
    mask = pk_ref[...] <= pq_ref[...]
    keys, values = spread(k_ref[...], first_lanes), spread(v_ref[...], first_lanes)
    fetch_wait(wo_a, wo, sems.at[0])
    dm = dm_out[...]
    dk_sums, dv_sums = [[None, None], [None, None]], [[None, None], [None, None]]

    def add(sums, head, side, term):
        sums[head][side] = term if sums[head][side] is None else sums[head][side] + term

    for p in range(q_ref.shape[1] // 128):
        cut = slice(p * 128, (p + 1) * 128)
        head = p // 2
        q = q_ref[:, cut]
        d_att = nt(dm, wo[cut, :]).astype(BF)
        d_q = None
        for side in range(2):
            probs = soft(q, keys[head][side], mask)
            d_probs = nt(d_att, values[head][side])
            inner = jnp.sum(d_probs * probs, axis=-1, keepdims=True)
            d_raw = (probs * (d_probs - inner) * HD**-0.5).astype(BF)
            term = nn(d_raw, keys[head][side])
            d_q = term if d_q is None else d_q + term
            add(dk_sums, head, side, tn(d_raw, q))
            add(dv_sums, head, side, tn(probs.astype(BF), d_att))
        dq_out[:, cut] = turn(d_q, cos, sin, low).astype(BF)

    def folded(sums):
        return jnp.where(
            first_lanes,
            sums[0][0] + pltpu.roll(sums[0][1], 64, 1),
            pltpu.roll(sums[1][0], 64, 1) + sums[1][1],
        )

    dk_out[...] = turn(folded(dk_sums), cos, sin, low).astype(BF)
    dv_out[...] = folded(dv_sums).astype(BF)
    for n in range(1, 4):
        fetch_wait(pairs[n][0], pairs[n][2], sems.at[n])
    dq, dk, dv = dq_out[...], dk_out[...], dv_out[...]
    columns = 512
    for c in range(p0.shape[1] // columns):
        cut = slice(c * columns, (c + 1) * columns)
        out = (nt(dq, wq[cut, :]) + nt(dk, wk[cut, :]) + nt(dv, wv[cut, :])).astype(BF)
        for n, part in enumerate((p0, p1, p2, p3)):
            part[:, cut] = out[n * rows : (n + 1) * rows, :]


def attend_bwd(layer, blocks, qkv, weights, tables):
    rows, depth = blocks[0].shape
    wq, wk, wv, wo = weights
    whole, width, narrow = 4 * rows, wq[0].shape[1], wk[0].shape[1]
    block = shaped((rows, depth), BF)
    return pl.pallas_call(
        functools.partial(attend_bwd_kernel, layer),
        out_shape=(block,) * 4
        + (
            shaped((whole, depth), BF),
            shaped((whole, width), BF),
            shaped((whole, narrow), BF),
            shaped((whole, narrow), BF),
        ),
        in_specs=[VMEM] * 7 + [ANY] * 8 + [VMEM] * 4,
        out_specs=(VMEM,) * 8,
        scratch_shapes=[
            pltpu.VMEM(wq[0].shape, BF),
            pltpu.VMEM(wk[0].shape, BF),
            pltpu.VMEM(wv[0].shape, BF),
            pltpu.VMEM(wo[0].shape, BF),
            pltpu.SemaphoreType.DMA((4,)),
        ],
        compiler_params=pltpu.CompilerParams(vmem_limit_bytes=LIMIT),
        cost_estimate=cost(5e9, 14e6),
    )(*blocks, *qkv, *wq, *wk, *wv, *wo, *tables)


TILE = 256


def chosen(layer, a, b, sec):
    pass


def mlp_fwd_kernel(
    layer, s_ref, x0, x1, x2, x3, wg_a, wg_b, wu_a, wu_b, wd_a, wd_b,
    p0, p1, p2, p3, x_out, gate_out, up_out, total,
):
    f = pl.program_id(0)
    rows = x0.shape[0]

    @pl.when(f == 0)
    def _():
        for n, x in enumerate((x0, x1, x2, x3)):
            x_out[n * rows : (n + 1) * rows, :] = x[...]
        total[...] = jnp.zeros_like(total)

    def work(wg, wu, wd):
        x = x_out[...]
        gate, up = nn(x, wg[...]), nn(x, wu[...])
        gate_out[...] = gate.astype(BF)
        up_out[...] = up.astype(BF)
        hidden = (gate * jax.nn.sigmoid(gate) * up).astype(BF)
        total[...] += nn(hidden, wd[...])

    mine = s_ref[0] == layer
    pl.when(mine)(lambda: work(wg_a, wu_a, wd_a))
    pl.when(jnp.logical_not(mine))(lambda: work(wg_b, wu_b, wd_b))

    @pl.when(f == pl.num_programs(0) - 1)
    def _():
        for n, part in enumerate((p0, p1, p2, p3)):
            part[...] = total[n * rows : (n + 1) * rows, :].astype(BF)


def pair_specs(layer, shape, dim, tile):
    block = tuple(tile if d == dim else size for d, size in enumerate(shape))

    def spec(flip):
        def index(f, s):
            used = (s[0] == layer) != flip
            return tuple(jnp.where(used, f, 0) if d == dim else 0 for d in range(2))

        return pl.BlockSpec(block, index)

    return [spec(False), spec(True)]


def whole_spec(shape):
    return pl.BlockSpec(shape, lambda f, s: (0,) * len(shape))


def mlp_fwd(layer, sec, blocks, weights):
    rows, depth = blocks[0].shape
    wg, wu, wd = weights
    units, whole = wg[0].shape[1], 4 * rows
    columns = pl.BlockSpec((whole, TILE), lambda f, s: (0, f))
    return pl.pallas_call(
        functools.partial(mlp_fwd_kernel, layer),
        grid_spec=pltpu.PrefetchScalarGridSpec(
            num_scalar_prefetch=1,
            grid=(units // TILE,),
            in_specs=[whole_spec((rows, depth))] * 4
            + pair_specs(layer, wg[0].shape, 1, TILE)
            + pair_specs(layer, wu[0].shape, 1, TILE)
            + pair_specs(layer, wd[0].shape, 0, TILE),
            out_specs=[whole_spec((rows, depth))] * 4 + [whole_spec((whole, depth)), columns, columns],
            scratch_shapes=[pltpu.VMEM((whole, depth), F32)],
        ),
        out_shape=[shaped((rows, depth), BF)] * 4
        + [shaped((whole, depth), BF), shaped((whole, units), BF), shaped((whole, units), BF)],
        compiler_params=pltpu.CompilerParams(vmem_limit_bytes=LIMIT),
        cost_estimate=cost(6 * whole * units * depth, 30e6),
    )(sec, *blocks, *wg, *wu, *wd)


def mlp_bwd_kernel(
    layer, s_ref, g0, g1, g2, g3, gate_ref, up_ref, wg_a, wg_b, wu_a, wu_b, wd_a, wd_b,
    p0, p1, p2, p3, g_out, total,
):
    f = pl.program_id(0)
    rows = g0.shape[0]

    @pl.when(f == 0)
    def _():
        for n, g in enumerate((g0, g1, g2, g3)):
            g_out[n * rows : (n + 1) * rows, :] = g[...]
        total[...] = jnp.zeros_like(total)

    def work(wg, wu, wd):
        d_hidden = nt(g_out[...], wd[...])
        gate, up = gate_ref[...].astype(F32), up_ref[...].astype(F32)
        s = jax.nn.sigmoid(gate)
        d_up = (d_hidden * gate * s).astype(BF)
        d_gate = (d_hidden * up * s * (1.0 + gate * (1.0 - s))).astype(BF)
        total[...] += nt(d_gate, wg[...]) + nt(d_up, wu[...])

    mine = s_ref[0] == layer
    pl.when(mine)(lambda: work(wg_a, wu_a, wd_a))
    pl.when(jnp.logical_not(mine))(lambda: work(wg_b, wu_b, wd_b))

    @pl.when(f == pl.num_programs(0) - 1)
    def _():
        for n, part in enumerate((p0, p1, p2, p3)):
            part[...] = total[n * rows : (n + 1) * rows, :].astype(BF)


def mlp_bwd(layer, sec, blocks, gate, up, weights):
    rows, depth = blocks[0].shape
    wg, wu, wd = weights
    units, whole = wg[0].shape[1], 4 * rows
    columns = pl.BlockSpec((whole, TILE), lambda f, s: (0, f))
    return pl.pallas_call(
        functools.partial(mlp_bwd_kernel, layer),
        grid_spec=pltpu.PrefetchScalarGridSpec(
            num_scalar_prefetch=1,
            grid=(units // TILE,),
            in_specs=[whole_spec((rows, depth))] * 4
            + [columns, columns]
            + pair_specs(layer, wg[0].shape, 1, TILE)
            + pair_specs(layer, wu[0].shape, 1, TILE)
            + pair_specs(layer, wd[0].shape, 0, TILE),
            out_specs=[whole_spec((rows, depth))] * 4 + [whole_spec((whole, depth))],
            scratch_shapes=[pltpu.VMEM((whole, depth), F32)],
        ),
        out_shape=[shaped((rows, depth), BF)] * 4 + [shaped((whole, depth), BF)],
        compiler_params=pltpu.CompilerParams(vmem_limit_bytes=LIMIT),
        cost_estimate=cost(6 * whole * units * depth, 30e6),
    )(sec, *blocks, gate, up, *wg, *wu, *wd)


WIDE = 512
CHUNK = 512


def mlp_grads_kernel(x_ref, g_ref, wg, wu, wd, dwg, dwu, dwd):
    c = pl.program_id(1)
    share = dwg.shape[0]
    start = pl.multiple_of(lax.axis_index("dp") * share, share)
    x, g = x_ref[...], g_ref[...]
    gate, up = nn(x, wg[...]), nn(x, wu[...])
    d_hidden = nt(g, wd[...])
    s = jax.nn.sigmoid(gate)
    gated = gate * s
    hidden = (gated * up).astype(BF)
    d_up = (d_hidden * gated).astype(BF)
    d_gate = (d_hidden * up * s * (1.0 + gate * (1.0 - s))).astype(BF)
    x_cut, g_cut = x_ref[:, pl.ds(start, share)], g_ref[:, pl.ds(start, share)]

    @pl.when(c == 0)
    def _():
        dwg[...] = jnp.zeros_like(dwg)
        dwu[...] = jnp.zeros_like(dwu)
        dwd[...] = jnp.zeros_like(dwd)

    dwg[...] += tn(x_cut, d_gate)
    dwu[...] += tn(x_cut, d_up)
    dwd[...] += tn(hidden, g_cut)


def mlp_grads(x, g, wg, wu, wd, groups):
    rows, depth = x.shape
    units, share = wg.shape[1], depth // groups
    return pl.pallas_call(
        mlp_grads_kernel,
        grid=(units // WIDE, rows // CHUNK),
        in_specs=[
            pl.BlockSpec((CHUNK, depth), lambda f, c: (c, 0)),
            pl.BlockSpec((CHUNK, depth), lambda f, c: (c, 0)),
            pl.BlockSpec((depth, WIDE), lambda f, c: (0, f)),
            pl.BlockSpec((depth, WIDE), lambda f, c: (0, f)),
            pl.BlockSpec((WIDE, depth), lambda f, c: (f, 0)),
        ],
        out_specs=[
            pl.BlockSpec((share, WIDE), lambda f, c: (0, f)),
            pl.BlockSpec((share, WIDE), lambda f, c: (0, f)),
            pl.BlockSpec((WIDE, share), lambda f, c: (f, 0)),
        ],
        out_shape=[shaped((share, units), F32), shaped((share, units), F32), shaped((units, share), F32)],
        compiler_params=pltpu.CompilerParams(vmem_limit_bytes=LIMIT),
        cost_estimate=cost(6 * rows * units * (depth + share), 100e6),
    )(x, g, wg, wu, wd)


def rope_tables(places, head_size):
    half_width = head_size // 2
    counter = jnp.arange(half_width, dtype=F32)
    base_freq = 1.0 / 500000.0 ** (2.0 * counter / head_size)
    wavelength = 2.0 * jnp.pi / base_freq
    blend_part = (8192.0 / wavelength - 1.0) / 3.0
    middle = (1.0 - blend_part) * base_freq / 32.0 + blend_part * base_freq
    frequency = jnp.where(
        wavelength < 2048.0, base_freq, jnp.where(wavelength > 8192.0, base_freq / 32.0, middle)
    )
    angles = places.astype(F32)[:, None] * frequency[None, :]
    cosine, sine = jnp.cos(angles), jnp.sin(angles)
    return (
        jnp.concatenate([cosine] * 4, axis=1),
        jnp.concatenate([-sine, sine, -sine, sine], axis=1),
    )


def summed_shares(parts, tensor_size, groups):
    kinds, depth = parts.shape
    t, i = lax.axis_index("tensor"), lax.axis_index("dp")
    share = depth // (tensor_size * groups)
    cut = parts.reshape(kinds, groups, tensor_size, share)
    total = lax.dynamic_index_in_dim(cut, t, 2, False)
    for k, pairs in enumerate(partners(tensor_size), 1):
        total = total + lax.ppermute(lax.dynamic_index_in_dim(cut, t ^ k, 2, False), "tensor", pairs)
    mine = lax.dynamic_index_in_dim(total, i, 1, False)
    for k in range(1, groups):
        pairs = [(a, (a + k) % groups) for a in range(groups)]
        send = lax.dynamic_index_in_dim(total, lax.rem(i + k, groups), 1, False)
        mine = mine + lax.ppermute(send, "dp", pairs)
    return mine


def attend_grads(sec, groups, x, att, dm, dq, dk, dv):
    depth = x.shape[1]
    d_qkv = jnp.concatenate([dq, dk, dv], axis=1)
    cut = x.reshape(x.shape[0], groups, 2, depth // (2 * groups))
    halves = [cut[:, :, c].reshape(x.shape[0], depth // 2) for c in range(2)]
    half_att = [att[:, : att.shape[1] // 2], att[:, att.shape[1] // 2 :]]
    first = sec == 0
    keep_x, send_x = jnp.where(first, halves[0], halves[1]), jnp.where(first, halves[1], halves[0])
    keep_a = jnp.where(first, half_att[0], half_att[1])
    send_a = jnp.where(first, half_att[1], half_att[0])
    in_grad = tn(keep_x, d_qkv) + tn(swapped(send_x), swapped(d_qkv))
    out_grad = tn(keep_a, dm) + tn(swapped(send_a), swapped(dm))
    return (
        lax.psum_scatter(in_grad.astype(BF), "dp", scatter_dimension=0, tiled=True),
        lax.psum_scatter(out_grad.astype(BF), "dp", scatter_dimension=1, tiled=True),
    )


def local(groups, size, tokens, lengths, cotangent, attn_gain, mlp_gain, *weights):
    sec, t = lax.axis_index("section"), lax.axis_index("tensor")
    first = sec == 0
    rows, depth = tokens.shape[1:]
    mine = [w[0] for w in weights]
    gains = jnp.concatenate([attn_gain, mlp_gain], axis=0)
    other_gains = swapped(gains)
    pairs = [(w, swapped(w)) for w in mine]
    attn_w, mlp_w = pairs[:4], pairs[4:]
    layer_gains = [jnp.where(sec == l, gains, other_gains) for l in range(2)]
    attn_gains = [g[0:1] for g in layer_gains]
    mlp_gains = [g[1:2] for g in layer_gains]
    length = lax.dynamic_index_in_dim(lengths[:, 0], sec, 0, keepdims=False)
    tok = lax.dynamic_index_in_dim(tokens, sec, 0, keepdims=False)
    cot = lax.dynamic_index_in_dim(cotangent, sec, 0, keepdims=False)
    within = jnp.arange(rows, dtype=jnp.int32)
    own_places = t * rows + within
    places = jnp.concatenate([(t ^ k) * rows + within for k in range(size)])
    readable = jnp.where(places < length, places, jnp.int32(1 << 20))
    tables = rope_tables(places, HD) + (places[:, None], readable[None, :])
    sec_ref = sec.reshape(1).astype(jnp.int32)

    def over_groups(x):
        return lax.all_gather(x, "dp", axis=0, tiled=True)

    g_low = jnp.where((own_places < length)[:, None], cot, jnp.zeros_like(cot))
    g_blocks = gather_rows(g_low, size)

    stream, acts, kept = tok, [], []
    normed = norm_rows(tok, attn_gains[0])
    for l in range(2):
        *parts, x_attn, q, k, v, att = attend_fwd(l, gather_rows(normed, size), attn_w, tables)
        mid, normed = add_norm(stream, scatter_rows(parts, size), mlp_gains[l], False)
        *parts, x_mlp, gate, up = mlp_fwd(l, sec_ref, gather_rows(normed, size), mlp_w)
        act, normed = add_norm(mid, scatter_rows(parts, size), attn_gains[1], True)
        kept.append((stream, x_attn, q, k, v, att, mid, x_mlp, gate, up))
        acts.append(act)
        stream = act

    d_res = g_low
    input_grads, gain_parts, attn_shares, xs, gs = [None] * 2, [None] * 2, [None] * 2, [None] * 2, [None] * 2
    for l in (1, 0):
        stream, x_attn, q, k, v, att, mid, x_mlp, gate, up = kept[l]
        if l == 0:
            g_blocks = gather_rows(d_res, size)
        *parts, g_all = mlp_bwd(l, sec_ref, g_blocks, gate, up, mlp_w)
        d_mid, d_mid_low, mlp_part = norm_back(mid, scatter_rows(parts, size), mlp_gains[l], d_res)
        *parts, dm, dq, dk, dv = attend_bwd(l, gather_rows(d_mid_low, size), (q, k, v), attn_w, tables)
        d_stream, d_low, attn_part = norm_back(stream, scatter_rows(parts, size), attn_gains[l], d_mid)
        attn_shares[l] = attend_grads(sec, groups, x_attn, att, dm, dq, dk, dv)
        xs[l], gs[l] = over_groups(x_mlp), over_groups(g_all)
        input_grads[l], gain_parts[l], d_res = d_stream, (attn_part, mlp_part), d_low

    def for_layer(pair):
        keep, send = jnp.where(first, pair[0], pair[1]), jnp.where(first, pair[1], pair[0])
        return keep, swapped(send)

    def both(pair):
        keep, came = for_layer(pair)
        return jnp.stack([jnp.where(first, keep, came), jnp.where(first, came, keep)])

    x = jnp.concatenate(for_layer(xs), axis=0)
    g = jnp.concatenate(for_layer(gs), axis=0)
    gate_grad, up_grad, down_grad = mlp_grads(x, g, *mine[4:], groups)
    in_rows = jnp.concatenate(list(both([s[0] for s in attn_shares])), axis=0).astype(F32)
    out_grad = jnp.concatenate(list(both([s[1] for s in attn_shares])), axis=0).astype(F32)
    width, narrow = mine[0].shape[1], mine[1].shape[1]
    keep, came = for_layer([jnp.concatenate(parts, axis=0) for parts in gain_parts])
    shares = summed_shares(keep + came, size, groups)
    return (
        both(acts)[None],
        both(input_grads)[None],
        shares[0:1],
        shares[1:2],
        in_rows[None, :, :width],
        in_rows[None, :, width : width + narrow],
        in_rows[None, :, width + narrow :],
        out_grad[None],
        gate_grad[None],
        up_grad[None],
        down_grad[None],
    )


def solution(mesh):
    rows = P(None, ("dp", "tensor"), None)
    in_specs = (
        rows,
        P(None, "dp"),
        rows,
        P("section", None),
        P("section", None),
        P("section", None, "tensor"),
        P("section", None, "tensor"),
        P("section", None, "tensor"),
        P("section", "tensor", None),
        P("section", None, "tensor"),
        P("section", None, "tensor"),
        P("section", "tensor", None),
    )
    out_rows = P("section", None, ("dp", "tensor"), None)
    shares = P("section", ("dp", "tensor"))
    by_dp, by_tensor = P("section", "dp", "tensor"), P("section", "tensor", "dp")
    out_specs = (
        out_rows, out_rows, shares, shares, by_dp, by_dp, by_dp, by_tensor, by_dp, by_dp, by_tensor,
    )
    step = functools.partial(local, mesh.shape["dp"], mesh.shape["tensor"])
    return jax.shard_map(step, mesh=mesh, in_specs=in_specs, out_specs=out_specs, check_vma=False)
```

```python
import functools

import jax
import jax.numpy as jnp
from jax import lax
from jax.experimental import pallas as pl
from jax.experimental.pallas import tpu as pltpu
from jax.sharding import PartitionSpec as P

HD = 64
EPSILON = 1e-05
NEGATIVE = -1e30
BF = jnp.bfloat16
F32 = jnp.float32
VMEM = pl.BlockSpec(memory_space=pltpu.VMEM)
HBM = pl.BlockSpec(memory_space=pltpu.HBM)
ANY = pl.BlockSpec(memory_space=pl.ANY)
MIB = 1024 * 1024
SHRINK = 50


def nn(a, b):
    return jnp.dot(a, b, preferred_element_type=F32)


def nt(a, b):
    return lax.dot_general(a, b, (((1,), (1,)), ((), ())), preferred_element_type=F32)


def tn(a, b):
    return lax.dot_general(a, b, (((0,), (0,)), ((), ())), preferred_element_type=F32)


def shaped(shape, dtype):
    return jax.ShapeDtypeStruct(shape, dtype)


def far(shape, dtype=BF):
    return pltpu.HBM(shape, dtype)


def in_hbm(*arrays):
    return [pltpu.with_memory_space_constraint(a, pltpu.HBM) for a in arrays]


def tied(first, *others):
    return lax.optimization_barrier((first, *others))[0]


def cost(flops, nbytes):
    return pl.CostEstimate(flops=int(flops / SHRINK), bytes_accessed=int(nbytes / SHRINK), transcendentals=0)


def partners(size):
    return [[(a, a ^ k) for a in range(size)] for k in range(1, size)]


def gather_rows(x, size):
    return [x] + [lax.ppermute(x, "tensor", pairs) for pairs in partners(size)]


def scatter_rows(parts, size):
    return [parts[0]] + [
        lax.ppermute(part, "tensor", pairs) for part, pairs in zip(parts[1:], partners(size))
    ]


def swapped(x):
    return lax.ppermute(x, "section", [(0, 1), (1, 0)])


def norm_kernel(x_ref, gain_ref, out_ref):
    x = x_ref[...].astype(F32)
    scale = lax.rsqrt(jnp.mean(x * x, axis=-1, keepdims=True) + EPSILON)
    out_ref[...] = (x * scale * gain_ref[...]).astype(BF)


def norm_rows(x, gain):
    return pl.pallas_call(
        norm_kernel, name="norm", cost_estimate=cost(0, 1e6), out_shape=shaped(x.shape, BF), in_specs=[VMEM] * 2, out_specs=VMEM
    )(x, gain)


def add_norm_kernel(round_out, base_ref, a_ref, b_ref, c_ref, d_ref, gain_ref, out_ref, normed_ref):
    x = base_ref[...].astype(F32) + (
        (a_ref[...].astype(F32) + b_ref[...].astype(F32))
        + (c_ref[...].astype(F32) + d_ref[...].astype(F32))
    )
    if round_out:
        x = x.astype(BF)
        out_ref[...] = x
        x = x.astype(F32)
    else:
        out_ref[...] = x
    scale = lax.rsqrt(jnp.mean(x * x, axis=-1, keepdims=True) + EPSILON)
    normed_ref[...] = (x * scale * gain_ref[...]).astype(BF)


def add_norm(base, terms, gain, round_out):
    return pl.pallas_call(
        functools.partial(add_norm_kernel, round_out),
        name="add_norm",
        cost_estimate=cost(0, 2e6),
        out_shape=(shaped(base.shape, BF if round_out else F32), shaped(base.shape, BF)),
        in_specs=[VMEM] * 6,
        out_specs=(VMEM, VMEM),
    )(base, *terms, gain)


def norm_back_kernel(base_ref, a_ref, b_ref, c_ref, d_ref, gain_ref, res_ref, out_ref, low_ref, gp_ref):
    g = (a_ref[...].astype(F32) + b_ref[...].astype(F32)) + (
        c_ref[...].astype(F32) + d_ref[...].astype(F32)
    )
    x = base_ref[...].astype(F32)
    scale = lax.rsqrt(jnp.mean(x * x, axis=-1, keepdims=True) + EPSILON)
    y = x * scale
    gp_ref[...] = jnp.sum(g * y, axis=0, keepdims=True)
    e = g * gain_ref[...]
    out = res_ref[...].astype(F32) + scale * (e - y * jnp.mean(e * y, axis=-1, keepdims=True))
    out_ref[...] = out
    low_ref[...] = out.astype(BF)


def norm_back(base, terms, gain, residual):
    return pl.pallas_call(
        norm_back_kernel,
        name="norm_back",
        cost_estimate=cost(0, 3e6),
        out_shape=(shaped(base.shape, F32), shaped(base.shape, BF), shaped((1, base.shape[1]), F32)),
        in_specs=[VMEM] * 7,
        out_specs=(VMEM,) * 3,
    )(base, *terms, gain, residual)


def prefetch_kernel(layer, cuts, after_ref, *refs):
    sources, refs = refs[: 2 * len(cuts)], refs[2 * len(cuts) :]
    total = sum(len(cut) - 1 for cut in cuts)
    buffers, token, sems = refs[:total], refs[total], refs[-1]
    token[...] = jnp.zeros_like(token)
    mine = lax.axis_index("section") == layer

    def copies(side):
        moves = []
        for source, cut in zip(sources[side::2], cuts):
            for at, to in zip(cut, cut[1:]):
                n = len(moves)
                part = source.at[pl.ds(at, to - at), :]
                moves.append(pltpu.make_async_copy(part, buffers[n], sems.at[n]))
        return moves

    @pl.when(mine)
    def _():
        for copy in copies(0):
            copy.start()

    @pl.when(jnp.logical_not(mine))
    def _():
        for copy in copies(1):
            copy.start()

    for copy in copies(0):
        copy.wait()


def prefetch(layer, pairs, cuts, after):
    shapes = [
        (to - at, own.shape[1]) for (own, _), cut in zip(pairs, cuts) for at, to in zip(cut, cut[1:])
    ]
    return pl.pallas_call(
        functools.partial(prefetch_kernel, layer, cuts),
        out_shape=[pltpu.VMEM(shape, BF) for shape in shapes] + [shaped((8, 128), F32)],
        in_specs=[ANY] + [HBM] * (2 * len(pairs)),
        out_specs=[VMEM] * (len(shapes) + 1),
        scratch_shapes=[pltpu.SemaphoreType.DMA((len(shapes),))],
        compiler_params=pltpu.CompilerParams(vmem_limit_bytes=MIB),
        cost_estimate=cost(0, sum(4 * a * b for a, b in shapes)),
        name="prefetch",
    )(after, *in_hbm(*[w for pair in pairs for w in pair]))


def turn(x, cos, sin, low):
    return x * cos + jnp.where(low, pltpu.roll(x, 96, 1), pltpu.roll(x, 32, 1)) * sin


def spread(x, first_lanes):
    x = x.astype(F32)
    moved = pltpu.roll(x, 64, 1)
    zero = jnp.zeros_like(x)
    return [
        (jnp.where(first_lanes, x, zero).astype(BF), jnp.where(first_lanes, zero, moved).astype(BF)),
        (jnp.where(first_lanes, moved, zero).astype(BF), jnp.where(first_lanes, zero, x).astype(BF)),
    ]


def soft(q, k, mask):
    scores = jnp.where(mask, nt(q, k) * HD**-0.5, NEGATIVE)
    lifted = jnp.exp(scores - jnp.max(scores, axis=-1, keepdims=True))
    return lifted * (1.0 / jnp.sum(lifted, axis=-1, keepdims=True))


class Rows:
    def __init__(self, blocks, buffer, sems, *kept):
        rows = blocks[0].shape[0]
        self.come = [
            pltpu.make_async_copy(b, buffer.at[pl.ds(n * rows, rows), :], sems.at[n])
            for n, b in enumerate(blocks)
        ]
        self.go = []
        for ref, order in kept:
            for at, n in enumerate(order):
                source, target = buffer.at[pl.ds(n * rows, rows), :], ref.at[pl.ds(at * rows, rows), :]
                sem = sems.at[len(blocks) + len(self.go)]
                self.go.append(pltpu.make_async_copy(source, target, sem))
        for copy in self.come:
            copy.start()

    def ready(self):
        for copy in self.come:
            copy.wait()
        for copy in self.go:
            copy.start()

    def end(self):
        for copy in self.go:
            copy.wait()


ALL = (0, 1, 2, 3)


COLUMNS = 512


def attend_fwd_kernel(
    x0, x1, x2, x3, w_in, wo, cos_ref, sin_ref, pq_ref, pk_ref,
    p0, p1, p2, p3, x_kept, q_out, k_out, v_out, att_out, x_all, sems,
):
    rows = x0.shape[0]
    held = Rows((x0, x1, x2, x3), x_all, sems, (x_kept, ALL))
    whole = 4 * rows
    lane = lax.broadcasted_iota(jnp.int32, (whole, 128), 1)
    low = (lane & (HD - 1)) < HD // 2
    first_lanes = lane < HD
    cos, sin = cos_ref[...], sin_ref[...]
    mask = pk_ref[...] <= pq_ref[...]
    held.ready()
    x = x_all[...]
    width, narrow = q_out.shape[1], k_out.shape[1]
    k = turn(nn(x, w_in[:, width : width + narrow]), cos, sin, low).astype(BF)
    v = nn(x, w_in[:, width + narrow :]).astype(BF)
    k_out[...] = k
    v_out[...] = v
    keys, values = spread(k, first_lanes), spread(v, first_lanes)
    for p in range(q_out.shape[1] // 128):
        cut = slice(p * 128, (p + 1) * 128)
        q = turn(nn(x, w_in[:, cut]), cos, sin, low).astype(BF)
        q_out[:, cut] = q
        head = p // 2
        att_out[:, cut] = (
            nn(soft(q, keys[head][0], mask).astype(BF), values[head][0])
            + nn(soft(q, keys[head][1], mask).astype(BF), values[head][1])
        ).astype(BF)
    att = att_out[...]
    for c in range(p0.shape[1] // COLUMNS):
        cut = slice(c * COLUMNS, (c + 1) * COLUMNS)
        out = nn(att, wo[:, cut]).astype(BF)
        for n, part in enumerate((p0, p1, p2, p3)):
            part[:, cut] = out[n * rows : (n + 1) * rows, :]
    held.end()


def attend_fwd(blocks, weights, tables):
    rows, depth = blocks[0].shape
    whole, width = 4 * rows, weights[1].shape[0]
    narrow = (weights[0].shape[1] - width) // 2
    block = shaped((rows, depth), BF)
    return pl.pallas_call(
        attend_fwd_kernel,
        out_shape=(block,) * 4
        + (
            far((whole, depth)),
            shaped((whole, width), BF),
            shaped((whole, narrow), BF),
            shaped((whole, narrow), BF),
            shaped((whole, width), BF),
        ),
        in_specs=[HBM] * 4 + [VMEM] * 6,
        out_specs=(VMEM,) * 4 + (HBM,) + (VMEM,) * 4,
        scratch_shapes=[pltpu.VMEM((whole, depth), BF), pltpu.SemaphoreType.DMA((8,))],
        compiler_params=pltpu.CompilerParams(vmem_limit_bytes=12 * MIB),
        cost_estimate=cost(5e9, 12e6),
        name="attend_fwd",
    )(*in_hbm(*blocks), *weights, *tables)


def attend_bwd_kernel(
    d0, d1, d2, d3, q_ref, k_ref, v_ref, w_in, wo, cos_ref, sin_ref, pq_ref, pk_ref,
    p0, p1, p2, p3, dm_kept, d_out, dm_all, sems,
):
    rows = d0.shape[0]
    held = Rows((d0, d1, d2, d3), dm_all, sems, (dm_kept, ALL))
    width, narrow = q_ref.shape[1], k_ref.shape[1]
    whole = 4 * rows
    lane = lax.broadcasted_iota(jnp.int32, (whole, 128), 1)
    low = (lane & (HD - 1)) < HD // 2
    first_lanes = lane < HD
    cos, sin = cos_ref[...], -sin_ref[...]
    mask = pk_ref[...] <= pq_ref[...]
    keys, values = spread(k_ref[...], first_lanes), spread(v_ref[...], first_lanes)
    held.ready()
    dm = dm_all[...]
    dk_sums, dv_sums = [[None, None], [None, None]], [[None, None], [None, None]]

    def add(sums, head, side, term):
        sums[head][side] = term if sums[head][side] is None else sums[head][side] + term

    for p in range(q_ref.shape[1] // 128):
        cut = slice(p * 128, (p + 1) * 128)
        head = p // 2
        q = q_ref[:, cut]
        d_att = nt(dm, wo[cut, :]).astype(BF)
        d_q = None
        for side in range(2):
            probs = soft(q, keys[head][side], mask)
            d_probs = nt(d_att, values[head][side])
            inner = jnp.sum(d_probs * probs, axis=-1, keepdims=True)
            d_raw = (probs * (d_probs - inner) * HD**-0.5).astype(BF)
            term = nn(d_raw, keys[head][side])
            d_q = term if d_q is None else d_q + term
            add(dk_sums, head, side, tn(d_raw, q))
            add(dv_sums, head, side, tn(probs.astype(BF), d_att))
        d_out[:, cut] = turn(d_q, cos, sin, low).astype(BF)

    def folded(sums):
        return jnp.where(
            first_lanes,
            sums[0][0] + pltpu.roll(sums[0][1], 64, 1),
            pltpu.roll(sums[1][0], 64, 1) + sums[1][1],
        )

    dk = turn(folded(dk_sums), cos, sin, low).astype(BF)
    dv = folded(dv_sums).astype(BF)
    d_out[:, width : width + narrow] = dk
    d_out[:, width + narrow :] = dv
    for c in range(p0.shape[1] // COLUMNS):
        cut = slice(c * COLUMNS, (c + 1) * COLUMNS)
        out = nt(d_out[...], w_in[cut, :]).astype(BF)
        for n, part in enumerate((p0, p1, p2, p3)):
            part[:, cut] = out[n * rows : (n + 1) * rows, :]
    held.end()


def attend_bwd(blocks, qkv, weights, tables):
    rows, depth = blocks[0].shape
    whole, width = 4 * rows, weights[1].shape[0]
    narrow = (weights[0].shape[1] - width) // 2
    block = shaped((rows, depth), BF)
    return pl.pallas_call(
        attend_bwd_kernel,
        out_shape=(block,) * 4
        + (far((whole, depth)), shaped((whole, width + 2 * narrow), BF)),
        in_specs=[HBM] * 4 + [VMEM] * 9,
        out_specs=(VMEM,) * 4 + (HBM, VMEM),
        scratch_shapes=[pltpu.VMEM((whole, depth), BF), pltpu.SemaphoreType.DMA((8,))],
        compiler_params=pltpu.CompilerParams(vmem_limit_bytes=14 * MIB),
        cost_estimate=cost(7e9, 14e6),
        name="attend_bwd",
    )(*in_hbm(*blocks), *qkv, *weights, *tables)


TILE = 512


def mlp_fwd_kernel(
    x0, x1, x2, x3, wg, wu, wd, p0, p1, p2, p3, gate_out, up_out, x_kept, x_all, total, sems
):
    rows = x0.shape[0]
    held = Rows((x0, x1, x2, x3), x_all, sems, (x_kept, (0, 2)))
    held.ready()

    def step(f, first):
        cut = slice(0, TILE) if first else pl.ds(pl.multiple_of(f * TILE, TILE), TILE)
        x = x_all[...]
        gate, up = nn(x, wg[:, cut]), nn(x, wu[:, cut])
        gate_out[:, cut] = gate.astype(BF)
        up_out[:, cut] = up.astype(BF)
        term = nn((gate * jax.nn.sigmoid(gate) * up).astype(BF), wd[cut, :])
        total[...] = term if first else total[...] + term

    step(0, True)
    pl.loop(1, wg.shape[1] // TILE)(lambda f: step(f, False))
    for n, part in enumerate((p0, p1, p2, p3)):
        part[...] = total[n * rows : (n + 1) * rows, :].astype(BF)
    held.end()


def mlp_fwd(blocks, weights):
    rows, depth = blocks[0].shape
    units, whole = weights[0].shape[1], 4 * rows
    return pl.pallas_call(
        mlp_fwd_kernel,
        in_specs=[HBM] * 4 + [VMEM] * 3,
        out_specs=[VMEM] * 6 + [HBM],
        scratch_shapes=[
            pltpu.VMEM((whole, depth), BF),
            pltpu.VMEM((whole, depth), F32),
            pltpu.SemaphoreType.DMA((8,)),
        ],
        out_shape=[shaped((rows, depth), BF)] * 4
        + [shaped((whole, units), BF)] * 2
        + [far((whole // 2, depth))],
        compiler_params=pltpu.CompilerParams(vmem_limit_bytes=12 * MIB),
        cost_estimate=cost(6 * whole * units * depth, 30e6),
        name="mlp_fwd",
    )(*in_hbm(*blocks), *weights)


def mlp_bwd_kernel(
    g0, g1, g2, g3, gate_ref, up_ref, wg, wu, wd, p0, p1, p2, p3, g_kept, g_all, total, sems
):
    rows = g0.shape[0]
    held = Rows((g0, g1, g2, g3), g_all, sems, (g_kept, ALL))
    held.ready()

    def step(f, first):
        cut = slice(0, TILE) if first else pl.ds(pl.multiple_of(f * TILE, TILE), TILE)
        d_hidden = nt(g_all[...], wd[cut, :])
        gate, up = gate_ref[:, cut].astype(F32), up_ref[:, cut].astype(F32)
        s = jax.nn.sigmoid(gate)
        d_up = (d_hidden * gate * s).astype(BF)
        d_gate = (d_hidden * up * s * (1.0 + gate * (1.0 - s))).astype(BF)
        term = nt(d_gate, wg[:, cut]) + nt(d_up, wu[:, cut])
        total[...] = term if first else total[...] + term

    step(0, True)
    pl.loop(1, wg.shape[1] // TILE)(lambda f: step(f, False))
    for n, part in enumerate((p0, p1, p2, p3)):
        part[...] = total[n * rows : (n + 1) * rows, :].astype(BF)
    held.end()


def mlp_bwd(blocks, gate, up, weights):
    rows, depth = blocks[0].shape
    units, whole = weights[0].shape[1], 4 * rows
    return pl.pallas_call(
        mlp_bwd_kernel,
        in_specs=[HBM] * 4 + [VMEM] * 5,
        out_specs=[VMEM] * 4 + [HBM],
        scratch_shapes=[
            pltpu.VMEM((whole, depth), BF),
            pltpu.VMEM((whole, depth), F32),
            pltpu.SemaphoreType.DMA((8,)),
        ],
        out_shape=[shaped((rows, depth), BF)] * 4 + [far((whole, depth))],
        compiler_params=pltpu.CompilerParams(vmem_limit_bytes=12 * MIB),
        cost_estimate=cost(6 * whole * units * depth, 30e6),
        name="mlp_bwd",
    )(*in_hbm(*blocks), gate, up, *weights)


def mlp_both_kernel(
    x0, x1, x2, x3, g0, g1, g2, g3, wg, wu, wd,
    p0, p1, p2, p3, r0, r1, r2, r3, x_kept, x_all, g_all, gate_all, up_all, total, x_sems, g_sems,
):
    rows = x0.shape[0]
    held = Rows((x0, x1, x2, x3), x_all, x_sems, (x_kept, ALL))
    held_g = Rows((g0, g1, g2, g3), g_all, g_sems)
    held.ready()

    def tile(f, first):
        return slice(0, TILE) if first else pl.ds(pl.multiple_of(f * TILE, TILE), TILE)

    def forward(f, first):
        cut = tile(f, first)
        x = x_all[...]
        gate, up = nn(x, wg[:, cut]), nn(x, wu[:, cut])
        gate_all[:, cut] = gate.astype(BF)
        up_all[:, cut] = up.astype(BF)
        term = nn((gate * jax.nn.sigmoid(gate) * up).astype(BF), wd[cut, :])
        total[...] = term if first else total[...] + term

    def backward(f, first):
        cut = tile(f, first)
        d_hidden = nt(g_all[...], wd[cut, :])
        gate, up = gate_all[:, cut].astype(F32), up_all[:, cut].astype(F32)
        s = jax.nn.sigmoid(gate)
        d_up = (d_hidden * gate * s).astype(BF)
        d_gate = (d_hidden * up * s * (1.0 + gate * (1.0 - s))).astype(BF)
        term = nt(d_gate, wg[:, cut]) + nt(d_up, wu[:, cut])
        total[...] = term if first else total[...] + term

    for step, parts in ((forward, (p0, p1, p2, p3)), (backward, (r0, r1, r2, r3))):
        step(0, True)
        pl.loop(1, wg.shape[1] // TILE)(lambda f: step(f, False))
        for n, part in enumerate(parts):
            part[...] = total[n * rows : (n + 1) * rows, :].astype(BF)
        if step is forward:
            held_g.ready()
    held.end()


def mlp_both(blocks, g_blocks, weights):
    rows, depth = blocks[0].shape
    units, whole = weights[0].shape[1], 4 * rows
    return pl.pallas_call(
        mlp_both_kernel,
        in_specs=[HBM] * 8 + [VMEM] * 3,
        out_specs=[VMEM] * 8 + [HBM],
        scratch_shapes=[
            pltpu.VMEM((whole, depth), BF),
            pltpu.VMEM((whole, depth), BF),
            pltpu.VMEM((whole, units), BF),
            pltpu.VMEM((whole, units), BF),
            pltpu.VMEM((whole, depth), F32),
            pltpu.SemaphoreType.DMA((8,)),
            pltpu.SemaphoreType.DMA((4,)),
        ],
        out_shape=[shaped((rows, depth), BF)] * 8 + [far((whole, depth))],
        compiler_params=pltpu.CompilerParams(vmem_limit_bytes=14 * MIB),
        cost_estimate=cost(12 * whole * units * depth, 30e6),
        name="mlp_both",
    )(*in_hbm(*blocks, *g_blocks), *weights)


PIECE = 512


def mlp_grads_kernel(layer, f, first, last, x_orders, g_orders, *refs):
    n_x, n_g = len(x_orders), len(g_orders)
    x_refs, g_refs, refs = refs[:n_x], refs[n_x : n_x + n_g], refs[n_x + n_g :]
    *weights, out = refs[:7]
    wg, wu, wd, x_all, g_all, total, w_sems, sems = refs[7:]
    share = out.shape[0]
    units = weights[0].shape[1]
    mine = lax.axis_index("section") == layer
    column = lax.axis_index("section") * (units // 2) + f * PIECE
    cut = pl.ds(pl.multiple_of(column, PIECE), PIECE)
    start = pl.ds(pl.multiple_of(lax.axis_index("dp") * share, share), share)

    def chunk(p, slot):
        moves = []
        for to, arrays, orders in ((x_all, x_refs, x_orders), (g_all, g_refs, g_orders)):
            for a, (half, order) in zip(arrays, orders):
                rows = a.shape[1] // len(order)
                at = p if a.shape[0] > last - first else p - first
                for n, place in enumerate(order):
                    target = to.at[slot, pl.ds((half * 4 + place) * rows, rows), :]
                    source = a.at[at, pl.ds(n * rows, rows), :]
                    moves.append(pltpu.make_async_copy(source, target, sems.at[slot, len(moves)]))
        return moves

    def copies(g, u, d):
        return [
            pltpu.make_async_copy(g.at[:, cut], wg, w_sems.at[0]),
            pltpu.make_async_copy(u.at[:, cut], wu, w_sems.at[1]),
            pltpu.make_async_copy(d.at[cut, :], wd, w_sems.at[2]),
        ]

    @pl.when(mine)
    def _():
        for copy in copies(*weights[0::2]):
            copy.start()

    @pl.when(jnp.logical_not(mine))
    def _():
        for copy in copies(*weights[1::2]):
            copy.start()

    for copy in chunk(first, 0):
        copy.start()
    total[...] = jnp.zeros_like(total)
    for copy in copies(*weights[0::2]):
        copy.wait()

    @pl.loop(first, last)
    def _(p):
        slot = lax.rem(p - first, 2)

        @pl.when(p + 1 < last)
        def _():
            for copy in chunk(p + 1, 1 - slot):
                copy.start()

        for copy in chunk(p, slot):
            copy.wait()
        x = x_all[slot]
        gate, up = nn(x, wg[...]), nn(x, wu[...])
        d_hidden = nt(g_all[slot], wd[...])
        s = jax.nn.sigmoid(gate)
        gated = gate * s
        hidden = (gated * up).astype(BF)
        d_up = (d_hidden * gated).astype(BF)
        d_gate = (d_hidden * up * s * (1.0 + gate * (1.0 - s))).astype(BF)
        x_cut, g_cut = x_all[slot, :, start], g_all[slot, :, start]
        total[:, :PIECE] += tn(x_cut, d_gate)
        total[:, PIECE : 2 * PIECE] += tn(x_cut, d_up)
        total[:, 2 * PIECE :] += tn(g_cut, hidden)

    out[...] = total[...].astype(BF)


def mlp_grads(layer, f, part, xs, gs, pairs):
    groups, _, depth = xs[0][0].shape
    first, last = part * (groups // 2), (part + 1) * (groups // 2)
    rows = sum(a.shape[1] for a, _ in xs)
    share = depth // groups
    return pl.pallas_call(
        functools.partial(
            mlp_grads_kernel, layer, f, first, last, [o for _, o in xs], [o for _, o in gs]
        ),
        in_specs=[HBM] * (len(xs) + len(gs) + 6),
        out_specs=VMEM,
        out_shape=shaped((share, 3 * PIECE), BF),
        scratch_shapes=[
            pltpu.VMEM((depth, PIECE), BF),
            pltpu.VMEM((depth, PIECE), BF),
            pltpu.VMEM((PIECE, depth), BF),
            pltpu.VMEM((2, rows, depth), BF),
            pltpu.VMEM((2, rows, depth), BF),
            pltpu.VMEM((share, 3 * PIECE), F32),
            pltpu.SemaphoreType.DMA((3,)),
            pltpu.SemaphoreType.DMA((2, 16)),
        ],
        compiler_params=pltpu.CompilerParams(vmem_limit_bytes=50 * MIB),
        cost_estimate=cost(3 * rows * groups * PIECE * (depth + share), 20e6),
        name="mlp_grads",
    )(*in_hbm(*[a for a, _ in xs], *[a for a, _ in gs], *[w for pair in pairs for w in pair]))


def assemble_kernel(n, *refs):
    sources, outs, scratch = refs[: 4 * (n + 1)], refs[4 * (n + 1) : 4 * (n + 1) + 7], refs[4 * (n + 1) + 7 :]
    q_out, k_out, v_out, o_out, gate_out, up_out, down_out = outs
    held, attn, in_rows, wide, tall, flat, sems, out_sems = scratch
    sec = lax.axis_index("section")

    def fetches(layer):
        mine = sources[layer * 2 * (n + 1) : (layer + 1) * 2 * (n + 1)]
        moves = []
        for side in range(2):
            for f in range(n + 1):
                source = mine[side * (n + 1) + f]
                target = held.at[side, f] if f < n else attn.at[side]
                moves.append(pltpu.make_async_copy(source, target, sems.at[len(moves)]))
        return moves

    for layer in range(2):

        @pl.when(sec == layer)
        def _(layer=layer):
            for move in fetches(layer):
                move.start()

    for move in fetches(0):
        move.wait()
    share, width = attn.shape[1:]
    columns = in_rows.shape[1] // 2
    half_units = wide.shape[2] // 2
    going = []

    def leave(source, target):
        going.append(pltpu.make_async_copy(source, target, out_sems.at[len(going)]))
        going[-1].start()

    q, k = q_out.shape[1], k_out.shape[1]
    halves = [sec, 1 - sec]
    rest = width - columns
    for side, half in enumerate(halves):
        in_rows[:, pl.ds(pl.multiple_of(half * columns, columns), columns)] = attn[side, :, :columns].astype(F32)
        flat[pl.ds(pl.multiple_of(half * rest, rest), rest), :] = attn[side, :, columns:].astype(F32).T
    leave(flat, o_out)
    leave(in_rows.at[:, pl.ds(0, q)], q_out)
    leave(in_rows.at[:, pl.ds(q, k)], k_out)
    leave(in_rows.at[:, pl.ds(q + k, k)], v_out)
    for kind, (target, out) in enumerate(((wide.at[0], gate_out), (wide.at[1], up_out), (tall, down_out))):
        for side, half in enumerate(halves):
            for f in range(n // 2):
                at = pl.ds(pl.multiple_of(half * half_units + f * PIECE, PIECE), PIECE)
                cut = slice(kind * PIECE, (kind + 1) * PIECE)
                tile = held[side, 2 * f, :, cut].astype(F32) + held[side, 2 * f + 1, :, cut].astype(F32)
                if kind < 2:
                    target[:, at] = tile
                else:
                    target[at, :] = tile.T
        leave(target, out)
    for move in going:
        move.wait()


def assemble(layers, width, narrow, units):
    n = len(layers[0][0])
    share, attn_width = layers[0][1].shape
    depth_out = 2 * attn_width - width - 2 * narrow
    sources = []
    for tiles, part, other_tiles, other_part in layers:
        sources += [*tiles, part, *other_tiles, other_part]
    shapes = [(share, width), (share, narrow), (share, narrow), (depth_out, share)]
    shapes += [(share, units), (share, units), (units, share)]
    return pl.pallas_call(
        functools.partial(assemble_kernel, n),
        in_specs=[HBM] * len(sources),
        out_specs=[HBM] * 7,
        out_shape=[far(shape, F32) for shape in shapes],
        scratch_shapes=[
            pltpu.VMEM((2, n, share, 3 * PIECE), BF),
            pltpu.VMEM((2, share, attn_width), BF),
            pltpu.VMEM((share, width + 2 * narrow), F32),
            pltpu.VMEM((2, share, units), F32),
            pltpu.VMEM((units, share), F32),
            pltpu.VMEM((depth_out, share), F32),
            pltpu.SemaphoreType.DMA((2 * (n + 1),)),
            pltpu.SemaphoreType.DMA((7,)),
        ],
        compiler_params=pltpu.CompilerParams(vmem_limit_bytes=48 * MIB),
        cost_estimate=cost(0, 30e6),
        name="assemble",
    )(*in_hbm(*sources))


def attend_grads_kernel(x_own, x_other, d_own, d_other, m_own, m_other, a_own, a_other, out):
    sec = lax.axis_index("section")
    at = 0
    for left_own, left_other, own, other in (
        (x_own, x_other, d_own, d_other),
        (m_own, m_other, a_own, a_other),
    ):
        width = own.shape[1] // 2
        half = pl.ds(pl.multiple_of(sec * width, width), width)
        out[:, at : at + width] = (tn(left_own[...], own[:, half]) + tn(left_other[...], other[:, half])).astype(BF)
        at += width


def attend_grads(x, d_qkv, d_mid, att):
    depth, width = x.shape[1], (d_qkv.shape[1] + att.shape[1]) // 2
    terms = [x, swapped(x), d_qkv, swapped(d_qkv), d_mid, swapped(d_mid), att, swapped(att)]
    both = pl.pallas_call(
        attend_grads_kernel,
        in_specs=[VMEM] * 8,
        out_specs=VMEM,
        out_shape=shaped((depth, width), BF),
        compiler_params=pltpu.CompilerParams(vmem_limit_bytes=14 * MIB),
        cost_estimate=cost(4 * x.size * width, 6e6),
        name="attend_grads",
    )(*terms)
    return both


def summed_over_groups(x):
    return lax.psum_scatter(x, "dp", scatter_dimension=0, tiled=True)


def rope_tables(places, head_size):
    half_width = head_size // 2
    counter = jnp.arange(half_width, dtype=F32)
    base_freq = 1.0 / 500000.0 ** (2.0 * counter / head_size)
    wavelength = 2.0 * jnp.pi / base_freq
    blend_part = (8192.0 / wavelength - 1.0) / 3.0
    middle = (1.0 - blend_part) * base_freq / 32.0 + blend_part * base_freq
    frequency = jnp.where(
        wavelength < 2048.0, base_freq, jnp.where(wavelength > 8192.0, base_freq / 32.0, middle)
    )
    angles = places.astype(F32)[:, None] * frequency[None, :]
    cosine, sine = jnp.cos(angles), jnp.sin(angles)
    return (
        jnp.concatenate([cosine] * 4, axis=1),
        jnp.concatenate([-sine, sine, -sine, sine], axis=1),
    )


def halved(total, axis, size, bit, dim):
    low, high = lax.slice_in_dim(total, 0, bit, axis=dim), lax.slice_in_dim(total, bit, 2 * bit, axis=dim)
    upper = (lax.axis_index(axis) & bit) != 0
    keep, send = jnp.where(upper, high, low), jnp.where(upper, low, high)
    return keep + lax.ppermute(send, axis, [(a, a ^ bit) for a in range(size)])


def over_groups(x):
    return lax.all_gather(x, "dp", axis=0, tiled=False)


def from_both_cores(*arrays):
    return [(a, (0, places)) for a, places in arrays] + [(swapped(a), (1, places)) for a, places in arrays]


def local(groups, size, tokens, lengths, cotangent, attn_gain, mlp_gain, *weights):
    sec, t = lax.axis_index("section"), lax.axis_index("tensor")
    first = sec == 0
    rows, depth = tokens.shape[1:]
    mine = [w[0] for w in weights]
    gains = jnp.concatenate([attn_gain, mlp_gain], axis=0)
    other_gains = swapped(gains)
    layer_gains = [jnp.where(sec == l, gains, other_gains) for l in range(2)]
    attn_gains = [g[0:1] for g in layer_gains]
    mlp_gains = [g[1:2] for g in layer_gains]
    length = lax.dynamic_index_in_dim(lengths[:, 0], sec, 0, keepdims=False)
    tok = lax.dynamic_index_in_dim(tokens, sec, 0, keepdims=False)
    cot = lax.dynamic_index_in_dim(cotangent, sec, 0, keepdims=False)
    within = jnp.arange(rows, dtype=jnp.int32)
    own_places = t * rows + within
    places = jnp.concatenate([(t ^ k) * rows + within for k in range(size)])
    readable = jnp.where(places < length, places, jnp.int32(1 << 20))
    tables = rope_tables(places, HD) + (places[:, None], readable[None, :])

    g_low = jnp.where((own_places < length)[:, None], cot, jnp.zeros_like(cot))

    def for_layer(pair):
        keep, send = jnp.where(first, pair[0], pair[1]), jnp.where(first, pair[1], pair[0])
        return keep, swapped(send)

    def both(pair):
        keep, came = for_layer(pair)
        return [jnp.where(first, keep, came), jnp.where(first, came, keep)]

    attn_mine = [jnp.concatenate(mine[:3], axis=1), mine[3]]
    attn_w = [(w, swapped(tied(w, other_gains))) for w in attn_mine]
    attn_cuts = [(0, w.shape[0]) for w in attn_mine]
    g_blocks1 = gather_rows(g_low, size)
    normed = tied(norm_rows(tok, attn_gains[0]), *g_blocks1)
    *weights_in, token = prefetch(0, attn_w, attn_cuts, normed)
    blocks = gather_rows(normed, size)
    all_g1 = jnp.concatenate(g_blocks1, axis=0)
    blocks[0] = tied(blocks[0], all_g1)
    all_g1 = over_groups(all_g1)
    *parts, x_attn0, q0, k0, v0, att0 = attend_fwd(blocks, weights_in, tables)
    gate_other, up_other = [swapped(tied(w, normed, *[o for _, o in attn_w])) for w in mine[4:6]]
    down_other = swapped(tied(mine[6], gate_other, parts[0]))
    mlp_w = list(zip(mine[4:], (gate_other, up_other, down_other)))
    mlp_cuts = [(0, w.shape[0]) for w in mine[4:]]
    mid0, normed = add_norm(tok, scatter_rows(parts, size), mlp_gains[0], False)
    *weights_in, token = prefetch(0, mlp_w, mlp_cuts, normed)
    *parts, gate0, up0, x_half = mlp_fwd(gather_rows(normed, size), weights_in)
    act0, normed = add_norm(mid0, scatter_rows(parts, size), attn_gains[1], True)

    *weights_in, token = prefetch(1, attn_w, attn_cuts, normed)
    *parts, x_attn1, q1, k1, v1, att1 = attend_fwd(gather_rows(normed, size), weights_in, tables)
    parts[0] = tied(parts[0], all_g1)
    half_x0 = over_groups(tied(x_half, all_g1, parts[0]))
    mid1, normed = add_norm(act0, scatter_rows(parts, size), mlp_gains[1], False)
    *weights_in, token = prefetch(1, mlp_w, mlp_cuts, normed)
    *both_parts, x_all = mlp_both(gather_rows(normed, size), g_blocks1, weights_in)
    parts1, parts = both_parts[:size], both_parts[size:]
    parts[0] = tied(parts[0], half_x0)
    all_x1 = over_groups(tied(x_all, half_x0, parts[0]))
    d_mid, d_mid_low, mlp_part1 = norm_back(mid1, scatter_rows(parts, size), mlp_gains[1], g_low)
    *weights_in, token = prefetch(1, attn_w, attn_cuts, d_mid_low)
    *parts, dm, dqkv = attend_bwd(gather_rows(d_mid_low, size), (q1, k1, v1), weights_in, tables)
    attn_terms1 = attend_grads(x_attn1, dqkv, dm, att1)
    came = scatter_rows(parts, size)
    came[0] = tied(came[0], attn_terms1)
    d_stream1, d_low, attn_part1 = norm_back(act0, came, attn_gains[1], d_mid)

    *weights_in, token = prefetch(0, mlp_w, mlp_cuts, d_low)
    *parts, g_all = mlp_bwd(gather_rows(d_low, size), gate0, up0, weights_in)
    parts[0] = tied(parts[0], all_x1)
    all_g0 = over_groups(tied(g_all, all_x1, parts[0]))
    x1, g1 = from_both_cores((all_x1, ALL)), from_both_cores((all_g1, ALL))
    pieces = [(f, part) for f in range(mine[4].shape[1] // (2 * PIECE)) for part in range(2)]
    tiles1 = []

    def piece1(*after):
        f, part = pieces[len(tiles1)]
        tiles1.append(mlp_grads(1, f, part, [(tied(a, *after), o) for a, o in x1], g1, mlp_w))
        return tiles1[-1]

    d_mid, d_mid_low, mlp_part0 = norm_back(mid0, scatter_rows(parts, size), mlp_gains[0], d_low)
    *weights_in, token = prefetch(0, attn_w, attn_cuts, d_mid_low)
    blocks = gather_rows(d_mid_low, size)
    blocks[0] = tied(blocks[0], piece1(d_mid_low, token))
    *parts, dm, dqkv = attend_bwd(blocks, (q0, k0, v0), weights_in, tables)
    attn_terms0 = attend_grads(x_attn0, dqkv, dm, att0)
    x_pair, at = partners(size)[0], groups // 2
    rest_x0 = [lax.ppermute(tied(x, parts[0]), "tensor", x_pair) for x in (half_x0[:at], half_x0[at:])]
    came = scatter_rows(parts, size)
    came[0] = tied(came[0], piece1(parts[0], attn_terms0))
    d_stream0, _, attn_part0 = norm_back(tok, came, attn_gains[0], d_mid)

    attn_share1 = summed_over_groups(tied(attn_terms1, all_g0, d_stream0))
    keep, came = for_layer(
        [jnp.concatenate(p, axis=0) for p in ((attn_part0, mlp_part0), (attn_part1, mlp_part1))]
    )
    shares = (keep + came).reshape(2, groups, size, depth // (groups * size))
    while len(tiles1) < len(pieces):
        piece1(tiles1[-1], d_stream0)
    x0 = from_both_cores((half_x0, (0, 2)))
    x0_rest = [from_both_cores((rest, (1, 3))) for rest in rest_x0]
    g0 = from_both_cores((all_g0, ALL))
    tiles0, others1 = [], [swapped(tile) for tile in tiles1]
    order0 = [(f, part) for part in range(2) for f in range(len(pieces) // 2)]

    def piece0(*after):
        f, part = order0[len(tiles0)]
        tiles0.append(mlp_grads(0, f, part, [(tied(a, *after), o) for a, o in x0 + x0_rest[part]], g0, mlp_w))
        return tiles0[-1]

    while len(tiles0) < len(pieces):
        piece0(tiles1[-1], *tiles0[-1:])
    attn_share0 = summed_over_groups(tied(attn_terms0, attn_share1, tiles0[0]))
    done = iter([tiles1[2], tiles1[3], *tiles0])
    for axis, count, dim in (("tensor", size, 2), ("dp", groups, 1)):
        bit = count // 2
        while bit:
            shares = halved(tied(shares, next(done, tiles0[-1])), axis, count, bit, dim)
            bit //= 2
    shares = shares.reshape(2, -1)
    act1, _ = add_norm(
        mid1, scatter_rows([tied(p, tiles0[1]) for p in parts1], size), attn_gains[1], True
    )
    tiles0 = [tiles0[order0.index(piece)] for piece in pieces]
    others0 = [swapped(tile) for tile in tiles0]
    layers = [
        (tiles0, attn_share0, others0, swapped(attn_share0)),
        (tiles1, attn_share1, others1, swapped(attn_share1)),
    ]
    weight_grads = assemble(layers, mine[0].shape[1], mine[1].shape[1], mine[4].shape[1])
    acts, input_grads = (act0, act1), (d_stream0, d_stream1)

    return (
        jnp.stack(both(acts))[None],
        jnp.stack(both(input_grads))[None],
        shares[0:1],
        shares[1:2],
        *[grad[None] for grad in weight_grads],
    )


def solution(mesh):
    rows = P(None, ("dp", "tensor"), None)
    in_specs = (
        rows,
        P(None, "dp"),
        rows,
        P("section", None),
        P("section", None),
        P("section", None, "tensor"),
        P("section", None, "tensor"),
        P("section", None, "tensor"),
        P("section", "tensor", None),
        P("section", None, "tensor"),
        P("section", None, "tensor"),
        P("section", "tensor", None),
    )
    out_rows = P("section", None, ("dp", "tensor"), None)
    shares = P("section", ("dp", "tensor"))
    by_dp, by_tensor = P("section", "dp", "tensor"), P("section", "tensor", "dp")
    out_specs = (
        out_rows, out_rows, shares, shares, by_dp, by_dp, by_dp, by_tensor, by_dp, by_dp, by_tensor,
    )
    step = functools.partial(local, mesh.shape["dp"], mesh.shape["tensor"])
    return jax.shard_map(step, mesh=mesh, in_specs=in_specs, out_specs=out_specs, check_vma=False)
```

```python
import functools

import jax
import jax.numpy as jnp
from jax import lax
from jax.experimental import pallas as pl
from jax.experimental.pallas import tpu as pltpu
from jax.sharding import PartitionSpec as P

HD = 64
EPSILON = 1e-05
NEGATIVE = -1e30
BF = jnp.bfloat16
F32 = jnp.float32
VMEM = pl.BlockSpec(memory_space=pltpu.VMEM)
HBM = pl.BlockSpec(memory_space=pltpu.HBM)
ANY = pl.BlockSpec(memory_space=pl.ANY)
MIB = 1024 * 1024
SHRINK = 50


def nn(a, b):
    return jnp.dot(a, b, preferred_element_type=F32)


def nt(a, b):
    return lax.dot_general(a, b, (((1,), (1,)), ((), ())), preferred_element_type=F32)


def tn(a, b):
    return lax.dot_general(a, b, (((0,), (0,)), ((), ())), preferred_element_type=F32)


def shaped(shape, dtype):
    return jax.ShapeDtypeStruct(shape, dtype)


def far(shape, dtype=BF):
    return pltpu.HBM(shape, dtype)


def in_hbm(*arrays):
    return [pltpu.with_memory_space_constraint(a, pltpu.HBM) for a in arrays]


def tied(first, *others):
    return lax.optimization_barrier((first, *others))[0]


def cost(flops, nbytes):
    return pl.CostEstimate(flops=int(flops / SHRINK), bytes_accessed=int(nbytes / SHRINK), transcendentals=0)


def partners(size):
    return [[(a, a ^ k) for a in range(size)] for k in range(1, size)]


def gather_rows(x, size):
    return [x] + [lax.ppermute(x, "tensor", pairs) for pairs in partners(size)]


def scatter_rows(parts, size):
    return [parts[0]] + [
        lax.ppermute(part, "tensor", pairs) for part, pairs in zip(parts[1:], partners(size))
    ]


def swapped(x):
    return lax.ppermute(x, "section", [(0, 1), (1, 0)])


def norm_kernel(x_ref, gain_ref, out_ref):
    x = x_ref[...].astype(F32)
    scale = lax.rsqrt(jnp.mean(x * x, axis=-1, keepdims=True) + EPSILON)
    out_ref[...] = (x * scale * gain_ref[...]).astype(BF)


def norm_rows(x, gain):
    return pl.pallas_call(
        norm_kernel, name="norm", cost_estimate=cost(0, 1e6), out_shape=shaped(x.shape, BF), in_specs=[VMEM] * 2, out_specs=VMEM
    )(x, gain)


def add_norm_kernel(round_out, base_ref, a_ref, b_ref, c_ref, d_ref, gain_ref, out_ref, normed_ref):
    x = base_ref[...].astype(F32) + (
        (a_ref[...].astype(F32) + b_ref[...].astype(F32))
        + (c_ref[...].astype(F32) + d_ref[...].astype(F32))
    )
    if round_out:
        x = x.astype(BF)
        out_ref[...] = x
        x = x.astype(F32)
    else:
        out_ref[...] = x
    scale = lax.rsqrt(jnp.mean(x * x, axis=-1, keepdims=True) + EPSILON)
    normed_ref[...] = (x * scale * gain_ref[...]).astype(BF)


def add_norm(base, terms, gain, round_out):
    return pl.pallas_call(
        functools.partial(add_norm_kernel, round_out),
        name="add_norm",
        cost_estimate=cost(0, 2e6),
        out_shape=(shaped(base.shape, BF if round_out else F32), shaped(base.shape, BF)),
        in_specs=[VMEM] * 6,
        out_specs=(VMEM, VMEM),
    )(base, *terms, gain)


def norm_back_kernel(base_ref, a_ref, b_ref, c_ref, d_ref, gain_ref, res_ref, out_ref, low_ref, gp_ref):
    g = (a_ref[...].astype(F32) + b_ref[...].astype(F32)) + (
        c_ref[...].astype(F32) + d_ref[...].astype(F32)
    )
    x = base_ref[...].astype(F32)
    scale = lax.rsqrt(jnp.mean(x * x, axis=-1, keepdims=True) + EPSILON)
    y = x * scale
    gp_ref[...] = jnp.sum(g * y, axis=0, keepdims=True)
    e = g * gain_ref[...]
    out = res_ref[...].astype(F32) + scale * (e - y * jnp.mean(e * y, axis=-1, keepdims=True))
    out_ref[...] = out
    low_ref[...] = out.astype(BF)


def norm_back(base, terms, gain, residual):
    return pl.pallas_call(
        norm_back_kernel,
        name="norm_back",
        cost_estimate=cost(0, 3e6),
        out_shape=(shaped(base.shape, F32), shaped(base.shape, BF), shaped((1, base.shape[1]), F32)),
        in_specs=[VMEM] * 7,
        out_specs=(VMEM,) * 3,
    )(base, *terms, gain, residual)


def prefetch_kernel(layer, cuts, after_ref, *refs):
    sources, refs = refs[: 2 * len(cuts)], refs[2 * len(cuts) :]
    total = sum(len(cut) - 1 for cut in cuts)
    buffers, token, sems = refs[:total], refs[total], refs[-1]
    token[...] = jnp.zeros_like(token)
    mine = lax.axis_index("section") == layer

    def copies(side):
        moves = []
        for source, cut in zip(sources[side::2], cuts):
            for at, to in zip(cut, cut[1:]):
                n = len(moves)
                part = source.at[pl.ds(at, to - at), :]
                moves.append(pltpu.make_async_copy(part, buffers[n], sems.at[n]))
        return moves

    @pl.when(mine)
    def _():
        for copy in copies(0):
            copy.start()

    @pl.when(jnp.logical_not(mine))
    def _():
        for copy in copies(1):
            copy.start()

    for copy in copies(0):
        copy.wait()


def prefetch(layer, pairs, cuts, after):
    shapes = [
        (to - at, own.shape[1]) for (own, _), cut in zip(pairs, cuts) for at, to in zip(cut, cut[1:])
    ]
    return pl.pallas_call(
        functools.partial(prefetch_kernel, layer, cuts),
        out_shape=[pltpu.VMEM(shape, BF) for shape in shapes] + [shaped((8, 128), F32)],
        in_specs=[ANY] + [HBM] * (2 * len(pairs)),
        out_specs=[VMEM] * (len(shapes) + 1),
        scratch_shapes=[pltpu.SemaphoreType.DMA((len(shapes),))],
        compiler_params=pltpu.CompilerParams(vmem_limit_bytes=MIB),
        cost_estimate=cost(0, sum(4 * a * b for a, b in shapes)),
        name="prefetch",
    )(after, *in_hbm(*[w for pair in pairs for w in pair]))


def turn(x, cos, sin, low):
    return x * cos + jnp.where(low, pltpu.roll(x, 96, 1), pltpu.roll(x, 32, 1)) * sin


def spread(x, first_lanes):
    x = x.astype(F32)
    moved = pltpu.roll(x, 64, 1)
    zero = jnp.zeros_like(x)
    return [
        (jnp.where(first_lanes, x, zero).astype(BF), jnp.where(first_lanes, zero, moved).astype(BF)),
        (jnp.where(first_lanes, moved, zero).astype(BF), jnp.where(first_lanes, zero, x).astype(BF)),
    ]


def soft(q, k, mask):
    scores = jnp.where(mask, nt(q, k) * HD**-0.5, NEGATIVE)
    lifted = jnp.exp(scores - jnp.max(scores, axis=-1, keepdims=True))
    return lifted * (1.0 / jnp.sum(lifted, axis=-1, keepdims=True))


class Rows:
    def __init__(self, blocks, buffer, sems, *kept):
        rows = blocks[0].shape[0]
        self.come = [
            pltpu.make_async_copy(b, buffer.at[pl.ds(n * rows, rows), :], sems.at[n])
            for n, b in enumerate(blocks)
        ]
        self.go = []
        for ref, order in kept:
            for at, n in enumerate(order):
                source, target = buffer.at[pl.ds(n * rows, rows), :], ref.at[pl.ds(at * rows, rows), :]
                sem = sems.at[len(blocks) + len(self.go)]
                self.go.append(pltpu.make_async_copy(source, target, sem))
        for copy in self.come:
            copy.start()

    def ready(self):
        for copy in self.come:
            copy.wait()
        for copy in self.go:
            copy.start()

    def end(self):
        for copy in self.go:
            copy.wait()


ALL = (0, 1, 2, 3)


COLUMNS = 512


def attend_fwd_kernel(
    x0, x1, x2, x3, w_in, wo, cos_ref, sin_ref, pq_ref, pk_ref,
    p0, p1, p2, p3, x_kept, q_out, k_out, v_out, att_out, x_all, sems,
):
    rows = x0.shape[0]
    held = Rows((x0, x1, x2, x3), x_all, sems, (x_kept, ALL))
    whole = 4 * rows
    lane = lax.broadcasted_iota(jnp.int32, (whole, 128), 1)
    low = (lane & (HD - 1)) < HD // 2
    first_lanes = lane < HD
    cos, sin = cos_ref[...], sin_ref[...]
    mask = pk_ref[...] <= pq_ref[...]
    held.ready()
    x = x_all[...]
    width, narrow = q_out.shape[1], k_out.shape[1]
    k = turn(nn(x, w_in[:, width : width + narrow]), cos, sin, low).astype(BF)
    v = nn(x, w_in[:, width + narrow :]).astype(BF)
    k_out[...] = k
    v_out[...] = v
    keys, values = spread(k, first_lanes), spread(v, first_lanes)
    for p in range(q_out.shape[1] // 128):
        cut = slice(p * 128, (p + 1) * 128)
        q = turn(nn(x, w_in[:, cut]), cos, sin, low).astype(BF)
        q_out[:, cut] = q
        head = p // 2
        att_out[:, cut] = (
            nn(soft(q, keys[head][0], mask).astype(BF), values[head][0])
            + nn(soft(q, keys[head][1], mask).astype(BF), values[head][1])
        ).astype(BF)
    att = att_out[...]
    for c in range(p0.shape[1] // COLUMNS):
        cut = slice(c * COLUMNS, (c + 1) * COLUMNS)
        out = nn(att, wo[:, cut]).astype(BF)
        for n, part in enumerate((p0, p1, p2, p3)):
            part[:, cut] = out[n * rows : (n + 1) * rows, :]
    held.end()


def attend_fwd(blocks, weights, tables):
    rows, depth = blocks[0].shape
    whole, width = 4 * rows, weights[1].shape[0]
    narrow = (weights[0].shape[1] - width) // 2
    block = shaped((rows, depth), BF)
    return pl.pallas_call(
        attend_fwd_kernel,
        out_shape=(block,) * 4
        + (
            far((whole, depth)),
            shaped((whole, width), BF),
            shaped((whole, narrow), BF),
            shaped((whole, narrow), BF),
            shaped((whole, width), BF),
        ),
        in_specs=[HBM] * 4 + [VMEM] * 6,
        out_specs=(VMEM,) * 4 + (HBM,) + (VMEM,) * 4,
        scratch_shapes=[pltpu.VMEM((whole, depth), BF), pltpu.SemaphoreType.DMA((8,))],
        compiler_params=pltpu.CompilerParams(vmem_limit_bytes=12 * MIB),
        cost_estimate=cost(5e9, 12e6),
        name="attend_fwd",
    )(*in_hbm(*blocks), *weights, *tables)


def attend_bwd_kernel(
    d0, d1, d2, d3, q_ref, k_ref, v_ref, w_in, wo, cos_ref, sin_ref, pq_ref, pk_ref,
    p0, p1, p2, p3, dm_kept, d_out, dm_all, sems,
):
    rows = d0.shape[0]
    held = Rows((d0, d1, d2, d3), dm_all, sems, (dm_kept, ALL))
    width, narrow = q_ref.shape[1], k_ref.shape[1]
    whole = 4 * rows
    lane = lax.broadcasted_iota(jnp.int32, (whole, 128), 1)
    low = (lane & (HD - 1)) < HD // 2
    first_lanes = lane < HD
    cos, sin = cos_ref[...], -sin_ref[...]
    mask = pk_ref[...] <= pq_ref[...]
    keys, values = spread(k_ref[...], first_lanes), spread(v_ref[...], first_lanes)
    held.ready()
    dm = dm_all[...]
    dk_sums, dv_sums = [[None, None], [None, None]], [[None, None], [None, None]]

    def add(sums, head, side, term):
        sums[head][side] = term if sums[head][side] is None else sums[head][side] + term

    for p in range(q_ref.shape[1] // 128):
        cut = slice(p * 128, (p + 1) * 128)
        head = p // 2
        q = q_ref[:, cut]
        d_att = nt(dm, wo[cut, :]).astype(BF)
        d_q = None
        for side in range(2):
            probs = soft(q, keys[head][side], mask)
            d_probs = nt(d_att, values[head][side])
            inner = jnp.sum(d_probs * probs, axis=-1, keepdims=True)
            d_raw = (probs * (d_probs - inner) * HD**-0.5).astype(BF)
            term = nn(d_raw, keys[head][side])
            d_q = term if d_q is None else d_q + term
            add(dk_sums, head, side, tn(d_raw, q))
            add(dv_sums, head, side, tn(probs.astype(BF), d_att))
        d_out[:, cut] = turn(d_q, cos, sin, low).astype(BF)

    def folded(sums):
        return jnp.where(
            first_lanes,
            sums[0][0] + pltpu.roll(sums[0][1], 64, 1),
            pltpu.roll(sums[1][0], 64, 1) + sums[1][1],
        )

    dk = turn(folded(dk_sums), cos, sin, low).astype(BF)
    dv = folded(dv_sums).astype(BF)
    d_out[:, width : width + narrow] = dk
    d_out[:, width + narrow :] = dv
    for c in range(p0.shape[1] // COLUMNS):
        cut = slice(c * COLUMNS, (c + 1) * COLUMNS)
        out = nt(d_out[...], w_in[cut, :]).astype(BF)
        for n, part in enumerate((p0, p1, p2, p3)):
            part[:, cut] = out[n * rows : (n + 1) * rows, :]
    held.end()


def attend_bwd(blocks, qkv, weights, tables):
    rows, depth = blocks[0].shape
    whole, width = 4 * rows, weights[1].shape[0]
    narrow = (weights[0].shape[1] - width) // 2
    block = shaped((rows, depth), BF)
    return pl.pallas_call(
        attend_bwd_kernel,
        out_shape=(block,) * 4
        + (far((whole, depth)), shaped((whole, width + 2 * narrow), BF)),
        in_specs=[HBM] * 4 + [VMEM] * 9,
        out_specs=(VMEM,) * 4 + (HBM, VMEM),
        scratch_shapes=[pltpu.VMEM((whole, depth), BF), pltpu.SemaphoreType.DMA((8,))],
        compiler_params=pltpu.CompilerParams(vmem_limit_bytes=14 * MIB),
        cost_estimate=cost(7e9, 14e6),
        name="attend_bwd",
    )(*in_hbm(*blocks), *qkv, *weights, *tables)


TILE = 512


def mlp_fwd_kernel(
    x0, x1, x2, x3, wg, wu, wd, p0, p1, p2, p3, gate_out, up_out, x_kept, x_all, total, sems
):
    rows = x0.shape[0]
    held = Rows((x0, x1, x2, x3), x_all, sems, (x_kept, (0, 2)))
    held.ready()

    def step(f, first):
        cut = slice(0, TILE) if first else pl.ds(pl.multiple_of(f * TILE, TILE), TILE)
        x = x_all[...]
        gate, up = nn(x, wg[:, cut]), nn(x, wu[:, cut])
        gate_out[:, cut] = gate.astype(BF)
        up_out[:, cut] = up.astype(BF)
        term = nn((gate * jax.nn.sigmoid(gate) * up).astype(BF), wd[cut, :])
        total[...] = term if first else total[...] + term

    step(0, True)
    pl.loop(1, wg.shape[1] // TILE)(lambda f: step(f, False))
    for n, part in enumerate((p0, p1, p2, p3)):
        part[...] = total[n * rows : (n + 1) * rows, :].astype(BF)
    held.end()


def mlp_fwd(blocks, weights):
    rows, depth = blocks[0].shape
    units, whole = weights[0].shape[1], 4 * rows
    return pl.pallas_call(
        mlp_fwd_kernel,
        in_specs=[HBM] * 4 + [VMEM] * 3,
        out_specs=[VMEM] * 6 + [HBM],
        scratch_shapes=[
            pltpu.VMEM((whole, depth), BF),
            pltpu.VMEM((whole, depth), F32),
            pltpu.SemaphoreType.DMA((8,)),
        ],
        out_shape=[shaped((rows, depth), BF)] * 4
        + [shaped((whole, units), BF)] * 2
        + [far((whole // 2, depth))],
        compiler_params=pltpu.CompilerParams(vmem_limit_bytes=12 * MIB),
        cost_estimate=cost(6 * whole * units * depth, 30e6),
        name="mlp_fwd",
    )(*in_hbm(*blocks), *weights)


def mlp_bwd_kernel(
    g0, g1, g2, g3, gate_ref, up_ref, wg, wu, wd, p0, p1, p2, p3, g_kept, g_all, total, sems
):
    rows = g0.shape[0]
    held = Rows((g0, g1, g2, g3), g_all, sems, (g_kept, ALL))
    held.ready()

    def step(f, first):
        cut = slice(0, TILE) if first else pl.ds(pl.multiple_of(f * TILE, TILE), TILE)
        d_hidden = nt(g_all[...], wd[cut, :])
        gate, up = gate_ref[:, cut].astype(F32), up_ref[:, cut].astype(F32)
        s = jax.nn.sigmoid(gate)
        d_up = (d_hidden * gate * s).astype(BF)
        d_gate = (d_hidden * up * s * (1.0 + gate * (1.0 - s))).astype(BF)
        term = nt(d_gate, wg[:, cut]) + nt(d_up, wu[:, cut])
        total[...] = term if first else total[...] + term

    step(0, True)
    pl.loop(1, wg.shape[1] // TILE)(lambda f: step(f, False))
    for n, part in enumerate((p0, p1, p2, p3)):
        part[...] = total[n * rows : (n + 1) * rows, :].astype(BF)
    held.end()


def mlp_bwd(blocks, gate, up, weights):
    rows, depth = blocks[0].shape
    units, whole = weights[0].shape[1], 4 * rows
    return pl.pallas_call(
        mlp_bwd_kernel,
        in_specs=[HBM] * 4 + [VMEM] * 5,
        out_specs=[VMEM] * 4 + [HBM],
        scratch_shapes=[
            pltpu.VMEM((whole, depth), BF),
            pltpu.VMEM((whole, depth), F32),
            pltpu.SemaphoreType.DMA((8,)),
        ],
        out_shape=[shaped((rows, depth), BF)] * 4 + [far((whole, depth))],
        compiler_params=pltpu.CompilerParams(vmem_limit_bytes=12 * MIB),
        cost_estimate=cost(6 * whole * units * depth, 30e6),
        name="mlp_bwd",
    )(*in_hbm(*blocks), gate, up, *weights)


def mlp_both_kernel(
    x0, x1, x2, x3, g0, g1, g2, g3, wg, wu, wd,
    p0, p1, p2, p3, r0, r1, r2, r3, x_kept, x_all, g_all, gate_all, up_all, total, x_sems, g_sems,
):
    rows = x0.shape[0]
    held = Rows((x0, x1, x2, x3), x_all, x_sems, (x_kept, ALL))
    held_g = Rows((g0, g1, g2, g3), g_all, g_sems)
    held.ready()

    def tile(f, first):
        return slice(0, TILE) if first else pl.ds(pl.multiple_of(f * TILE, TILE), TILE)

    def forward(f, first):
        cut = tile(f, first)
        x = x_all[...]
        gate, up = nn(x, wg[:, cut]), nn(x, wu[:, cut])
        gate_all[:, cut] = gate.astype(BF)
        up_all[:, cut] = up.astype(BF)
        term = nn((gate * jax.nn.sigmoid(gate) * up).astype(BF), wd[cut, :])
        total[...] = term if first else total[...] + term

    def backward(f, first):
        cut = tile(f, first)
        d_hidden = nt(g_all[...], wd[cut, :])
        gate, up = gate_all[:, cut].astype(F32), up_all[:, cut].astype(F32)
        s = jax.nn.sigmoid(gate)
        d_up = (d_hidden * gate * s).astype(BF)
        d_gate = (d_hidden * up * s * (1.0 + gate * (1.0 - s))).astype(BF)
        term = nt(d_gate, wg[:, cut]) + nt(d_up, wu[:, cut])
        total[...] = term if first else total[...] + term

    for step, parts in ((forward, (p0, p1, p2, p3)), (backward, (r0, r1, r2, r3))):
        step(0, True)
        pl.loop(1, wg.shape[1] // TILE)(lambda f: step(f, False))
        for n, part in enumerate(parts):
            part[...] = total[n * rows : (n + 1) * rows, :].astype(BF)
        if step is forward:
            held_g.ready()
    held.end()


def mlp_both(blocks, g_blocks, weights):
    rows, depth = blocks[0].shape
    units, whole = weights[0].shape[1], 4 * rows
    return pl.pallas_call(
        mlp_both_kernel,
        in_specs=[HBM] * 8 + [VMEM] * 3,
        out_specs=[VMEM] * 8 + [HBM],
        scratch_shapes=[
            pltpu.VMEM((whole, depth), BF),
            pltpu.VMEM((whole, depth), BF),
            pltpu.VMEM((whole, units), BF),
            pltpu.VMEM((whole, units), BF),
            pltpu.VMEM((whole, depth), F32),
            pltpu.SemaphoreType.DMA((8,)),
            pltpu.SemaphoreType.DMA((4,)),
        ],
        out_shape=[shaped((rows, depth), BF)] * 8 + [far((whole, depth))],
        compiler_params=pltpu.CompilerParams(vmem_limit_bytes=14 * MIB),
        cost_estimate=cost(12 * whole * units * depth, 30e6),
        name="mlp_both",
    )(*in_hbm(*blocks, *g_blocks), *weights)


PIECE = 512


def mlp_grads_kernel(layer, f, first, last, x_orders, g_orders, *refs):
    n_x, n_g = len(x_orders), len(g_orders)
    x_refs, g_refs, refs = refs[:n_x], refs[n_x : n_x + n_g], refs[n_x + n_g :]
    *weights, out = refs[:7]
    wg, wu, wd, x_all, g_all, total, w_sems, sems = refs[7:]
    share = out.shape[0]
    units = weights[0].shape[1]
    mine = lax.axis_index("section") == layer
    column = lax.axis_index("section") * (units // 2) + f * PIECE
    cut = pl.ds(pl.multiple_of(column, PIECE), PIECE)
    start = pl.ds(pl.multiple_of(lax.axis_index("dp") * share, share), share)

    def chunk(p, slot):
        moves = []
        for to, arrays, orders in ((x_all, x_refs, x_orders), (g_all, g_refs, g_orders)):
            for a, (half, order) in zip(arrays, orders):
                rows = a.shape[1] // len(order)
                at = p if a.shape[0] > last - first else p - first
                for n, place in enumerate(order):
                    target = to.at[slot, pl.ds((half * 4 + place) * rows, rows), :]
                    source = a.at[at, pl.ds(n * rows, rows), :]
                    moves.append(pltpu.make_async_copy(source, target, sems.at[slot, len(moves)]))
        return moves

    def copies(g, u, d):
        return [
            pltpu.make_async_copy(g.at[:, cut], wg, w_sems.at[0]),
            pltpu.make_async_copy(u.at[:, cut], wu, w_sems.at[1]),
            pltpu.make_async_copy(d.at[cut, :], wd, w_sems.at[2]),
        ]

    @pl.when(mine)
    def _():
        for copy in copies(*weights[0::2]):
            copy.start()

    @pl.when(jnp.logical_not(mine))
    def _():
        for copy in copies(*weights[1::2]):
            copy.start()

    for copy in chunk(first, 0):
        copy.start()
    total[...] = jnp.zeros_like(total)
    for copy in copies(*weights[0::2]):
        copy.wait()

    @pl.loop(first, last)
    def _(p):
        slot = lax.rem(p - first, 2)

        @pl.when(p + 1 < last)
        def _():
            for copy in chunk(p + 1, 1 - slot):
                copy.start()

        for copy in chunk(p, slot):
            copy.wait()
        x = x_all[slot]
        gate, up = nn(x, wg[...]), nn(x, wu[...])
        d_hidden = nt(g_all[slot], wd[...])
        s = jax.nn.sigmoid(gate)
        gated = gate * s
        hidden = (gated * up).astype(BF)
        d_up = (d_hidden * gated).astype(BF)
        d_gate = (d_hidden * up * s * (1.0 + gate * (1.0 - s))).astype(BF)
        x_cut, g_cut = x_all[slot, :, start], g_all[slot, :, start]
        total[:, :PIECE] += tn(x_cut, d_gate)
        total[:, PIECE : 2 * PIECE] += tn(x_cut, d_up)
        total[:, 2 * PIECE :] += tn(g_cut, hidden)

    out[...] = total[...].astype(BF)


def mlp_grads(layer, f, part, xs, gs, pairs):
    groups, _, depth = xs[0][0].shape
    first, last = part * (groups // 2), (part + 1) * (groups // 2)
    rows = sum(a.shape[1] for a, _ in xs)
    share = depth // groups
    return pl.pallas_call(
        functools.partial(
            mlp_grads_kernel, layer, f, first, last, [o for _, o in xs], [o for _, o in gs]
        ),
        in_specs=[HBM] * (len(xs) + len(gs) + 6),
        out_specs=VMEM,
        out_shape=shaped((share, 3 * PIECE), BF),
        scratch_shapes=[
            pltpu.VMEM((depth, PIECE), BF),
            pltpu.VMEM((depth, PIECE), BF),
            pltpu.VMEM((PIECE, depth), BF),
            pltpu.VMEM((2, rows, depth), BF),
            pltpu.VMEM((2, rows, depth), BF),
            pltpu.VMEM((share, 3 * PIECE), F32),
            pltpu.SemaphoreType.DMA((3,)),
            pltpu.SemaphoreType.DMA((2, 16)),
        ],
        compiler_params=pltpu.CompilerParams(vmem_limit_bytes=50 * MIB),
        cost_estimate=cost(3 * rows * groups * PIECE * (depth + share), 20e6),
        name="mlp_grads",
    )(*in_hbm(*[a for a, _ in xs], *[a for a, _ in gs], *[w for pair in pairs for w in pair]))


def assemble_kernel(n, *refs):
    sources, outs, scratch = refs[: 4 * (n + 1)], refs[4 * (n + 1) : 4 * (n + 1) + 7], refs[4 * (n + 1) + 7 :]
    q_out, k_out, v_out, o_out, gate_out, up_out, down_out = outs
    held, attn, in_rows, wide, tall, flat, sems, out_sems = scratch
    sec = lax.axis_index("section")

    def fetches(layer):
        mine = sources[layer * 2 * (n + 1) : (layer + 1) * 2 * (n + 1)]
        moves = []
        for side in range(2):
            for f in range(n + 1):
                source = mine[side * (n + 1) + f]
                target = held.at[side, f] if f < n else attn.at[side]
                moves.append(pltpu.make_async_copy(source, target, sems.at[len(moves)]))
        return moves

    for layer in range(2):

        @pl.when(sec == layer)
        def _(layer=layer):
            for move in fetches(layer):
                move.start()

    for move in fetches(0):
        move.wait()
    share, width = attn.shape[1:]
    columns = in_rows.shape[1] // 2
    half_units = wide.shape[2] // 2
    going = []

    def leave(source, target):
        going.append(pltpu.make_async_copy(source, target, out_sems.at[len(going)]))
        going[-1].start()

    q, k = q_out.shape[1], k_out.shape[1]
    halves = [sec, 1 - sec]
    rest = width - columns
    for side, half in enumerate(halves):
        in_rows[:, pl.ds(pl.multiple_of(half * columns, columns), columns)] = attn[side, :, :columns].astype(F32)
        flat[pl.ds(pl.multiple_of(half * rest, rest), rest), :] = attn[side, :, columns:].astype(F32).T
    leave(flat, o_out)
    leave(in_rows.at[:, pl.ds(0, q)], q_out)
    leave(in_rows.at[:, pl.ds(q, k)], k_out)
    leave(in_rows.at[:, pl.ds(q + k, k)], v_out)
    for kind, (target, out) in enumerate(((wide.at[0], gate_out), (wide.at[1], up_out), (tall, down_out))):
        for side, half in enumerate(halves):
            for f in range(n // 2):
                at = pl.ds(pl.multiple_of(half * half_units + f * PIECE, PIECE), PIECE)
                cut = slice(kind * PIECE, (kind + 1) * PIECE)
                tile = held[side, 2 * f, :, cut].astype(F32) + held[side, 2 * f + 1, :, cut].astype(F32)
                if kind < 2:
                    target[:, at] = tile
                else:
                    target[at, :] = tile.T
        leave(target, out)
    for move in going:
        move.wait()


def assemble(layers, width, narrow, units):
    n = len(layers[0][0])
    share, attn_width = layers[0][1].shape
    depth_out = 2 * attn_width - width - 2 * narrow
    sources = []
    for tiles, part, other_tiles, other_part in layers:
        sources += [*tiles, part, *other_tiles, other_part]
    shapes = [(share, width), (share, narrow), (share, narrow), (depth_out, share)]
    shapes += [(share, units), (share, units), (units, share)]
    return pl.pallas_call(
        functools.partial(assemble_kernel, n),
        in_specs=[HBM] * len(sources),
        out_specs=[HBM] * 7,
        out_shape=[far(shape, F32) for shape in shapes],
        scratch_shapes=[
            pltpu.VMEM((2, n, share, 3 * PIECE), BF),
            pltpu.VMEM((2, share, attn_width), BF),
            pltpu.VMEM((share, width + 2 * narrow), F32),
            pltpu.VMEM((2, share, units), F32),
            pltpu.VMEM((units, share), F32),
            pltpu.VMEM((depth_out, share), F32),
            pltpu.SemaphoreType.DMA((2 * (n + 1),)),
            pltpu.SemaphoreType.DMA((7,)),
        ],
        compiler_params=pltpu.CompilerParams(vmem_limit_bytes=48 * MIB),
        cost_estimate=cost(0, 30e6),
        name="assemble",
    )(*in_hbm(*sources))


def attend_grads_kernel(x_own, x_other, d_own, d_other, m_own, m_other, a_own, a_other, out):
    sec = lax.axis_index("section")
    at = 0
    for left_own, left_other, own, other in (
        (x_own, x_other, d_own, d_other),
        (m_own, m_other, a_own, a_other),
    ):
        width = own.shape[1] // 2
        half = pl.ds(pl.multiple_of(sec * width, width), width)
        out[:, at : at + width] = (tn(left_own[...], own[:, half]) + tn(left_other[...], other[:, half])).astype(BF)
        at += width


def attend_grads(x, d_qkv, d_mid, att):
    depth, width = x.shape[1], (d_qkv.shape[1] + att.shape[1]) // 2
    terms = [x, swapped(x), d_qkv, swapped(d_qkv), d_mid, swapped(d_mid), att, swapped(att)]
    both = pl.pallas_call(
        attend_grads_kernel,
        in_specs=[VMEM] * 8,
        out_specs=VMEM,
        out_shape=shaped((depth, width), BF),
        compiler_params=pltpu.CompilerParams(vmem_limit_bytes=14 * MIB),
        cost_estimate=cost(4 * x.size * width, 6e6),
        name="attend_grads",
    )(*terms)
    return both


def summed_over_groups(x):
    return lax.psum_scatter(x, "dp", scatter_dimension=0, tiled=True)


def rope_tables(places, head_size):
    half_width = head_size // 2
    counter = jnp.arange(half_width, dtype=F32)
    base_freq = 1.0 / 500000.0 ** (2.0 * counter / head_size)
    wavelength = 2.0 * jnp.pi / base_freq
    blend_part = (8192.0 / wavelength - 1.0) / 3.0
    middle = (1.0 - blend_part) * base_freq / 32.0 + blend_part * base_freq
    frequency = jnp.where(
        wavelength < 2048.0, base_freq, jnp.where(wavelength > 8192.0, base_freq / 32.0, middle)
    )
    angles = places.astype(F32)[:, None] * frequency[None, :]
    cosine, sine = jnp.cos(angles), jnp.sin(angles)
    return (
        jnp.concatenate([cosine] * 4, axis=1),
        jnp.concatenate([-sine, sine, -sine, sine], axis=1),
    )


def halved(total, axis, size, bit, dim):
    low, high = lax.slice_in_dim(total, 0, bit, axis=dim), lax.slice_in_dim(total, bit, 2 * bit, axis=dim)
    upper = (lax.axis_index(axis) & bit) != 0
    keep, send = jnp.where(upper, high, low), jnp.where(upper, low, high)
    return keep + lax.ppermute(send, axis, [(a, a ^ bit) for a in range(size)])


def over_groups(x):
    return lax.all_gather(x, "dp", axis=0, tiled=False)


def from_both_cores(*arrays):
    return [(a, (0, places)) for a, places in arrays] + [(swapped(a), (1, places)) for a, places in arrays]


def local(groups, size, tokens, lengths, cotangent, attn_gain, mlp_gain, *weights):
    sec, t = lax.axis_index("section"), lax.axis_index("tensor")
    first = sec == 0
    rows, depth = tokens.shape[1:]
    mine = [w[0] for w in weights]
    gains = jnp.concatenate([attn_gain, mlp_gain], axis=0)
    other_gains = swapped(gains)
    layer_gains = [jnp.where(sec == l, gains, other_gains) for l in range(2)]
    attn_gains = [g[0:1] for g in layer_gains]
    mlp_gains = [g[1:2] for g in layer_gains]
    length = lax.dynamic_index_in_dim(lengths[:, 0], sec, 0, keepdims=False)
    tok = lax.dynamic_index_in_dim(tokens, sec, 0, keepdims=False)
    cot = lax.dynamic_index_in_dim(cotangent, sec, 0, keepdims=False)
    within = jnp.arange(rows, dtype=jnp.int32)
    own_places = t * rows + within
    places = jnp.concatenate([(t ^ k) * rows + within for k in range(size)])
    readable = jnp.where(places < length, places, jnp.int32(1 << 20))
    tables = rope_tables(places, HD) + (places[:, None], readable[None, :])

    g_low = jnp.where((own_places < length)[:, None], cot, jnp.zeros_like(cot))

    def for_layer(pair):
        keep, send = jnp.where(first, pair[0], pair[1]), jnp.where(first, pair[1], pair[0])
        return keep, swapped(send)

    def both(pair):
        keep, came = for_layer(pair)
        return [jnp.where(first, keep, came), jnp.where(first, came, keep)]

    attn_mine = [jnp.concatenate(mine[:3], axis=1), mine[3]]
    attn_w = [(w, swapped(tied(w, other_gains))) for w in attn_mine]
    attn_cuts = [(0, w.shape[0]) for w in attn_mine]
    g_blocks1 = gather_rows(g_low, size)
    normed = tied(norm_rows(tok, attn_gains[0]), *g_blocks1)
    *weights_in, token = prefetch(0, attn_w, attn_cuts, normed)
    blocks = gather_rows(normed, size)
    all_g1 = jnp.concatenate(g_blocks1, axis=0)
    blocks[0] = tied(blocks[0], all_g1)
    all_g1 = over_groups(all_g1)
    *parts, x_attn0, q0, k0, v0, att0 = attend_fwd(blocks, weights_in, tables)
    gate_other, up_other = [swapped(tied(w, normed, *[o for _, o in attn_w])) for w in mine[4:6]]
    down_other = swapped(tied(mine[6], gate_other, parts[0]))
    mlp_w = list(zip(mine[4:], (gate_other, up_other, down_other)))
    mlp_cuts = [(0, w.shape[0]) for w in mine[4:]]
    mid0, normed = add_norm(tok, scatter_rows(parts, size), mlp_gains[0], False)
    *weights_in, token = prefetch(0, mlp_w, mlp_cuts, normed)
    *parts, gate0, up0, x_half = mlp_fwd(gather_rows(normed, size), weights_in)
    act0, normed = add_norm(mid0, scatter_rows(parts, size), attn_gains[1], True)

    *weights_in, token = prefetch(1, attn_w, attn_cuts, normed)
    *parts, x_attn1, q1, k1, v1, att1 = attend_fwd(gather_rows(normed, size), weights_in, tables)
    parts[0] = tied(parts[0], all_g1)
    half_x0 = over_groups(tied(x_half, all_g1, parts[0]))
    mid1, normed = add_norm(act0, scatter_rows(parts, size), mlp_gains[1], False)
    *weights_in, token = prefetch(1, mlp_w, mlp_cuts, normed)
    *both_parts, x_all = mlp_both(gather_rows(normed, size), g_blocks1, weights_in)
    parts1, parts = both_parts[:size], both_parts[size:]
    parts[0] = tied(parts[0], half_x0)
    all_x1 = over_groups(tied(x_all, half_x0, parts[0]))
    d_mid, d_mid_low, mlp_part1 = norm_back(mid1, scatter_rows(parts, size), mlp_gains[1], g_low)
    rest_x0 = []

    def with_chunk(blocks, results):
        chunk = lax.ppermute(tied(half_x0[len(rest_x0)], *blocks), "tensor", partners(size)[0])
        results, chunk = lax.optimization_barrier((list(results), chunk))
        rest_x0.append(chunk)
        return results

    *weights_in, token = prefetch(1, attn_w, attn_cuts, d_mid_low)
    blocks = gather_rows(d_mid_low, size)
    *parts, dm, dqkv = with_chunk(blocks, attend_bwd(blocks, (q1, k1, v1), weights_in, tables))
    attn_terms1 = attend_grads(x_attn1, dqkv, dm, att1)
    came = scatter_rows(parts, size)
    came[0] = tied(came[0], attn_terms1)
    d_stream1, d_low, attn_part1 = norm_back(act0, came, attn_gains[1], d_mid)

    *weights_in, token = prefetch(0, mlp_w, mlp_cuts, d_low)
    *parts, g_all = with_chunk([token], mlp_bwd(gather_rows(d_low, size), gate0, up0, weights_in))
    parts[0] = tied(parts[0], all_x1)
    all_g0 = over_groups(tied(g_all, all_x1, parts[0]))
    x1, g1 = from_both_cores((all_x1, ALL)), from_both_cores((all_g1, ALL))
    pieces = [(f, part) for f in range(mine[4].shape[1] // (2 * PIECE)) for part in range(2)]
    tiles1 = []

    def piece1(*after):
        f, part = pieces[len(tiles1)]
        tiles1.append(mlp_grads(1, f, part, [(tied(a, *after), o) for a, o in x1], g1, mlp_w))
        return tiles1[-1]

    d_mid, d_mid_low, mlp_part0 = norm_back(mid0, scatter_rows(parts, size), mlp_gains[0], d_low)
    *weights_in, token = prefetch(0, attn_w, attn_cuts, d_mid_low)
    blocks = gather_rows(d_mid_low, size)
    blocks[0] = tied(blocks[0], piece1(d_mid_low, token))
    *parts, dm, dqkv = with_chunk(blocks, attend_bwd(blocks, (q0, k0, v0), weights_in, tables))
    attn_terms0 = attend_grads(x_attn0, dqkv, dm, att0)
    came = scatter_rows(parts, size)
    came[0] = tied(came[0], piece1(parts[0], attn_terms0))
    d_stream0, _, attn_part0 = norm_back(tok, came, attn_gains[0], d_mid)

    attn_share1 = summed_over_groups(tied(attn_terms1, all_g0, d_stream0))

    def beside(results, *transfers):
        results, transfers = lax.optimization_barrier((results, list(transfers)))
        return results, transfers

    def halves(axis, count, dim, bit, total):
        low, high = lax.slice_in_dim(total, 0, bit, axis=dim), lax.slice_in_dim(total, bit, 2 * bit, axis=dim)
        upper = (lax.axis_index(axis) & bit) != 0
        came = lax.ppermute(jnp.where(upper, low, high), axis, [(a, a ^ bit) for a in range(count)])
        return jnp.where(upper, high, low), came

    keep, came = for_layer(
        [jnp.concatenate(p, axis=0) for p in ((attn_part0, mlp_part0), (attn_part1, mlp_part1))]
    )
    others1, others0 = [swapped(tile) for tile in tiles1], []
    while len(rest_x0) < groups:
        rest_x0.append(lax.ppermute(tied(half_x0[len(rest_x0)], d_stream0), "tensor", partners(size)[0]))
    tiles1[2], (came, rest_x0[-1], *others1) = beside(piece1(d_stream0), came, rest_x0[-1], *others1)
    shares = (keep + came).reshape(2, groups, size, depth // (groups * size))
    steps = [("tensor", size, 2, 1 << n) for n in reversed(range(size.bit_length() - 1))]
    steps += [("dp", groups, 1, 1 << n) for n in reversed(range(groups.bit_length() - 1))]

    def step_beside(results, *transfers):
        nonlocal shares
        keep, came = halves(*steps.pop(0), shares)
        results, (came, *transfers) = beside(results, came, *transfers)
        shares = keep + came
        return results, transfers

    at = groups // 2
    x0, g0 = from_both_cores((half_x0, (0, 2))), from_both_cores((all_g0, ALL))
    x0_rest = [
        from_both_cores((jnp.stack(part), (1, 3))) for part in (rest_x0[:at], rest_x0[at:])
    ]
    tiles1[3:], (moved,) = step_beside([piece1(tiles1[2])], swapped(tiles1[2]))
    others1.append(moved)
    order0 = [(f, part) for part in range(2) for f in range(len(pieces) // 2)]

    def piece0(after):
        f, part = order0[len(tiles0)]
        tiles0.append(mlp_grads(0, f, part, [(tied(a, after), o) for a, o in x0 + x0_rest[part]], g0, mlp_w))
        return tiles0[-1]

    tiles0 = []
    tiles0[0:], (moved,) = step_beside([piece0(tiles1[3])], swapped(tiles1[3]))
    others1.append(moved)
    attn_share0 = summed_over_groups(tied(attn_terms0, attn_share1, tiles0[0]))
    tiles0[1:], (moved,) = step_beside([piece0(tiles0[0])], swapped(tiles0[0]))
    others0.append(moved)
    act_terms = scatter_rows([tied(p, tiles0[0]) for p in parts1], size)
    tiles0[2:], (moved, *act_terms[1:]) = step_beside(
        [piece0(tiles0[1])], swapped(tiles0[1]), *act_terms[1:]
    )
    others0.append(moved)
    while steps:
        step_beside([])
    act1, _ = add_norm(mid1, act_terms, attn_gains[1], True)
    shares = shares.reshape(2, -1)
    tiles0[3:], (moved, swapped_share1) = beside(
        [piece0(tied(tiles0[2], act1, shares))], swapped(tiles0[2]), swapped(attn_share1)
    )
    others0.append(moved)
    attn_share0 = tied(attn_share0, tiles0[3])
    others0.append(swapped(tiles0[3]))
    others0 = [others0[order0.index(piece)] for piece in pieces]
    tiles0 = [tiles0[order0.index(piece)] for piece in pieces]
    layers = [
        (tiles0, attn_share0, others0, swapped(attn_share0)),
        (tiles1, attn_share1, others1, swapped_share1),
    ]
    weight_grads = assemble(layers, mine[0].shape[1], mine[1].shape[1], mine[4].shape[1])
    acts, input_grads = (act0, act1), (d_stream0, d_stream1)

    return (
        jnp.stack(both(acts))[None],
        jnp.stack(both(input_grads))[None],
        shares[0:1],
        shares[1:2],
        *[grad[None] for grad in weight_grads],
    )


def solution(mesh):
    rows = P(None, ("dp", "tensor"), None)
    in_specs = (
        rows,
        P(None, "dp"),
        rows,
        P("section", None),
        P("section", None),
        P("section", None, "tensor"),
        P("section", None, "tensor"),
        P("section", None, "tensor"),
        P("section", "tensor", None),
        P("section", None, "tensor"),
        P("section", None, "tensor"),
        P("section", "tensor", None),
    )
    out_rows = P("section", None, ("dp", "tensor"), None)
    shares = P("section", ("dp", "tensor"))
    by_dp, by_tensor = P("section", "dp", "tensor"), P("section", "tensor", "dp")
    out_specs = (
        out_rows, out_rows, shares, shares, by_dp, by_dp, by_dp, by_tensor, by_dp, by_dp, by_tensor,
    )
    step = functools.partial(local, mesh.shape["dp"], mesh.shape["tensor"])
    return jax.shard_map(step, mesh=mesh, in_specs=in_specs, out_specs=out_specs, check_vma=False)
```

```python
import functools

import jax
import jax.numpy as jnp
from jax import lax
from jax.experimental import pallas as pl
from jax.experimental.pallas import tpu as pltpu
from jax.sharding import PartitionSpec as P

HD = 64
EPSILON = 1e-05
NEGATIVE = -1e30
BF = jnp.bfloat16
F32 = jnp.float32
VMEM = pl.BlockSpec(memory_space=pltpu.VMEM)
HBM = pl.BlockSpec(memory_space=pltpu.HBM)
ANY = pl.BlockSpec(memory_space=pl.ANY)
MIB = 1024 * 1024
SHRINK = 50


def nn(a, b):
    return jnp.dot(a, b, preferred_element_type=F32)


def nt(a, b):
    return lax.dot_general(a, b, (((1,), (1,)), ((), ())), preferred_element_type=F32)


def tn(a, b):
    return lax.dot_general(a, b, (((0,), (0,)), ((), ())), preferred_element_type=F32)


def shaped(shape, dtype):
    return jax.ShapeDtypeStruct(shape, dtype)


def far(shape, dtype=BF):
    return pltpu.HBM(shape, dtype)


def in_hbm(*arrays):
    return [pltpu.with_memory_space_constraint(a, pltpu.HBM) for a in arrays]


def tied(first, *others):
    return lax.optimization_barrier((first, *others))[0]


def cost(flops, nbytes):
    return pl.CostEstimate(flops=int(flops / SHRINK), bytes_accessed=int(nbytes / SHRINK), transcendentals=0)


def partners(size):
    return [[(a, a ^ k) for a in range(size)] for k in range(1, size)]


def gather_rows(x, size):
    return [x] + [lax.ppermute(x, "tensor", pairs) for pairs in partners(size)]


def scatter_rows(parts, size):
    return [parts[0]] + [
        lax.ppermute(part, "tensor", pairs) for part, pairs in zip(parts[1:], partners(size))
    ]


def swapped(x):
    return lax.ppermute(x, "section", [(0, 1), (1, 0)])


def norm_kernel(x_ref, gain_ref, out_ref):
    x = x_ref[...].astype(F32)
    scale = lax.rsqrt(jnp.mean(x * x, axis=-1, keepdims=True) + EPSILON)
    out_ref[...] = (x * scale * gain_ref[...]).astype(BF)


def norm_rows(x, gain):
    return pl.pallas_call(
        norm_kernel, name="norm", cost_estimate=cost(0, 1e6), out_shape=shaped(x.shape, BF), in_specs=[VMEM] * 2, out_specs=VMEM
    )(x, gain)


def add_norm_kernel(round_out, base_ref, a_ref, b_ref, c_ref, d_ref, gain_ref, out_ref, normed_ref):
    x = base_ref[...].astype(F32) + (
        (a_ref[...].astype(F32) + b_ref[...].astype(F32))
        + (c_ref[...].astype(F32) + d_ref[...].astype(F32))
    )
    if round_out:
        x = x.astype(BF)
        out_ref[...] = x
        x = x.astype(F32)
    else:
        out_ref[...] = x
    scale = lax.rsqrt(jnp.mean(x * x, axis=-1, keepdims=True) + EPSILON)
    normed_ref[...] = (x * scale * gain_ref[...]).astype(BF)


def add_norm(base, terms, gain, round_out):
    return pl.pallas_call(
        functools.partial(add_norm_kernel, round_out),
        name="add_norm",
        cost_estimate=cost(0, 2e6),
        out_shape=(shaped(base.shape, BF if round_out else F32), shaped(base.shape, BF)),
        in_specs=[VMEM] * 6,
        out_specs=(VMEM, VMEM),
    )(base, *terms, gain)


def norm_back_kernel(base_ref, a_ref, b_ref, c_ref, d_ref, gain_ref, res_ref, out_ref, low_ref, gp_ref):
    g = (a_ref[...].astype(F32) + b_ref[...].astype(F32)) + (
        c_ref[...].astype(F32) + d_ref[...].astype(F32)
    )
    x = base_ref[...].astype(F32)
    scale = lax.rsqrt(jnp.mean(x * x, axis=-1, keepdims=True) + EPSILON)
    y = x * scale
    gp_ref[...] = jnp.sum(g * y, axis=0, keepdims=True)
    e = g * gain_ref[...]
    out = res_ref[...].astype(F32) + scale * (e - y * jnp.mean(e * y, axis=-1, keepdims=True))
    out_ref[...] = out
    low_ref[...] = out.astype(BF)


def norm_back(base, terms, gain, residual):
    return pl.pallas_call(
        norm_back_kernel,
        name="norm_back",
        cost_estimate=cost(0, 3e6),
        out_shape=(shaped(base.shape, F32), shaped(base.shape, BF), shaped((1, base.shape[1]), F32)),
        in_specs=[VMEM] * 7,
        out_specs=(VMEM,) * 3,
    )(base, *terms, gain, residual)


def prefetch_kernel(layer, cuts, after_ref, *refs):
    sources, refs = refs[: 2 * len(cuts)], refs[2 * len(cuts) :]
    total = sum(len(cut) - 1 for cut in cuts)
    buffers, token, sems = refs[:total], refs[total], refs[-1]
    token[...] = jnp.zeros_like(token)
    mine = lax.axis_index("section") == layer

    def copies(side):
        moves = []
        for source, cut in zip(sources[side::2], cuts):
            for at, to in zip(cut, cut[1:]):
                n = len(moves)
                part = source.at[pl.ds(at, to - at), :]
                moves.append(pltpu.make_async_copy(part, buffers[n], sems.at[n]))
        return moves

    @pl.when(mine)
    def _():
        for copy in copies(0):
            copy.start()

    @pl.when(jnp.logical_not(mine))
    def _():
        for copy in copies(1):
            copy.start()

    for copy in copies(0):
        copy.wait()


def prefetch(layer, pairs, cuts, after):
    shapes = [
        (to - at, own.shape[1]) for (own, _), cut in zip(pairs, cuts) for at, to in zip(cut, cut[1:])
    ]
    return pl.pallas_call(
        functools.partial(prefetch_kernel, layer, cuts),
        out_shape=[pltpu.VMEM(shape, BF) for shape in shapes] + [shaped((8, 128), F32)],
        in_specs=[ANY] + [HBM] * (2 * len(pairs)),
        out_specs=[VMEM] * (len(shapes) + 1),
        scratch_shapes=[pltpu.SemaphoreType.DMA((len(shapes),))],
        compiler_params=pltpu.CompilerParams(vmem_limit_bytes=MIB),
        cost_estimate=cost(0, sum(4 * a * b for a, b in shapes)),
        name="prefetch",
    )(after, *in_hbm(*[w for pair in pairs for w in pair]))


def turn(x, cos, sin, low):
    return x * cos + jnp.where(low, pltpu.roll(x, 96, 1), pltpu.roll(x, 32, 1)) * sin


def spread(x, first_lanes):
    x = x.astype(F32)
    moved = pltpu.roll(x, 64, 1)
    zero = jnp.zeros_like(x)
    return [
        (jnp.where(first_lanes, x, zero).astype(BF), jnp.where(first_lanes, zero, moved).astype(BF)),
        (jnp.where(first_lanes, moved, zero).astype(BF), jnp.where(first_lanes, zero, x).astype(BF)),
    ]


def soft(q, k, mask):
    scores = jnp.where(mask, nt(q, k) * HD**-0.5, NEGATIVE)
    lifted = jnp.exp(scores - jnp.max(scores, axis=-1, keepdims=True))
    return lifted * (1.0 / jnp.sum(lifted, axis=-1, keepdims=True))


class Rows:
    def __init__(self, blocks, buffer, sems, *kept):
        rows = blocks[0].shape[0]
        self.come = [
            pltpu.make_async_copy(b, buffer.at[pl.ds(n * rows, rows), :], sems.at[n])
            for n, b in enumerate(blocks)
        ]
        self.go = []
        for ref, order in kept:
            for at, n in enumerate(order):
                source, target = buffer.at[pl.ds(n * rows, rows), :], ref.at[pl.ds(at * rows, rows), :]
                sem = sems.at[len(blocks) + len(self.go)]
                self.go.append(pltpu.make_async_copy(source, target, sem))
        for copy in self.come:
            copy.start()

    def ready(self):
        for copy in self.come:
            copy.wait()
        for copy in self.go:
            copy.start()

    def end(self):
        for copy in self.go:
            copy.wait()


ALL = (0, 1, 2, 3)


COLUMNS = 512


def attend_fwd_kernel(
    x0, x1, x2, x3, w_in, wo, cos_ref, sin_ref, pq_ref, pk_ref,
    p0, p1, p2, p3, x_kept, q_out, k_out, v_out, att_out, x_all, sems,
):
    rows = x0.shape[0]
    held = Rows((x0, x1, x2, x3), x_all, sems, (x_kept, ALL))
    whole = 4 * rows
    lane = lax.broadcasted_iota(jnp.int32, (whole, 128), 1)
    low = (lane & (HD - 1)) < HD // 2
    first_lanes = lane < HD
    cos, sin = cos_ref[...], sin_ref[...]
    mask = pk_ref[...] <= pq_ref[...]
    held.ready()
    x = x_all[...]
    width, narrow = q_out.shape[1], k_out.shape[1]
    k = turn(nn(x, w_in[:, width : width + narrow]), cos, sin, low).astype(BF)
    v = nn(x, w_in[:, width + narrow :]).astype(BF)
    k_out[...] = k
    v_out[...] = v
    keys, values = spread(k, first_lanes), spread(v, first_lanes)
    for p in range(q_out.shape[1] // 128):
        cut = slice(p * 128, (p + 1) * 128)
        q = turn(nn(x, w_in[:, cut]), cos, sin, low).astype(BF)
        q_out[:, cut] = q
        head = p // 2
        att_out[:, cut] = (
            nn(soft(q, keys[head][0], mask).astype(BF), values[head][0])
            + nn(soft(q, keys[head][1], mask).astype(BF), values[head][1])
        ).astype(BF)
    att = att_out[...]
    for c in range(p0.shape[1] // COLUMNS):
        cut = slice(c * COLUMNS, (c + 1) * COLUMNS)
        out = nn(att, wo[:, cut]).astype(BF)
        for n, part in enumerate((p0, p1, p2, p3)):
            part[:, cut] = out[n * rows : (n + 1) * rows, :]
    held.end()


def attend_fwd(blocks, weights, tables):
    rows, depth = blocks[0].shape
    whole, width = 4 * rows, weights[1].shape[0]
    narrow = (weights[0].shape[1] - width) // 2
    block = shaped((rows, depth), BF)
    return pl.pallas_call(
        attend_fwd_kernel,
        out_shape=(block,) * 4
        + (
            far((whole, depth)),
            shaped((whole, width), BF),
            shaped((whole, narrow), BF),
            shaped((whole, narrow), BF),
            shaped((whole, width), BF),
        ),
        in_specs=[HBM] * 4 + [VMEM] * 6,
        out_specs=(VMEM,) * 4 + (HBM,) + (VMEM,) * 4,
        scratch_shapes=[pltpu.VMEM((whole, depth), BF), pltpu.SemaphoreType.DMA((8,))],
        compiler_params=pltpu.CompilerParams(vmem_limit_bytes=12 * MIB),
        cost_estimate=cost(5e9, 12e6),
        name="attend_fwd",
    )(*in_hbm(*blocks), *weights, *tables)


def attend_bwd_kernel(
    d0, d1, d2, d3, q_ref, k_ref, v_ref, w_in, wo, cos_ref, sin_ref, pq_ref, pk_ref,
    p0, p1, p2, p3, dm_kept, d_out, dm_all, sems,
):
    rows = d0.shape[0]
    held = Rows((d0, d1, d2, d3), dm_all, sems, (dm_kept, ALL))
    width, narrow = q_ref.shape[1], k_ref.shape[1]
    whole = 4 * rows
    lane = lax.broadcasted_iota(jnp.int32, (whole, 128), 1)
    low = (lane & (HD - 1)) < HD // 2
    first_lanes = lane < HD
    cos, sin = cos_ref[...], -sin_ref[...]
    mask = pk_ref[...] <= pq_ref[...]
    keys, values = spread(k_ref[...], first_lanes), spread(v_ref[...], first_lanes)
    held.ready()
    dm = dm_all[...]
    dk_sums, dv_sums = [[None, None], [None, None]], [[None, None], [None, None]]

    def add(sums, head, side, term):
        sums[head][side] = term if sums[head][side] is None else sums[head][side] + term

    for p in range(q_ref.shape[1] // 128):
        cut = slice(p * 128, (p + 1) * 128)
        head = p // 2
        q = q_ref[:, cut]
        d_att = nt(dm, wo[cut, :]).astype(BF)
        d_q = None
        for side in range(2):
            probs = soft(q, keys[head][side], mask)
            d_probs = nt(d_att, values[head][side])
            inner = jnp.sum(d_probs * probs, axis=-1, keepdims=True)
            d_raw = (probs * (d_probs - inner) * HD**-0.5).astype(BF)
            term = nn(d_raw, keys[head][side])
            d_q = term if d_q is None else d_q + term
            add(dk_sums, head, side, tn(d_raw, q))
            add(dv_sums, head, side, tn(probs.astype(BF), d_att))
        d_out[:, cut] = turn(d_q, cos, sin, low).astype(BF)

    def folded(sums):
        return jnp.where(
            first_lanes,
            sums[0][0] + pltpu.roll(sums[0][1], 64, 1),
            pltpu.roll(sums[1][0], 64, 1) + sums[1][1],
        )

    dk = turn(folded(dk_sums), cos, sin, low).astype(BF)
    dv = folded(dv_sums).astype(BF)
    d_out[:, width : width + narrow] = dk
    d_out[:, width + narrow :] = dv
    for c in range(p0.shape[1] // COLUMNS):
        cut = slice(c * COLUMNS, (c + 1) * COLUMNS)
        out = nt(d_out[...], w_in[cut, :]).astype(BF)
        for n, part in enumerate((p0, p1, p2, p3)):
            part[:, cut] = out[n * rows : (n + 1) * rows, :]
    held.end()


def attend_bwd(blocks, qkv, weights, tables):
    rows, depth = blocks[0].shape
    whole, width = 4 * rows, weights[1].shape[0]
    narrow = (weights[0].shape[1] - width) // 2
    block = shaped((rows, depth), BF)
    return pl.pallas_call(
        attend_bwd_kernel,
        out_shape=(block,) * 4
        + (far((whole, depth)), shaped((whole, width + 2 * narrow), BF)),
        in_specs=[HBM] * 4 + [VMEM] * 9,
        out_specs=(VMEM,) * 4 + (HBM, VMEM),
        scratch_shapes=[pltpu.VMEM((whole, depth), BF), pltpu.SemaphoreType.DMA((8,))],
        compiler_params=pltpu.CompilerParams(vmem_limit_bytes=14 * MIB),
        cost_estimate=cost(7e9, 14e6),
        name="attend_bwd",
    )(*in_hbm(*blocks), *qkv, *weights, *tables)


TILE = 512


def mlp_fwd_kernel(
    x0, x1, x2, x3, wg, wu, wd, p0, p1, p2, p3, gate_out, up_out, x_kept, x_rest, x_all, total, sems
):
    rows = x0.shape[0]
    held = Rows((x0, x1, x2, x3), x_all, sems, (x_kept, (0, 2)), (x_rest, (1, 3)))
    held.ready()

    def step(f, first):
        cut = slice(0, TILE) if first else pl.ds(pl.multiple_of(f * TILE, TILE), TILE)
        x = x_all[...]
        gate, up = nn(x, wg[:, cut]), nn(x, wu[:, cut])
        gate_out[:, cut] = gate.astype(BF)
        up_out[:, cut] = up.astype(BF)
        term = nn((gate * jax.nn.sigmoid(gate) * up).astype(BF), wd[cut, :])
        total[...] = term if first else total[...] + term

    step(0, True)
    pl.loop(1, wg.shape[1] // TILE)(lambda f: step(f, False))
    for n, part in enumerate((p0, p1, p2, p3)):
        part[...] = total[n * rows : (n + 1) * rows, :].astype(BF)
    held.end()


def mlp_fwd(blocks, weights):
    rows, depth = blocks[0].shape
    units, whole = weights[0].shape[1], 4 * rows
    return pl.pallas_call(
        mlp_fwd_kernel,
        in_specs=[HBM] * 4 + [VMEM] * 3,
        out_specs=[VMEM] * 6 + [HBM] * 2,
        scratch_shapes=[
            pltpu.VMEM((whole, depth), BF),
            pltpu.VMEM((whole, depth), F32),
            pltpu.SemaphoreType.DMA((8,)),
        ],
        out_shape=[shaped((rows, depth), BF)] * 4
        + [shaped((whole, units), BF)] * 2
        + [far((whole // 2, depth))] * 2,
        compiler_params=pltpu.CompilerParams(vmem_limit_bytes=12 * MIB),
        cost_estimate=cost(6 * whole * units * depth, 30e6),
        name="mlp_fwd",
    )(*in_hbm(*blocks), *weights)


def mlp_bwd_kernel(
    g0, g1, g2, g3, gate_ref, up_ref, wg, wu, wd, p0, p1, p2, p3, g_kept, g_all, total, sems
):
    rows = g0.shape[0]
    held = Rows((g0, g1, g2, g3), g_all, sems, (g_kept, ALL))
    held.ready()

    def step(f, first):
        cut = slice(0, TILE) if first else pl.ds(pl.multiple_of(f * TILE, TILE), TILE)
        d_hidden = nt(g_all[...], wd[cut, :])
        gate, up = gate_ref[:, cut].astype(F32), up_ref[:, cut].astype(F32)
        s = jax.nn.sigmoid(gate)
        d_up = (d_hidden * gate * s).astype(BF)
        d_gate = (d_hidden * up * s * (1.0 + gate * (1.0 - s))).astype(BF)
        term = nt(d_gate, wg[:, cut]) + nt(d_up, wu[:, cut])
        total[...] = term if first else total[...] + term

    step(0, True)
    pl.loop(1, wg.shape[1] // TILE)(lambda f: step(f, False))
    for n, part in enumerate((p0, p1, p2, p3)):
        part[...] = total[n * rows : (n + 1) * rows, :].astype(BF)
    held.end()


def mlp_bwd(blocks, gate, up, weights):
    rows, depth = blocks[0].shape
    units, whole = weights[0].shape[1], 4 * rows
    return pl.pallas_call(
        mlp_bwd_kernel,
        in_specs=[HBM] * 4 + [VMEM] * 5,
        out_specs=[VMEM] * 4 + [HBM],
        scratch_shapes=[
            pltpu.VMEM((whole, depth), BF),
            pltpu.VMEM((whole, depth), F32),
            pltpu.SemaphoreType.DMA((8,)),
        ],
        out_shape=[shaped((rows, depth), BF)] * 4 + [far((whole, depth))],
        compiler_params=pltpu.CompilerParams(vmem_limit_bytes=12 * MIB),
        cost_estimate=cost(6 * whole * units * depth, 30e6),
        name="mlp_bwd",
    )(*in_hbm(*blocks), gate, up, *weights)


def mlp_both_kernel(
    x0, x1, x2, x3, g0, g1, g2, g3, wg, wu, wd,
    p0, p1, p2, p3, r0, r1, r2, r3, x_kept, x_all, g_all, gate_all, up_all, total, x_sems, g_sems,
):
    rows = x0.shape[0]
    held = Rows((x0, x1, x2, x3), x_all, x_sems, (x_kept, ALL))
    held_g = Rows((g0, g1, g2, g3), g_all, g_sems)
    held.ready()

    def tile(f, first):
        return slice(0, TILE) if first else pl.ds(pl.multiple_of(f * TILE, TILE), TILE)

    def forward(f, first):
        cut = tile(f, first)
        x = x_all[...]
        gate, up = nn(x, wg[:, cut]), nn(x, wu[:, cut])
        gate_all[:, cut] = gate.astype(BF)
        up_all[:, cut] = up.astype(BF)
        term = nn((gate * jax.nn.sigmoid(gate) * up).astype(BF), wd[cut, :])
        total[...] = term if first else total[...] + term

    def backward(f, first):
        cut = tile(f, first)
        d_hidden = nt(g_all[...], wd[cut, :])
        gate, up = gate_all[:, cut].astype(F32), up_all[:, cut].astype(F32)
        s = jax.nn.sigmoid(gate)
        d_up = (d_hidden * gate * s).astype(BF)
        d_gate = (d_hidden * up * s * (1.0 + gate * (1.0 - s))).astype(BF)
        term = nt(d_gate, wg[:, cut]) + nt(d_up, wu[:, cut])
        total[...] = term if first else total[...] + term

    for step, parts in ((forward, (p0, p1, p2, p3)), (backward, (r0, r1, r2, r3))):
        step(0, True)
        pl.loop(1, wg.shape[1] // TILE)(lambda f: step(f, False))
        for n, part in enumerate(parts):
            part[...] = total[n * rows : (n + 1) * rows, :].astype(BF)
        if step is forward:
            held_g.ready()
    held.end()


def mlp_both(blocks, g_blocks, weights):
    rows, depth = blocks[0].shape
    units, whole = weights[0].shape[1], 4 * rows
    return pl.pallas_call(
        mlp_both_kernel,
        in_specs=[HBM] * 8 + [VMEM] * 3,
        out_specs=[VMEM] * 8 + [HBM],
        scratch_shapes=[
            pltpu.VMEM((whole, depth), BF),
            pltpu.VMEM((whole, depth), BF),
            pltpu.VMEM((whole, units), BF),
            pltpu.VMEM((whole, units), BF),
            pltpu.VMEM((whole, depth), F32),
            pltpu.SemaphoreType.DMA((8,)),
            pltpu.SemaphoreType.DMA((4,)),
        ],
        out_shape=[shaped((rows, depth), BF)] * 8 + [far((whole, depth))],
        compiler_params=pltpu.CompilerParams(vmem_limit_bytes=14 * MIB),
        cost_estimate=cost(12 * whole * units * depth, 30e6),
        name="mlp_both",
    )(*in_hbm(*blocks, *g_blocks), *weights)


PIECE = 512


def mlp_grads_kernel(layer, f, first, last, has_prior, x_orders, g_orders, *refs):
    n_x, n_g = len(x_orders), len(g_orders)
    x_refs, g_refs, refs = refs[:n_x], refs[n_x : n_x + n_g], refs[n_x + n_g :]
    weights, refs = refs[:6], refs[6:]
    prior, refs = (refs[0], refs[1:]) if has_prior else (None, refs)
    out, wg, wu, wd, x_all, g_all, total, w_sems, sems = refs
    share = out.shape[0]
    units = weights[0].shape[1]
    mine = lax.axis_index("section") == layer
    column = lax.axis_index("section") * (units // 2) + f * PIECE
    cut = pl.ds(pl.multiple_of(column, PIECE), PIECE)
    start = pl.ds(pl.multiple_of(lax.axis_index("dp") * share, share), share)

    def chunk(p, slot):
        moves = []
        for to, arrays, orders in ((x_all, x_refs, x_orders), (g_all, g_refs, g_orders)):
            for a, (half, order, *relative) in zip(arrays, orders):
                rows = a.shape[1] // len(order)
                at = lax.rem(p - lax.axis_index("dp") + a.shape[0], a.shape[0]) if relative else p
                for n, place in enumerate(order):
                    target = to.at[slot, pl.ds((half * 4 + place) * rows, rows), :]
                    source = a.at[at, pl.ds(n * rows, rows), :]
                    moves.append(pltpu.make_async_copy(source, target, sems.at[slot, len(moves)]))
        return moves

    def copies(g, u, d):
        return [
            pltpu.make_async_copy(g.at[:, cut], wg, w_sems.at[0]),
            pltpu.make_async_copy(u.at[:, cut], wu, w_sems.at[1]),
            pltpu.make_async_copy(d.at[cut, :], wd, w_sems.at[2]),
        ]

    @pl.when(mine)
    def _():
        for copy in copies(*weights[0::2]):
            copy.start()

    @pl.when(jnp.logical_not(mine))
    def _():
        for copy in copies(*weights[1::2]):
            copy.start()

    for copy in chunk(first, 0):
        copy.start()
    total[...] = prior[...].astype(F32) if has_prior else jnp.zeros_like(total)
    for copy in copies(*weights[0::2]):
        copy.wait()

    @pl.loop(first, last)
    def _(p):
        slot = lax.rem(p - first, 2)

        @pl.when(p + 1 < last)
        def _():
            for copy in chunk(p + 1, 1 - slot):
                copy.start()

        for copy in chunk(p, slot):
            copy.wait()
        x = x_all[slot]
        gate, up = nn(x, wg[...]), nn(x, wu[...])
        d_hidden = nt(g_all[slot], wd[...])
        s = jax.nn.sigmoid(gate)
        gated = gate * s
        hidden = (gated * up).astype(BF)
        d_up = (d_hidden * gated).astype(BF)
        d_gate = (d_hidden * up * s * (1.0 + gate * (1.0 - s))).astype(BF)
        x_cut, g_cut = x_all[slot, :, start], g_all[slot, :, start]
        total[:, :PIECE] += tn(x_cut, d_gate)
        total[:, PIECE : 2 * PIECE] += tn(x_cut, d_up)
        total[:, 2 * PIECE :] += tn(g_cut, hidden)

    out[...] = total[...].astype(BF)


def mlp_grads(layer, f, span, xs, gs, pairs, prior=()):
    groups, _, depth = xs[0][0].shape
    first, last = span
    rows = sum(a.shape[1] for a, _ in xs)
    share = depth // groups
    return pl.pallas_call(
        functools.partial(
            mlp_grads_kernel, layer, f, first, last, bool(prior), [o for _, o in xs], [o for _, o in gs]
        ),
        in_specs=[HBM] * (len(xs) + len(gs) + 6) + [VMEM] * len(prior),
        out_specs=VMEM,
        out_shape=shaped((share, 3 * PIECE), BF),
        scratch_shapes=[
            pltpu.VMEM((depth, PIECE), BF),
            pltpu.VMEM((depth, PIECE), BF),
            pltpu.VMEM((PIECE, depth), BF),
            pltpu.VMEM((2, rows, depth), BF),
            pltpu.VMEM((2, rows, depth), BF),
            pltpu.VMEM((share, 3 * PIECE), F32),
            pltpu.SemaphoreType.DMA((3,)),
            pltpu.SemaphoreType.DMA((2, 16)),
        ],
        compiler_params=pltpu.CompilerParams(vmem_limit_bytes=50 * MIB),
        cost_estimate=cost(6 * rows * (last - first) * PIECE * (depth + share), 20e6),
        name="mlp_grads",
    )(*in_hbm(*[a for a, _ in xs], *[a for a, _ in gs], *[w for pair in pairs for w in pair]), *prior)


def assemble_kernel(n, *refs):
    shares, refs = refs[:2], refs[2:]
    sources, outs, scratch = refs[: 4 * n], refs[4 * n : 4 * n + 7], refs[4 * n + 7 :]
    q_out, k_out, v_out, o_out, gate_out, up_out, down_out = outs
    held, attn, in_rows, wide, tall, flat, sems, out_sems = scratch
    sec = lax.axis_index("section")

    def fetches(layer):
        mine = sources[layer * 2 * n : (layer + 1) * 2 * n]
        width = attn.shape[2]
        pairs = [(shares[side].at[:, pl.ds(layer * width, width)], attn.at[side]) for side in range(2)]
        pairs += [(mine[side * n + f], held.at[side, f]) for side in range(2) for f in range(n)]
        return [pltpu.make_async_copy(a, to, sems.at[k]) for k, (a, to) in enumerate(pairs)]

    for layer in range(2):

        @pl.when(sec == layer)
        def _(layer=layer):
            for move in fetches(layer):
                move.start()

    for move in fetches(0):
        move.wait()
    share, width = attn.shape[1:]
    columns = in_rows.shape[1] // 2
    half_units = wide.shape[2] // 2
    going = []

    def leave(source, target):
        going.append(pltpu.make_async_copy(source, target, out_sems.at[len(going)]))
        going[-1].start()

    q, k = q_out.shape[1], k_out.shape[1]
    halves = [sec, 1 - sec]
    rest = width - columns
    for side, half in enumerate(halves):
        in_rows[:, pl.ds(pl.multiple_of(half * columns, columns), columns)] = attn[side, :, :columns].astype(F32)
        flat[pl.ds(pl.multiple_of(half * rest, rest), rest), :] = attn[side, :, columns:].astype(F32).T
    leave(flat, o_out)
    leave(in_rows.at[:, pl.ds(0, q)], q_out)
    leave(in_rows.at[:, pl.ds(q, k)], k_out)
    leave(in_rows.at[:, pl.ds(q + k, k)], v_out)
    for kind, (target, out) in enumerate(((wide.at[0], gate_out), (wide.at[1], up_out), (tall, down_out))):
        for side, half in enumerate(halves):
            for f in range(n):
                at = pl.ds(pl.multiple_of(half * half_units + f * PIECE, PIECE), PIECE)
                cut = slice(kind * PIECE, (kind + 1) * PIECE)
                tile = held[side, f, :, cut].astype(F32)
                if kind < 2:
                    target[:, at] = tile
                else:
                    target[at, :] = tile.T
        leave(target, out)
    for move in going:
        move.wait()


def assemble(shares, layers, width, narrow, units):
    n = len(layers[0][0])
    share, attn_width = shares[0].shape[0], shares[0].shape[1] // 2
    depth_out = 2 * attn_width - width - 2 * narrow
    sources = [*shares]
    for tiles, other_tiles in layers:
        sources += [*tiles, *other_tiles]
    shapes = [(share, width), (share, narrow), (share, narrow), (depth_out, share)]
    shapes += [(share, units), (share, units), (units, share)]
    return pl.pallas_call(
        functools.partial(assemble_kernel, n),
        in_specs=[HBM] * len(sources),
        out_specs=[HBM] * 7,
        out_shape=[far(shape, F32) for shape in shapes],
        scratch_shapes=[
            pltpu.VMEM((2, n, share, 3 * PIECE), BF),
            pltpu.VMEM((2, share, attn_width), BF),
            pltpu.VMEM((share, width + 2 * narrow), F32),
            pltpu.VMEM((2, share, units), F32),
            pltpu.VMEM((units, share), F32),
            pltpu.VMEM((depth_out, share), F32),
            pltpu.SemaphoreType.DMA((2 * (n + 1),)),
            pltpu.SemaphoreType.DMA((7,)),
        ],
        compiler_params=pltpu.CompilerParams(vmem_limit_bytes=48 * MIB),
        cost_estimate=cost(0, 30e6),
        name="assemble",
    )(*in_hbm(*sources))


def attend_grads_kernel(x_own, x_other, d_own, d_other, m_own, m_other, a_own, a_other, *refs):
    out, sec = refs[-1], lax.axis_index("section")
    at = 0
    for left_own, left_other, own, other in (
        (x_own, x_other, d_own, d_other),
        (m_own, m_other, a_own, a_other),
    ):
        width = own.shape[1] // 2
        half = pl.ds(pl.multiple_of(sec * width, width), width)
        out[:, at : at + width] = (tn(left_own[...], own[:, half]) + tn(left_other[...], other[:, half])).astype(BF)
        at += width
    if len(refs) > 1:
        out[:, at:] = refs[0][...]


def attend_grads(x, d_qkv, d_mid, att, *before):
    depth, width = x.shape[1], (d_qkv.shape[1] + att.shape[1]) // 2
    terms = [x, swapped(x), d_qkv, swapped(d_qkv), d_mid, swapped(d_mid), att, swapped(att)]
    return pl.pallas_call(
        attend_grads_kernel,
        in_specs=[VMEM] * (8 + len(before)),
        out_specs=VMEM,
        out_shape=shaped((depth, width + sum(b.shape[1] for b in before)), BF),
        compiler_params=pltpu.CompilerParams(vmem_limit_bytes=14 * MIB),
        cost_estimate=cost(4 * x.size * width, 6e6),
        name="attend_grads",
    )(*terms, *before)


def summed_over_groups(x):
    return lax.psum_scatter(x, "dp", scatter_dimension=0, tiled=True)


def rope_tables(places, head_size):
    half_width = head_size // 2
    counter = jnp.arange(half_width, dtype=F32)
    base_freq = 1.0 / 500000.0 ** (2.0 * counter / head_size)
    wavelength = 2.0 * jnp.pi / base_freq
    blend_part = (8192.0 / wavelength - 1.0) / 3.0
    middle = (1.0 - blend_part) * base_freq / 32.0 + blend_part * base_freq
    frequency = jnp.where(
        wavelength < 2048.0, base_freq, jnp.where(wavelength > 8192.0, base_freq / 32.0, middle)
    )
    angles = places.astype(F32)[:, None] * frequency[None, :]
    cosine, sine = jnp.cos(angles), jnp.sin(angles)
    return (
        jnp.concatenate([cosine] * 4, axis=1),
        jnp.concatenate([-sine, sine, -sine, sine], axis=1),
    )


def halved(total, axis, size, bit, dim):
    low, high = lax.slice_in_dim(total, 0, bit, axis=dim), lax.slice_in_dim(total, bit, 2 * bit, axis=dim)
    upper = (lax.axis_index(axis) & bit) != 0
    keep, send = jnp.where(upper, high, low), jnp.where(upper, low, high)
    return keep + lax.ppermute(send, axis, [(a, a ^ bit) for a in range(size)])


def over_groups(x):
    return lax.all_gather(x, "dp", axis=0, tiled=False)


def from_both_cores(*arrays):
    return [(a, (0, places)) for a, places in arrays] + [(swapped(a), (1, places)) for a, places in arrays]


def local(groups, size, tokens, lengths, cotangent, attn_gain, mlp_gain, *weights):
    sec, t = lax.axis_index("section"), lax.axis_index("tensor")
    first = sec == 0
    rows, depth = tokens.shape[1:]
    mine = [w[0] for w in weights]
    gains = jnp.concatenate([attn_gain, mlp_gain], axis=0)
    other_gains = swapped(gains)
    layer_gains = [jnp.where(sec == l, gains, other_gains) for l in range(2)]
    attn_gains = [g[0:1] for g in layer_gains]
    mlp_gains = [g[1:2] for g in layer_gains]
    length = lax.dynamic_index_in_dim(lengths[:, 0], sec, 0, keepdims=False)
    tok = lax.dynamic_index_in_dim(tokens, sec, 0, keepdims=False)
    cot = lax.dynamic_index_in_dim(cotangent, sec, 0, keepdims=False)
    within = jnp.arange(rows, dtype=jnp.int32)
    own_places = t * rows + within
    places = jnp.concatenate([(t ^ k) * rows + within for k in range(size)])
    readable = jnp.where(places < length, places, jnp.int32(1 << 20))
    tables = rope_tables(places, HD) + (places[:, None], readable[None, :])

    g_low = jnp.where((own_places < length)[:, None], cot, jnp.zeros_like(cot))

    attn_mine = [jnp.concatenate(mine[:3], axis=1), mine[3]]
    attn_w = [(w, swapped(tied(w, other_gains))) for w in attn_mine]
    attn_cuts = [(0, w.shape[0]) for w in attn_mine]
    g_blocks1 = gather_rows(g_low, size)
    normed = tied(norm_rows(tok, attn_gains[0]), *g_blocks1)
    *weights_in, token = prefetch(0, attn_w, attn_cuts, normed)
    blocks = gather_rows(normed, size)
    all_g1 = jnp.concatenate(g_blocks1, axis=0)
    blocks[0] = tied(blocks[0], all_g1)
    all_g1 = over_groups(all_g1)
    *parts, x_attn0, q0, k0, v0, att0 = attend_fwd(blocks, weights_in, tables)
    gate_other, up_other = [swapped(tied(w, normed, *[o for _, o in attn_w])) for w in mine[4:6]]
    down_other = swapped(tied(mine[6], gate_other, parts[0]))
    mlp_w = list(zip(mine[4:], (gate_other, up_other, down_other)))
    mlp_cuts = [(0, w.shape[0]) for w in mine[4:]]
    mid0, normed = add_norm(tok, scatter_rows(parts, size), mlp_gains[0], False)
    *weights_in, token = prefetch(0, mlp_w, mlp_cuts, normed)
    *parts, gate0, up0, x_half, x_rest = mlp_fwd(gather_rows(normed, size), weights_in)
    act0, normed = add_norm(mid0, scatter_rows(parts, size), attn_gains[1], True)

    *weights_in, token = prefetch(1, attn_w, attn_cuts, normed)
    *parts, x_attn1, q1, k1, v1, att1 = attend_fwd(gather_rows(normed, size), weights_in, tables)
    parts[0] = tied(parts[0], all_g1)
    half_x0 = over_groups(tied(x_half, all_g1, parts[0]))
    mid1, normed = add_norm(act0, scatter_rows(parts, size), mlp_gains[1], False)
    *weights_in, token = prefetch(1, mlp_w, mlp_cuts, normed)
    *both_parts, x_all = mlp_both(gather_rows(normed, size), g_blocks1, weights_in)
    parts1, parts = both_parts[:size], both_parts[size:]
    parts[0] = tied(parts[0], half_x0)
    all_x1 = over_groups(tied(x_all, half_x0, parts[0]))
    d_mid, d_mid_low, mlp_part1 = norm_back(mid1, scatter_rows(parts, size), mlp_gains[1], g_low)
    rest_x0 = [x_rest]

    def with_chunk(blocks, results):
        group = lax.rem(lax.axis_index("dp") + len(rest_x0), groups)
        sent = lax.dynamic_index_in_dim(half_x0, group, 0, False)
        chunk = lax.ppermute(tied(sent, *blocks), "tensor", partners(size)[0])
        results, chunk = lax.optimization_barrier((list(results), chunk))
        rest_x0.append(chunk)
        return results

    *weights_in, token = prefetch(1, attn_w, attn_cuts, d_mid_low)
    blocks = gather_rows(d_mid_low, size)
    *parts, dm, dqkv = with_chunk(blocks, attend_bwd(blocks, (q1, k1, v1), weights_in, tables))
    attn_terms1 = attend_grads(x_attn1, dqkv, dm, att1)
    came = scatter_rows(parts, size)
    came[0] = tied(came[0], attn_terms1)
    d_stream1, d_low, attn_part1 = norm_back(act0, came, attn_gains[1], d_mid)

    *weights_in, token = prefetch(0, mlp_w, mlp_cuts, d_low)
    *parts, g_rows = with_chunk([token], mlp_bwd(gather_rows(d_low, size), gate0, up0, weights_in))
    parts[0] = tied(parts[0], all_x1)
    all_g0 = over_groups(tied(g_rows, all_x1, parts[0]))
    x1, g1 = from_both_cores((all_x1, ALL)), from_both_cores((all_g1, ALL))
    middle = groups // 2
    d_mid, d_mid_low, mlp_part0 = norm_back(mid0, scatter_rows(parts, size), mlp_gains[0], d_low)
    *weights_in, token = prefetch(0, attn_w, attn_cuts, d_mid_low)
    blocks = gather_rows(d_mid_low, size)
    late_x1 = [(tied(a, d_mid_low, token), o) for a, o in x1]
    tile = mlp_grads(1, 0, (0, middle), late_x1, g1, mlp_w)
    blocks[0] = tied(blocks[0], tile)
    *parts, dm, dqkv = with_chunk(blocks, attend_bwd(blocks, (q0, k0, v0), weights_in, tables))
    attn_terms = attend_grads(x_attn0, dqkv, dm, att0, attn_terms1)
    late_x1 = [(tied(a, parts[0], attn_terms), o) for a, o in x1]
    tile = mlp_grads(1, 0, (middle, groups), late_x1, g1, mlp_w, (tile,))
    came = scatter_rows(parts, size)
    came[0] = tied(came[0], tile)
    d_stream0, _, attn_part0 = norm_back(tok, came, attn_gains[0], d_mid)

    def beside(results, *transfers):
        results, transfers = lax.optimization_barrier((results, list(transfers)))
        return results, transfers

    def halves(axis, count, dim, bit, total):
        low, high = lax.slice_in_dim(total, 0, bit, axis=dim), lax.slice_in_dim(total, bit, 2 * bit, axis=dim)
        upper = (lax.axis_index(axis) & bit) != 0
        came = lax.ppermute(jnp.where(upper, low, high), axis, [(a, a ^ bit) for a in range(count)])
        return jnp.where(upper, high, low), came

    steps = [("tensor", size, 2, 1 << n) for n in reversed(range(size.bit_length() - 1))]

    def step_beside(results, *transfers):
        nonlocal shares
        keep, came = halves(*steps.pop(0), shares)
        results, (came, *transfers) = beside(results, came, *transfers)
        shares = keep + came
        return results, transfers

    while len(rest_x0) < groups:
        with_chunk([d_stream0], [])
    rest_own = jnp.stack(rest_x0)
    attn_share = summed_over_groups(tied(attn_terms, all_g0, d_stream0))
    shares = jnp.concatenate([attn_part0, mlp_part0, attn_part1, mlp_part1], axis=0)
    shares = shares.reshape(2, 2 * groups, size, depth // (groups * size))
    stream_keep, stream_send = jnp.where(first, d_stream0, d_stream1), jnp.where(first, d_stream1, d_stream0)
    late_x1 = [(tied(a, d_stream0), o) for a, o in x1]
    tiles1 = [tile]
    tile, (rest_other, g0_other, moved, stream_came) = step_beside(
        mlp_grads(1, 1, (0, groups), late_x1, g1, mlp_w),
        swapped(rest_own),
        swapped(tied(all_g0, d_stream0)),
        swapped(tile),
        swapped(stream_send),
    )
    tiles1.append(tile)
    others1 = [moved]
    x0 = from_both_cores((half_x0, (0, 2))) + [(rest_own, (0, (1, 3), True)), (rest_other, (1, (1, 3), True))]
    g0 = [(all_g0, (0, ALL)), (g0_other, (1, ALL))]
    act_terms = scatter_rows([tied(p, tile) for p in parts1], size)
    tile, (moved, *act_terms[1:]) = step_beside(
        mlp_grads(0, 0, (0, groups), [(tied(a, tile), o) for a, o in x0], g0, mlp_w),
        swapped(tiles1[1]),
        *act_terms[1:],
    )
    tiles0 = [tile]
    others1.append(moved)
    act1, _ = add_norm(mid1, act_terms, attn_gains[1], True)
    act_keep, act_send = jnp.where(first, act0, act1), jnp.where(first, act1, act0)
    while steps:
        step_beside([])
    by_group, i = shares.reshape(4, groups, -1), lax.axis_index("dp")
    group_terms = []
    for k in range(1, groups):
        sent = lax.dynamic_index_in_dim(by_group, lax.rem(i + k, groups), 1, False)
        group_terms.append(lax.ppermute(sent, "dp", [(j, (j + k) % groups) for j in range(groups)]))
    tile, (moved, act_came, *group_terms) = beside(
        mlp_grads(0, 1, (0, groups), [(tied(a, tile, act_keep), o) for a, o in x0], g0, mlp_w),
        swapped(tiles0[0]),
        swapped(act_send),
        *group_terms,
    )
    shares = lax.dynamic_index_in_dim(by_group, i, 1, False) + sum(group_terms)
    shares = shares.reshape(2, 2, -1)
    shares_keep, shares_send = jnp.where(first, shares[0], shares[1]), jnp.where(first, shares[1], shares[0])
    tiles0.append(tile)
    others0 = [moved, swapped(tile)]
    attn_share = tied(attn_share, tile)
    attn_other = swapped(attn_share)
    weight_grads = assemble(
        (attn_share, attn_other),
        ((tiles0, others0), (tiles1, others1)),
        mine[0].shape[1],
        mine[1].shape[1],
        mine[4].shape[1],
    )
    weight_grads, (shares,) = beside(weight_grads, swapped(shares_send))
    shares = shares_keep + shares

    def both(keep, came):
        return jnp.stack([jnp.where(first, keep, came), jnp.where(first, came, keep)])[None]

    return (
        both(act_keep, act_came),
        both(stream_keep, stream_came),
        shares[0:1],
        shares[1:2],
        *[grad[None] for grad in weight_grads],
    )


def solution(mesh):
    rows = P(None, ("dp", "tensor"), None)
    in_specs = (
        rows,
        P(None, "dp"),
        rows,
        P("section", None),
        P("section", None),
        P("section", None, "tensor"),
        P("section", None, "tensor"),
        P("section", None, "tensor"),
        P("section", "tensor", None),
        P("section", None, "tensor"),
        P("section", None, "tensor"),
        P("section", "tensor", None),
    )
    out_rows = P("section", None, ("dp", "tensor"), None)
    shares = P("section", ("dp", "tensor"))
    by_dp, by_tensor = P("section", "dp", "tensor"), P("section", "tensor", "dp")
    out_specs = (
        out_rows, out_rows, shares, shares, by_dp, by_dp, by_dp, by_tensor, by_dp, by_dp, by_tensor,
    )
    step = functools.partial(local, mesh.shape["dp"], mesh.shape["tensor"])
    return jax.shard_map(step, mesh=mesh, in_specs=in_specs, out_specs=out_specs, check_vma=False)
```

```python
import functools

import jax
import jax.numpy as jnp
from jax import lax
from jax.experimental import pallas as pl
from jax.experimental.pallas import tpu as pltpu
from jax.sharding import PartitionSpec as P

HD = 64
EPSILON = 1e-05
NEGATIVE = -1e30
BF = jnp.bfloat16
F32 = jnp.float32
VMEM = pl.BlockSpec(memory_space=pltpu.VMEM)
HBM = pl.BlockSpec(memory_space=pltpu.HBM)
ANY = pl.BlockSpec(memory_space=pl.ANY)
MIB = 1024 * 1024
SHRINK = 20


def nn(a, b):
    return jnp.dot(a, b, preferred_element_type=F32)


def nt(a, b):
    return lax.dot_general(a, b, (((1,), (1,)), ((), ())), preferred_element_type=F32)


def tn(a, b):
    return lax.dot_general(a, b, (((0,), (0,)), ((), ())), preferred_element_type=F32)


def shaped(shape, dtype):
    return jax.ShapeDtypeStruct(shape, dtype)


def far(shape, dtype=BF):
    return pltpu.HBM(shape, dtype)


def in_hbm(*arrays):
    return [pltpu.with_memory_space_constraint(a, pltpu.HBM) for a in arrays]


def tied(first, *others):
    return lax.optimization_barrier((first, *others))[0]


def cost(flops, nbytes):
    return pl.CostEstimate(flops=int(flops / SHRINK), bytes_accessed=int(nbytes / SHRINK), transcendentals=0)


def partners(size):
    return [[(a, a ^ k) for a in range(size)] for k in range(1, size)]


def gather_rows(x, size):
    return [x] + [lax.ppermute(x, "tensor", pairs) for pairs in partners(size)]


def scatter_rows(parts, size):
    return [parts[0]] + [
        lax.ppermute(part, "tensor", pairs) for part, pairs in zip(parts[1:], partners(size))
    ]


def swapped(x):
    return lax.ppermute(x, "section", [(0, 1), (1, 0)])


def norm_kernel(x_ref, gain_ref, out_ref):
    x = x_ref[...].astype(F32)
    scale = lax.rsqrt(jnp.mean(x * x, axis=-1, keepdims=True) + EPSILON)
    out_ref[...] = (x * scale * gain_ref[...]).astype(BF)


def norm_rows(x, gain):
    return pl.pallas_call(
        norm_kernel, name="norm", cost_estimate=cost(0, 1e6), out_shape=shaped(x.shape, BF), in_specs=[VMEM] * 2, out_specs=VMEM
    )(x, gain)


def add_norm_kernel(round_out, base_ref, a_ref, b_ref, c_ref, d_ref, gain_ref, out_ref, normed_ref):
    x = base_ref[...].astype(F32) + (
        (a_ref[...].astype(F32) + b_ref[...].astype(F32))
        + (c_ref[...].astype(F32) + d_ref[...].astype(F32))
    )
    if round_out:
        x = x.astype(BF)
        out_ref[...] = x
        x = x.astype(F32)
    else:
        out_ref[...] = x
    scale = lax.rsqrt(jnp.mean(x * x, axis=-1, keepdims=True) + EPSILON)
    normed_ref[...] = (x * scale * gain_ref[...]).astype(BF)


def add_norm(base, terms, gain, round_out):
    return pl.pallas_call(
        functools.partial(add_norm_kernel, round_out),
        name="add_norm",
        cost_estimate=cost(0, 2e6),
        out_shape=(shaped(base.shape, BF if round_out else F32), shaped(base.shape, BF)),
        in_specs=[VMEM] * 6,
        out_specs=(VMEM, VMEM),
    )(base, *terms, gain)


def norm_back_kernel(base_ref, a_ref, b_ref, c_ref, d_ref, gain_ref, res_ref, out_ref, low_ref, gp_ref):
    g = (a_ref[...].astype(F32) + b_ref[...].astype(F32)) + (
        c_ref[...].astype(F32) + d_ref[...].astype(F32)
    )
    x = base_ref[...].astype(F32)
    scale = lax.rsqrt(jnp.mean(x * x, axis=-1, keepdims=True) + EPSILON)
    y = x * scale
    gp_ref[...] = jnp.sum(g * y, axis=0, keepdims=True)
    e = g * gain_ref[...]
    out = res_ref[...].astype(F32) + scale * (e - y * jnp.mean(e * y, axis=-1, keepdims=True))
    out_ref[...] = out
    low_ref[...] = out.astype(BF)


def norm_back(base, terms, gain, residual):
    return pl.pallas_call(
        norm_back_kernel,
        name="norm_back",
        cost_estimate=cost(0, 3e6),
        out_shape=(shaped(base.shape, F32), shaped(base.shape, BF), shaped((1, base.shape[1]), F32)),
        in_specs=[VMEM] * 7,
        out_specs=(VMEM,) * 3,
    )(base, *terms, gain, residual)


def prefetch_kernel(layer, cuts, after_ref, *refs):
    sources, refs = refs[: 2 * len(cuts)], refs[2 * len(cuts) :]
    total = sum(len(cut) - 1 for cut in cuts)
    buffers, token, sems = refs[:total], refs[total], refs[-1]
    token[...] = jnp.zeros_like(token)
    mine = lax.axis_index("section") == layer

    def copies(side):
        moves = []
        for source, cut in zip(sources[side::2], cuts):
            for at, to in zip(cut, cut[1:]):
                n = len(moves)
                part = source.at[pl.ds(at, to - at), :]
                moves.append(pltpu.make_async_copy(part, buffers[n], sems.at[n]))
        return moves

    @pl.when(mine)
    def _():
        for copy in copies(0):
            copy.start()

    @pl.when(jnp.logical_not(mine))
    def _():
        for copy in copies(1):
            copy.start()

    for copy in copies(0):
        copy.wait()


def prefetch(layer, pairs, cuts, after):
    shapes = [
        (to - at, own.shape[1]) for (own, _), cut in zip(pairs, cuts) for at, to in zip(cut, cut[1:])
    ]
    return pl.pallas_call(
        functools.partial(prefetch_kernel, layer, cuts),
        out_shape=[pltpu.VMEM(shape, BF) for shape in shapes] + [shaped((8, 128), F32)],
        in_specs=[ANY] + [HBM] * (2 * len(pairs)),
        out_specs=[VMEM] * (len(shapes) + 1),
        scratch_shapes=[pltpu.SemaphoreType.DMA((len(shapes),))],
        compiler_params=pltpu.CompilerParams(vmem_limit_bytes=MIB),
        cost_estimate=cost(0, sum(4 * a * b for a, b in shapes)),
        name="prefetch",
    )(after, *in_hbm(*[w for pair in pairs for w in pair]))


def turn(x, cos, sin, low):
    return x * cos + jnp.where(low, pltpu.roll(x, 96, 1), pltpu.roll(x, 32, 1)) * sin


def spread(x, first_lanes):
    x = x.astype(F32)
    moved = pltpu.roll(x, 64, 1)
    zero = jnp.zeros_like(x)
    return [
        (jnp.where(first_lanes, x, zero).astype(BF), jnp.where(first_lanes, zero, moved).astype(BF)),
        (jnp.where(first_lanes, moved, zero).astype(BF), jnp.where(first_lanes, zero, x).astype(BF)),
    ]


def soft(q, k, mask):
    scores = jnp.where(mask, nt(q, k) * HD**-0.5, NEGATIVE)
    lifted = jnp.exp(scores - jnp.max(scores, axis=-1, keepdims=True))
    return lifted * (1.0 / jnp.sum(lifted, axis=-1, keepdims=True))


class Rows:
    def __init__(self, blocks, buffer, sems, *kept):
        rows = blocks[0].shape[0]
        self.come = [
            pltpu.make_async_copy(b, buffer.at[pl.ds(n * rows, rows), :], sems.at[n])
            for n, b in enumerate(blocks)
        ]
        self.go = []
        for ref, order in kept:
            for at, n in enumerate(order):
                source, target = buffer.at[pl.ds(n * rows, rows), :], ref.at[pl.ds(at * rows, rows), :]
                sem = sems.at[len(blocks) + len(self.go)]
                self.go.append(pltpu.make_async_copy(source, target, sem))
        for copy in self.come:
            copy.start()

    def ready(self):
        for copy in self.come:
            copy.wait()
        for copy in self.go:
            copy.start()

    def end(self):
        for copy in self.go:
            copy.wait()


ALL = (0, 1, 2, 3)


COLUMNS = 512


def attend_fwd_kernel(
    x0, x1, x2, x3, w_in, wo, cos_ref, sin_ref, pq_ref, pk_ref,
    p0, p1, p2, p3, x_kept, q_out, k_out, v_out, att_out, x_all, sems,
):
    rows = x0.shape[0]
    held = Rows((x0, x1, x2, x3), x_all, sems, (x_kept, ALL))
    whole = 4 * rows
    lane = lax.broadcasted_iota(jnp.int32, (whole, 128), 1)
    low = (lane & (HD - 1)) < HD // 2
    first_lanes = lane < HD
    cos, sin = cos_ref[...], sin_ref[...]
    mask = pk_ref[...] <= pq_ref[...]
    held.ready()
    x = x_all[...]
    width, narrow = q_out.shape[1], k_out.shape[1]
    k = turn(nn(x, w_in[:, width : width + narrow]), cos, sin, low).astype(BF)
    v = nn(x, w_in[:, width + narrow :]).astype(BF)
    k_out[...] = k
    v_out[...] = v
    keys, values = spread(k, first_lanes), spread(v, first_lanes)
    for p in range(q_out.shape[1] // 128):
        cut = slice(p * 128, (p + 1) * 128)
        q = turn(nn(x, w_in[:, cut]), cos, sin, low).astype(BF)
        q_out[:, cut] = q
        head = p // 2
        att_out[:, cut] = (
            nn(soft(q, keys[head][0], mask).astype(BF), values[head][0])
            + nn(soft(q, keys[head][1], mask).astype(BF), values[head][1])
        ).astype(BF)
    att = att_out[...]
    for c in range(p0.shape[1] // COLUMNS):
        cut = slice(c * COLUMNS, (c + 1) * COLUMNS)
        out = nn(att, wo[:, cut]).astype(BF)
        for n, part in enumerate((p0, p1, p2, p3)):
            part[:, cut] = out[n * rows : (n + 1) * rows, :]
    held.end()


def attend_fwd(blocks, weights, tables):
    rows, depth = blocks[0].shape
    whole, width = 4 * rows, weights[1].shape[0]
    narrow = (weights[0].shape[1] - width) // 2
    block = shaped((rows, depth), BF)
    return pl.pallas_call(
        attend_fwd_kernel,
        out_shape=(block,) * 4
        + (
            far((whole, depth)),
            shaped((whole, width), BF),
            shaped((whole, narrow), BF),
            shaped((whole, narrow), BF),
            shaped((whole, width), BF),
        ),
        in_specs=[HBM] * 4 + [VMEM] * 6,
        out_specs=(VMEM,) * 4 + (HBM,) + (VMEM,) * 4,
        scratch_shapes=[pltpu.VMEM((whole, depth), BF), pltpu.SemaphoreType.DMA((8,))],
        compiler_params=pltpu.CompilerParams(vmem_limit_bytes=12 * MIB),
        cost_estimate=cost(5e9, 12e6),
        name="attend_fwd",
    )(*in_hbm(*blocks), *weights, *tables)


def attend_bwd_kernel(
    d0, d1, d2, d3, q_ref, k_ref, v_ref, w_in, wo, cos_ref, sin_ref, pq_ref, pk_ref,
    p0, p1, p2, p3, dm_kept, d_out, dm_all, sems,
):
    rows = d0.shape[0]
    held = Rows((d0, d1, d2, d3), dm_all, sems, (dm_kept, ALL))
    width, narrow = q_ref.shape[1], k_ref.shape[1]
    whole = 4 * rows
    lane = lax.broadcasted_iota(jnp.int32, (whole, 128), 1)
    low = (lane & (HD - 1)) < HD // 2
    first_lanes = lane < HD
    cos, sin = cos_ref[...], -sin_ref[...]
    mask = pk_ref[...] <= pq_ref[...]
    keys, values = spread(k_ref[...], first_lanes), spread(v_ref[...], first_lanes)
    held.ready()
    dm = dm_all[...]
    dk_sums, dv_sums = [[None, None], [None, None]], [[None, None], [None, None]]

    def add(sums, head, side, term):
        sums[head][side] = term if sums[head][side] is None else sums[head][side] + term

    for p in range(q_ref.shape[1] // 128):
        cut = slice(p * 128, (p + 1) * 128)
        head = p // 2
        q = q_ref[:, cut]
        d_att = nt(dm, wo[cut, :]).astype(BF)
        d_q = None
        for side in range(2):
            probs = soft(q, keys[head][side], mask)
            d_probs = nt(d_att, values[head][side])
            inner = jnp.sum(d_probs * probs, axis=-1, keepdims=True)
            d_raw = (probs * (d_probs - inner) * HD**-0.5).astype(BF)
            term = nn(d_raw, keys[head][side])
            d_q = term if d_q is None else d_q + term
            add(dk_sums, head, side, tn(d_raw, q))
            add(dv_sums, head, side, tn(probs.astype(BF), d_att))
        d_out[:, cut] = turn(d_q, cos, sin, low).astype(BF)

    def folded(sums):
        return jnp.where(
            first_lanes,
            sums[0][0] + pltpu.roll(sums[0][1], 64, 1),
            pltpu.roll(sums[1][0], 64, 1) + sums[1][1],
        )

    dk = turn(folded(dk_sums), cos, sin, low).astype(BF)
    dv = folded(dv_sums).astype(BF)
    d_out[:, width : width + narrow] = dk
    d_out[:, width + narrow :] = dv
    for c in range(p0.shape[1] // COLUMNS):
        cut = slice(c * COLUMNS, (c + 1) * COLUMNS)
        out = nt(d_out[...], w_in[cut, :]).astype(BF)
        for n, part in enumerate((p0, p1, p2, p3)):
            part[:, cut] = out[n * rows : (n + 1) * rows, :]
    held.end()


def attend_bwd(blocks, qkv, weights, tables):
    rows, depth = blocks[0].shape
    whole, width = 4 * rows, weights[1].shape[0]
    narrow = (weights[0].shape[1] - width) // 2
    block = shaped((rows, depth), BF)
    return pl.pallas_call(
        attend_bwd_kernel,
        out_shape=(block,) * 4
        + (far((whole, depth)), shaped((whole, width + 2 * narrow), BF)),
        in_specs=[HBM] * 4 + [VMEM] * 9,
        out_specs=(VMEM,) * 4 + (HBM, VMEM),
        scratch_shapes=[pltpu.VMEM((whole, depth), BF), pltpu.SemaphoreType.DMA((8,))],
        compiler_params=pltpu.CompilerParams(vmem_limit_bytes=14 * MIB),
        cost_estimate=cost(7e9, 14e6),
        name="attend_bwd",
    )(*in_hbm(*blocks), *qkv, *weights, *tables)


TILE = 512


def mlp_fwd_kernel(
    x0, x1, x2, x3, wg, wu, wd, p0, p1, p2, p3, gate_out, up_out, x_kept, x_rest, x_all, total, sems
):
    rows = x0.shape[0]
    held = Rows((x0, x1, x2, x3), x_all, sems, (x_kept, (0, 2)), (x_rest, (1, 3)))
    held.ready()

    def step(f, first):
        cut = slice(0, TILE) if first else pl.ds(pl.multiple_of(f * TILE, TILE), TILE)
        x = x_all[...]
        gate, up = nn(x, wg[:, cut]), nn(x, wu[:, cut])
        gate_out[:, cut] = gate.astype(BF)
        up_out[:, cut] = up.astype(BF)
        term = nn((gate * jax.nn.sigmoid(gate) * up).astype(BF), wd[cut, :])
        total[...] = term if first else total[...] + term

    step(0, True)
    pl.loop(1, wg.shape[1] // TILE)(lambda f: step(f, False))
    for n, part in enumerate((p0, p1, p2, p3)):
        part[...] = total[n * rows : (n + 1) * rows, :].astype(BF)
    held.end()


def mlp_fwd(blocks, weights):
    rows, depth = blocks[0].shape
    units, whole = weights[0].shape[1], 4 * rows
    return pl.pallas_call(
        mlp_fwd_kernel,
        in_specs=[HBM] * 4 + [VMEM] * 3,
        out_specs=[VMEM] * 6 + [HBM] * 2,
        scratch_shapes=[
            pltpu.VMEM((whole, depth), BF),
            pltpu.VMEM((whole, depth), F32),
            pltpu.SemaphoreType.DMA((8,)),
        ],
        out_shape=[shaped((rows, depth), BF)] * 4
        + [shaped((whole, units), BF)] * 2
        + [far((whole // 2, depth))] * 2,
        compiler_params=pltpu.CompilerParams(vmem_limit_bytes=12 * MIB),
        cost_estimate=cost(6 * whole * units * depth, 30e6),
        name="mlp_fwd",
    )(*in_hbm(*blocks), *weights)


def mlp_bwd_kernel(
    g0, g1, g2, g3, gate_ref, up_ref, wg, wu, wd, p0, p1, p2, p3, g_kept, g_all, total, sems
):
    rows = g0.shape[0]
    held = Rows((g0, g1, g2, g3), g_all, sems, (g_kept, ALL))
    held.ready()

    def step(f, first):
        cut = slice(0, TILE) if first else pl.ds(pl.multiple_of(f * TILE, TILE), TILE)
        d_hidden = nt(g_all[...], wd[cut, :])
        gate, up = gate_ref[:, cut].astype(F32), up_ref[:, cut].astype(F32)
        s = jax.nn.sigmoid(gate)
        d_up = (d_hidden * gate * s).astype(BF)
        d_gate = (d_hidden * up * s * (1.0 + gate * (1.0 - s))).astype(BF)
        term = nt(d_gate, wg[:, cut]) + nt(d_up, wu[:, cut])
        total[...] = term if first else total[...] + term

    step(0, True)
    pl.loop(1, wg.shape[1] // TILE)(lambda f: step(f, False))
    for n, part in enumerate((p0, p1, p2, p3)):
        part[...] = total[n * rows : (n + 1) * rows, :].astype(BF)
    held.end()


def mlp_bwd(blocks, gate, up, weights):
    rows, depth = blocks[0].shape
    units, whole = weights[0].shape[1], 4 * rows
    return pl.pallas_call(
        mlp_bwd_kernel,
        in_specs=[HBM] * 4 + [VMEM] * 5,
        out_specs=[VMEM] * 4 + [HBM],
        scratch_shapes=[
            pltpu.VMEM((whole, depth), BF),
            pltpu.VMEM((whole, depth), F32),
            pltpu.SemaphoreType.DMA((8,)),
        ],
        out_shape=[shaped((rows, depth), BF)] * 4 + [far((whole, depth))],
        compiler_params=pltpu.CompilerParams(vmem_limit_bytes=12 * MIB),
        cost_estimate=cost(6 * whole * units * depth, 30e6),
        name="mlp_bwd",
    )(*in_hbm(*blocks), gate, up, *weights)


def mlp_both_kernel(
    x0, x1, x2, x3, g0, g1, g2, g3, wg, wu, wd,
    p0, p1, p2, p3, r0, r1, r2, r3, x_kept, x_all, g_all, gate_all, up_all, total, x_sems, g_sems,
):
    rows = x0.shape[0]
    held = Rows((x0, x1, x2, x3), x_all, x_sems, (x_kept, ALL))
    held_g = Rows((g0, g1, g2, g3), g_all, g_sems)
    held.ready()

    def tile(f, first):
        return slice(0, TILE) if first else pl.ds(pl.multiple_of(f * TILE, TILE), TILE)

    def forward(f, first):
        cut = tile(f, first)
        x = x_all[...]
        gate, up = nn(x, wg[:, cut]), nn(x, wu[:, cut])
        gate_all[:, cut] = gate.astype(BF)
        up_all[:, cut] = up.astype(BF)
        term = nn((gate * jax.nn.sigmoid(gate) * up).astype(BF), wd[cut, :])
        total[...] = term if first else total[...] + term

    def backward(f, first):
        cut = tile(f, first)
        d_hidden = nt(g_all[...], wd[cut, :])
        gate, up = gate_all[:, cut].astype(F32), up_all[:, cut].astype(F32)
        s = jax.nn.sigmoid(gate)
        d_up = (d_hidden * gate * s).astype(BF)
        d_gate = (d_hidden * up * s * (1.0 + gate * (1.0 - s))).astype(BF)
        term = nt(d_gate, wg[:, cut]) + nt(d_up, wu[:, cut])
        total[...] = term if first else total[...] + term

    for step, parts in ((forward, (p0, p1, p2, p3)), (backward, (r0, r1, r2, r3))):
        step(0, True)
        pl.loop(1, wg.shape[1] // TILE)(lambda f: step(f, False))
        for n, part in enumerate(parts):
            part[...] = total[n * rows : (n + 1) * rows, :].astype(BF)
        if step is forward:
            held_g.ready()
    held.end()


def mlp_both(blocks, g_blocks, weights):
    rows, depth = blocks[0].shape
    units, whole = weights[0].shape[1], 4 * rows
    return pl.pallas_call(
        mlp_both_kernel,
        in_specs=[HBM] * 8 + [VMEM] * 3,
        out_specs=[VMEM] * 8 + [HBM],
        scratch_shapes=[
            pltpu.VMEM((whole, depth), BF),
            pltpu.VMEM((whole, depth), BF),
            pltpu.VMEM((whole, units), BF),
            pltpu.VMEM((whole, units), BF),
            pltpu.VMEM((whole, depth), F32),
            pltpu.SemaphoreType.DMA((8,)),
            pltpu.SemaphoreType.DMA((4,)),
        ],
        out_shape=[shaped((rows, depth), BF)] * 8 + [far((whole, depth))],
        compiler_params=pltpu.CompilerParams(vmem_limit_bytes=14 * MIB),
        cost_estimate=cost(12 * whole * units * depth, 30e6),
        name="mlp_both",
    )(*in_hbm(*blocks, *g_blocks), *weights)


PIECE = 512


def mlp_grads_kernel(layer, f, first, last, has_prior, x_orders, g_orders, *refs):
    n_x, n_g = len(x_orders), len(g_orders)
    x_refs, g_refs, refs = refs[:n_x], refs[n_x : n_x + n_g], refs[n_x + n_g :]
    weights, refs = refs[:6], refs[6:]
    prior, refs = (refs[0], refs[1:]) if has_prior else (None, refs)
    out, wg, wu, wd, x_all, g_all, total, w_sems, sems = refs
    share = out.shape[0]
    units = weights[0].shape[1]
    mine = lax.axis_index("section") == layer
    column = lax.axis_index("section") * (units // 2) + f * PIECE
    cut = pl.ds(pl.multiple_of(column, PIECE), PIECE)
    start = pl.ds(pl.multiple_of(lax.axis_index("dp") * share, share), share)

    def chunk(p, slot):
        moves = []
        for to, arrays, orders in ((x_all, x_refs, x_orders), (g_all, g_refs, g_orders)):
            for a, (half, order, *relative) in zip(arrays, orders):
                rows = a.shape[1] // len(order)
                at = lax.rem(p - lax.axis_index("dp") + a.shape[0], a.shape[0]) if relative else p
                for n, place in enumerate(order):
                    target = to.at[slot, pl.ds((half * 4 + place) * rows, rows), :]
                    source = a.at[at, pl.ds(n * rows, rows), :]
                    moves.append(pltpu.make_async_copy(source, target, sems.at[slot, len(moves)]))
        return moves

    def copies(g, u, d):
        return [
            pltpu.make_async_copy(g.at[:, cut], wg, w_sems.at[0]),
            pltpu.make_async_copy(u.at[:, cut], wu, w_sems.at[1]),
            pltpu.make_async_copy(d.at[cut, :], wd, w_sems.at[2]),
        ]

    @pl.when(mine)
    def _():
        for copy in copies(*weights[0::2]):
            copy.start()

    @pl.when(jnp.logical_not(mine))
    def _():
        for copy in copies(*weights[1::2]):
            copy.start()

    for copy in chunk(first, 0):
        copy.start()
    total[...] = prior[...].astype(F32) if has_prior else jnp.zeros_like(total)
    for copy in copies(*weights[0::2]):
        copy.wait()

    @pl.loop(first, last)
    def _(p):
        slot = lax.rem(p - first, 2)

        @pl.when(p + 1 < last)
        def _():
            for copy in chunk(p + 1, 1 - slot):
                copy.start()

        for copy in chunk(p, slot):
            copy.wait()
        x = x_all[slot]
        gate, up = nn(x, wg[...]), nn(x, wu[...])
        d_hidden = nt(g_all[slot], wd[...])
        s = jax.nn.sigmoid(gate)
        gated = gate * s
        hidden = (gated * up).astype(BF)
        d_up = (d_hidden * gated).astype(BF)
        d_gate = (d_hidden * up * s * (1.0 + gate * (1.0 - s))).astype(BF)
        x_cut, g_cut = x_all[slot, :, start], g_all[slot, :, start]
        total[:, :PIECE] += tn(x_cut, d_gate)
        total[:, PIECE : 2 * PIECE] += tn(x_cut, d_up)
        total[:, 2 * PIECE :] += tn(g_cut, hidden)

    out[...] = total[...].astype(BF)


def mlp_grads(layer, f, span, xs, gs, pairs, prior=()):
    groups, _, depth = xs[0][0].shape
    first, last = span
    rows = sum(a.shape[1] for a, _ in xs)
    share = depth // groups
    return pl.pallas_call(
        functools.partial(
            mlp_grads_kernel, layer, f, first, last, bool(prior), [o for _, o in xs], [o for _, o in gs]
        ),
        in_specs=[HBM] * (len(xs) + len(gs) + 6) + [VMEM] * len(prior),
        out_specs=VMEM,
        out_shape=shaped((share, 3 * PIECE), BF),
        scratch_shapes=[
            pltpu.VMEM((depth, PIECE), BF),
            pltpu.VMEM((depth, PIECE), BF),
            pltpu.VMEM((PIECE, depth), BF),
            pltpu.VMEM((2, rows, depth), BF),
            pltpu.VMEM((2, rows, depth), BF),
            pltpu.VMEM((share, 3 * PIECE), F32),
            pltpu.SemaphoreType.DMA((3,)),
            pltpu.SemaphoreType.DMA((2, 16)),
        ],
        compiler_params=pltpu.CompilerParams(vmem_limit_bytes=50 * MIB),
        cost_estimate=cost(6 * rows * (last - first) * PIECE * (depth + share), 20e6),
        name="mlp_grads",
    )(*in_hbm(*[a for a, _ in xs], *[a for a, _ in gs], *[w for pair in pairs for w in pair]), *prior)


def assemble_kernel(n, *refs):
    shares, refs = refs[:2], refs[2:]
    sources, outs, scratch = refs[: 4 * n], refs[4 * n : 4 * n + 7], refs[4 * n + 7 :]
    q_out, k_out, v_out, o_out, gate_out, up_out, down_out = outs
    held, attn, in_rows, wide, tall, flat, sems, out_sems = scratch
    sec = lax.axis_index("section")

    def fetches(layer):
        mine = sources[layer * 2 * n : (layer + 1) * 2 * n]
        width = attn.shape[2]
        pairs = [(shares[side].at[:, pl.ds(layer * width, width)], attn.at[side]) for side in range(2)]
        pairs += [(mine[side * n + f], held.at[side, f]) for side in range(2) for f in range(n)]
        return [pltpu.make_async_copy(a, to, sems.at[k]) for k, (a, to) in enumerate(pairs)]

    for layer in range(2):

        @pl.when(sec == layer)
        def _(layer=layer):
            for move in fetches(layer):
                move.start()

    for move in fetches(0):
        move.wait()
    share, width = attn.shape[1:]
    columns = in_rows.shape[1] // 2
    half_units = wide.shape[2] // 2
    going = []

    def leave(source, target):
        going.append(pltpu.make_async_copy(source, target, out_sems.at[len(going)]))
        going[-1].start()

    q, k = q_out.shape[1], k_out.shape[1]
    halves = [sec, 1 - sec]
    rest = width - columns
    for side, half in enumerate(halves):
        in_rows[:, pl.ds(pl.multiple_of(half * columns, columns), columns)] = attn[side, :, :columns].astype(F32)
        flat[pl.ds(pl.multiple_of(half * rest, rest), rest), :] = attn[side, :, columns:].astype(F32).T
    leave(flat, o_out)
    leave(in_rows.at[:, pl.ds(0, q)], q_out)
    leave(in_rows.at[:, pl.ds(q, k)], k_out)
    leave(in_rows.at[:, pl.ds(q + k, k)], v_out)
    for kind, (target, out) in enumerate(((wide.at[0], gate_out), (wide.at[1], up_out), (tall, down_out))):
        for side, half in enumerate(halves):
            for f in range(n):
                at = pl.ds(pl.multiple_of(half * half_units + f * PIECE, PIECE), PIECE)
                cut = slice(kind * PIECE, (kind + 1) * PIECE)
                tile = held[side, f, :, cut].astype(F32)
                if kind < 2:
                    target[:, at] = tile
                else:
                    target[at, :] = tile.T
        leave(target, out)
    for move in going:
        move.wait()


def assemble(shares, layers, width, narrow, units):
    n = len(layers[0][0])
    share, attn_width = shares[0].shape[0], shares[0].shape[1] // 2
    depth_out = 2 * attn_width - width - 2 * narrow
    sources = [*shares]
    for tiles, other_tiles in layers:
        sources += [*tiles, *other_tiles]
    shapes = [(share, width), (share, narrow), (share, narrow), (depth_out, share)]
    shapes += [(share, units), (share, units), (units, share)]
    return pl.pallas_call(
        functools.partial(assemble_kernel, n),
        in_specs=[HBM] * len(sources),
        out_specs=[HBM] * 7,
        out_shape=[far(shape, F32) for shape in shapes],
        scratch_shapes=[
            pltpu.VMEM((2, n, share, 3 * PIECE), BF),
            pltpu.VMEM((2, share, attn_width), BF),
            pltpu.VMEM((share, width + 2 * narrow), F32),
            pltpu.VMEM((2, share, units), F32),
            pltpu.VMEM((units, share), F32),
            pltpu.VMEM((depth_out, share), F32),
            pltpu.SemaphoreType.DMA((2 * (n + 1),)),
            pltpu.SemaphoreType.DMA((7,)),
        ],
        compiler_params=pltpu.CompilerParams(vmem_limit_bytes=48 * MIB),
        cost_estimate=cost(0, 30e6),
        name="assemble",
    )(*in_hbm(*sources))


def attend_grads_kernel(x_own, x_other, d_own, d_other, m_own, m_other, a_own, a_other, *refs):
    out, sec = refs[-1], lax.axis_index("section")
    at = 0
    for left_own, left_other, own, other in (
        (x_own, x_other, d_own, d_other),
        (m_own, m_other, a_own, a_other),
    ):
        width = own.shape[1] // 2
        half = pl.ds(pl.multiple_of(sec * width, width), width)
        out[:, at : at + width] = (tn(left_own[...], own[:, half]) + tn(left_other[...], other[:, half])).astype(BF)
        at += width
    if len(refs) > 1:
        out[:, at:] = refs[0][...]


def attend_grads(x, d_qkv, d_mid, att, *before):
    depth, width = x.shape[1], (d_qkv.shape[1] + att.shape[1]) // 2
    terms = [x, swapped(x), d_qkv, swapped(d_qkv), d_mid, swapped(d_mid), att, swapped(att)]
    return pl.pallas_call(
        attend_grads_kernel,
        in_specs=[VMEM] * (8 + len(before)),
        out_specs=VMEM,
        out_shape=shaped((depth, width + sum(b.shape[1] for b in before)), BF),
        compiler_params=pltpu.CompilerParams(vmem_limit_bytes=14 * MIB),
        cost_estimate=cost(4 * x.size * width, 6e6),
        name="attend_grads",
    )(*terms, *before)


def summed_over_groups(x):
    return lax.psum_scatter(x, "dp", scatter_dimension=0, tiled=True)


def rope_tables(places, head_size):
    half_width = head_size // 2
    counter = jnp.arange(half_width, dtype=F32)
    base_freq = 1.0 / 500000.0 ** (2.0 * counter / head_size)
    wavelength = 2.0 * jnp.pi / base_freq
    blend_part = (8192.0 / wavelength - 1.0) / 3.0
    middle = (1.0 - blend_part) * base_freq / 32.0 + blend_part * base_freq
    frequency = jnp.where(
        wavelength < 2048.0, base_freq, jnp.where(wavelength > 8192.0, base_freq / 32.0, middle)
    )
    angles = places.astype(F32)[:, None] * frequency[None, :]
    cosine, sine = jnp.cos(angles), jnp.sin(angles)
    return (
        jnp.concatenate([cosine] * 4, axis=1),
        jnp.concatenate([-sine, sine, -sine, sine], axis=1),
    )


def halved(total, axis, size, bit, dim):
    low, high = lax.slice_in_dim(total, 0, bit, axis=dim), lax.slice_in_dim(total, bit, 2 * bit, axis=dim)
    upper = (lax.axis_index(axis) & bit) != 0
    keep, send = jnp.where(upper, high, low), jnp.where(upper, low, high)
    return keep + lax.ppermute(send, axis, [(a, a ^ bit) for a in range(size)])


def over_groups(x):
    return lax.all_gather(x, "dp", axis=0, tiled=False)


def from_both_cores(*arrays):
    return [(a, (0, places)) for a, places in arrays] + [(swapped(a), (1, places)) for a, places in arrays]


def local(groups, size, tokens, lengths, cotangent, attn_gain, mlp_gain, *weights):
    sec, t = lax.axis_index("section"), lax.axis_index("tensor")
    first = sec == 0
    rows, depth = tokens.shape[1:]
    mine = [w[0] for w in weights]
    gains = jnp.concatenate([attn_gain, mlp_gain], axis=0)
    other_gains = swapped(gains)
    layer_gains = [jnp.where(sec == l, gains, other_gains) for l in range(2)]
    attn_gains = [g[0:1] for g in layer_gains]
    mlp_gains = [g[1:2] for g in layer_gains]
    length = lax.dynamic_index_in_dim(lengths[:, 0], sec, 0, keepdims=False)
    tok = lax.dynamic_index_in_dim(tokens, sec, 0, keepdims=False)
    cot = lax.dynamic_index_in_dim(cotangent, sec, 0, keepdims=False)
    within = jnp.arange(rows, dtype=jnp.int32)
    own_places = t * rows + within
    places = jnp.concatenate([(t ^ k) * rows + within for k in range(size)])
    readable = jnp.where(places < length, places, jnp.int32(1 << 20))
    tables = rope_tables(places, HD) + (places[:, None], readable[None, :])

    g_low = jnp.where((own_places < length)[:, None], cot, jnp.zeros_like(cot))

    attn_mine = [jnp.concatenate(mine[:3], axis=1), mine[3]]
    attn_w = [(w, swapped(tied(w, other_gains))) for w in attn_mine]
    attn_cuts = [(0, w.shape[0]) for w in attn_mine]
    g_blocks1 = gather_rows(g_low, size)
    normed = tied(norm_rows(tok, attn_gains[0]), *g_blocks1)
    *weights_in, token = prefetch(0, attn_w, attn_cuts, normed)
    blocks = gather_rows(normed, size)
    all_g1 = jnp.concatenate(g_blocks1, axis=0)
    blocks[0] = tied(blocks[0], all_g1)
    all_g1 = over_groups(all_g1)
    *parts, x_attn0, q0, k0, v0, att0 = attend_fwd(blocks, weights_in, tables)
    gate_other, up_other = [swapped(tied(w, normed, *[o for _, o in attn_w])) for w in mine[4:6]]
    down_other = swapped(tied(mine[6], gate_other, parts[0]))
    mlp_w = list(zip(mine[4:], (gate_other, up_other, down_other)))
    mlp_cuts = [(0, w.shape[0]) for w in mine[4:]]
    mid0, normed = add_norm(tok, scatter_rows(parts, size), mlp_gains[0], False)
    *weights_in, token = prefetch(0, mlp_w, mlp_cuts, normed)
    *parts, gate0, up0, x_half, x_rest = mlp_fwd(gather_rows(normed, size), weights_in)
    act0, normed = add_norm(mid0, scatter_rows(parts, size), attn_gains[1], True)

    *weights_in, token = prefetch(1, attn_w, attn_cuts, normed)
    *parts, x_attn1, q1, k1, v1, att1 = attend_fwd(gather_rows(normed, size), weights_in, tables)
    parts[0] = tied(parts[0], all_g1)
    half_x0 = over_groups(tied(x_half, all_g1, parts[0]))
    mid1, normed = add_norm(act0, scatter_rows(parts, size), mlp_gains[1], False)
    *weights_in, token = prefetch(1, mlp_w, mlp_cuts, normed)
    *both_parts, x_all = mlp_both(gather_rows(normed, size), g_blocks1, weights_in)
    parts1, parts = both_parts[:size], both_parts[size:]
    parts[0] = tied(parts[0], half_x0)
    all_x1 = over_groups(tied(x_all, half_x0, parts[0]))
    d_mid, d_mid_low, mlp_part1 = norm_back(mid1, scatter_rows(parts, size), mlp_gains[1], g_low)
    rest_x0 = [x_rest]

    def with_chunk(blocks, results):
        group = lax.rem(lax.axis_index("dp") + len(rest_x0), groups)
        sent = lax.dynamic_index_in_dim(half_x0, group, 0, False)
        chunk = lax.ppermute(tied(sent, *blocks), "tensor", partners(size)[0])
        results, chunk = lax.optimization_barrier((list(results), chunk))
        rest_x0.append(chunk)
        return results

    *weights_in, token = prefetch(1, attn_w, attn_cuts, d_mid_low)
    blocks = gather_rows(d_mid_low, size)
    *parts, dm, dqkv = with_chunk(blocks, attend_bwd(blocks, (q1, k1, v1), weights_in, tables))
    attn_terms1 = attend_grads(x_attn1, dqkv, dm, att1)
    came = scatter_rows(parts, size)
    came[0] = tied(came[0], attn_terms1)
    d_stream1, d_low, attn_part1 = norm_back(act0, came, attn_gains[1], d_mid)

    *weights_in, token = prefetch(0, mlp_w, mlp_cuts, d_low)
    *parts, g_rows = with_chunk([token], mlp_bwd(gather_rows(d_low, size), gate0, up0, weights_in))
    parts[0] = tied(parts[0], all_x1)
    all_g0 = over_groups(tied(g_rows, all_x1, parts[0]))
    x1, g1 = from_both_cores((all_x1, ALL)), from_both_cores((all_g1, ALL))
    middle = groups // 2
    d_mid, d_mid_low, mlp_part0 = norm_back(mid0, scatter_rows(parts, size), mlp_gains[0], d_low)
    *weights_in, token = prefetch(0, attn_w, attn_cuts, d_mid_low)
    blocks = gather_rows(d_mid_low, size)
    late_x1 = [(tied(a, d_mid_low, token), o) for a, o in x1]
    tile = mlp_grads(1, 0, (0, middle), late_x1, g1, mlp_w)
    blocks[0] = tied(blocks[0], tile)
    *parts, dm, dqkv = with_chunk(blocks, attend_bwd(blocks, (q0, k0, v0), weights_in, tables))
    attn_terms = attend_grads(x_attn0, dqkv, dm, att0, attn_terms1)
    late_x1 = [(tied(a, parts[0], attn_terms), o) for a, o in x1]
    tile = mlp_grads(1, 0, (middle, groups), late_x1, g1, mlp_w, (tile,))
    came = scatter_rows(parts, size)
    came[0] = tied(came[0], tile)
    d_stream0, _, attn_part0 = norm_back(tok, came, attn_gains[0], d_mid)

    def beside(results, *transfers):
        results, transfers = lax.optimization_barrier((results, list(transfers)))
        return results, transfers

    def halves(axis, count, dim, bit, total):
        low, high = lax.slice_in_dim(total, 0, bit, axis=dim), lax.slice_in_dim(total, bit, 2 * bit, axis=dim)
        upper = (lax.axis_index(axis) & bit) != 0
        came = lax.ppermute(jnp.where(upper, low, high), axis, [(a, a ^ bit) for a in range(count)])
        return jnp.where(upper, high, low), came

    steps = [("tensor", size, 2, 1 << n) for n in reversed(range(size.bit_length() - 1))]

    def step_beside(results, *transfers):
        nonlocal shares
        keep, came = halves(*steps.pop(0), shares)
        results, (came, *transfers) = beside(results, came, *transfers)
        shares = keep + came
        return results, transfers

    while len(rest_x0) < groups:
        with_chunk([d_stream0], [])
    rest_own = jnp.stack(rest_x0)
    attn_share = summed_over_groups(tied(attn_terms, all_g0, d_stream0))
    shares = jnp.concatenate([attn_part0, mlp_part0, attn_part1, mlp_part1], axis=0)
    shares = shares.reshape(2, 2 * groups, size, depth // (groups * size))
    stream_keep, stream_send = jnp.where(first, d_stream0, d_stream1), jnp.where(first, d_stream1, d_stream0)
    late_x1 = [(tied(a, d_stream0), o) for a, o in x1]
    tiles1 = [tile]
    tile, (rest_other, g0_other, moved, stream_came) = step_beside(
        mlp_grads(1, 1, (0, groups), late_x1, g1, mlp_w),
        swapped(rest_own),
        swapped(tied(all_g0, d_stream0)),
        swapped(tile),
        swapped(stream_send),
    )
    tiles1.append(tile)
    others1 = [moved]
    x0 = from_both_cores((half_x0, (0, 2))) + [(rest_own, (0, (1, 3), True)), (rest_other, (1, (1, 3), True))]
    g0 = [(all_g0, (0, ALL)), (g0_other, (1, ALL))]
    act_terms = scatter_rows([tied(p, tile) for p in parts1], size)
    tile, (moved, *act_terms[1:]) = step_beside(
        mlp_grads(0, 0, (0, groups), [(tied(a, tile), o) for a, o in x0], g0, mlp_w),
        swapped(tiles1[1]),
        *act_terms[1:],
    )
    tiles0 = [tile]
    others1.append(moved)
    act1, _ = add_norm(mid1, act_terms, attn_gains[1], True)
    act_keep, act_send = jnp.where(first, act0, act1), jnp.where(first, act1, act0)
    while steps:
        step_beside([])
    by_group, i = shares.reshape(4, groups, -1), lax.axis_index("dp")
    group_terms = []
    for k in range(1, groups):
        sent = lax.dynamic_index_in_dim(by_group, lax.rem(i + k, groups), 1, False)
        group_terms.append(lax.ppermute(sent, "dp", [(j, (j + k) % groups) for j in range(groups)]))
    tile, (moved, act_came, *group_terms) = beside(
        mlp_grads(0, 1, (0, groups), [(tied(a, tile, act_keep), o) for a, o in x0], g0, mlp_w),
        swapped(tiles0[0]),
        swapped(act_send),
        *group_terms,
    )
    shares = lax.dynamic_index_in_dim(by_group, i, 1, False) + sum(group_terms)
    shares = shares.reshape(2, 2, -1)
    shares_keep, shares_send = jnp.where(first, shares[0], shares[1]), jnp.where(first, shares[1], shares[0])
    tiles0.append(tile)
    others0 = [moved, swapped(tile)]
    attn_share = tied(attn_share, tile)
    attn_other = swapped(attn_share)
    weight_grads = assemble(
        (attn_share, attn_other),
        ((tiles0, others0), (tiles1, others1)),
        mine[0].shape[1],
        mine[1].shape[1],
        mine[4].shape[1],
    )
    weight_grads, (shares,) = beside(weight_grads, swapped(shares_send))
    shares = shares_keep + shares

    def both(keep, came):
        return jnp.stack([jnp.where(first, keep, came), jnp.where(first, came, keep)])[None]

    return (
        both(act_keep, act_came),
        both(stream_keep, stream_came),
        shares[0:1],
        shares[1:2],
        *[grad[None] for grad in weight_grads],
    )


def solution(mesh):
    rows = P(None, ("dp", "tensor"), None)
    in_specs = (
        rows,
        P(None, "dp"),
        rows,
        P("section", None),
        P("section", None),
        P("section", None, "tensor"),
        P("section", None, "tensor"),
        P("section", None, "tensor"),
        P("section", "tensor", None),
        P("section", None, "tensor"),
        P("section", None, "tensor"),
        P("section", "tensor", None),
    )
    out_rows = P("section", None, ("dp", "tensor"), None)
    shares = P("section", ("dp", "tensor"))
    by_dp, by_tensor = P("section", "dp", "tensor"), P("section", "tensor", "dp")
    out_specs = (
        out_rows, out_rows, shares, shares, by_dp, by_dp, by_dp, by_tensor, by_dp, by_dp, by_tensor,
    )
    step = functools.partial(local, mesh.shape["dp"], mesh.shape["tensor"])
    return jax.shard_map(step, mesh=mesh, in_specs=in_specs, out_specs=out_specs, check_vma=False)
```
